32 devices in a mesh: section: 2 (over core), dp: 16 (over z, y, x).
Axes of the slice: x: 2, y: 2, z: 4, core: 2. Of those that a mesh axis runs over, the one named last changes fastest.
Arguments:
- images: bfloat16 [2, 16, 16, 16, 512], P(None, 'dp'), may hold values from -6 to 6
- cotangent: bfloat16 [2, 16, 16, 16, 512], P(None, 'dp'), may hold values from -6 to 6
- crop_class: int32 [2, 16], P(None, 'dp'), may hold values from 0 to 2
- norm1_gain: bfloat16 [2, 512], P('section'), may hold values from 0.5 to 1.5
- norm1_shift: bfloat16 [2, 512], P('section'), may hold values from -1.796875 to 1.796875
- input_weight: bfloat16 [2, 512, 1024], P('section'), may hold values from -0.25 to 0.25
- input_bias: bfloat16 [2, 1024], P('section'), may hold values from -1.796875 to 1.796875
- conv_kernel: bfloat16 [2, 49, 960], P('section'), may hold values from -2.59375 to 2.59375
- conv_bias: bfloat16 [2, 960], P('section'), may hold values from -1.796875 to 1.796875
- gate1_weight: bfloat16 [2, 64, 128], P('section'), may hold values from -0.75 to 0.75
- gate1_bias: bfloat16 [2, 128], P('section'), may hold values from -1.796875 to 1.796875
- gate2_weight: bfloat16 [2, 128, 256], P('section'), may hold values from -0.5 to 0.5
- gate2_bias: bfloat16 [2, 256], P('section'), may hold values from -1.796875 to 1.796875
- gate3_weight: bfloat16 [2, 256, 512], P('section'), may hold values from -0.375 to 0.375
- gate3_bias: bfloat16 [2, 512], P('section'), may hold values from -1.796875 to 1.796875
- output_weight: bfloat16 [2, 512, 512], P('section'), may hold values from -0.25 to 0.25
- output_bias: bfloat16 [2, 512], P('section'), may hold values from -1.796875 to 1.796875
- branch_scale: bfloat16 [2, 512], P('section'), may hold values from 0.5 to 2
- norm2_gain: bfloat16 [2, 512], P('section'), may hold values from 0.5 to 1.5
- norm2_shift: bfloat16 [2, 512], P('section'), may hold values from -1.796875 to 1.796875
- expand_weight: bfloat16 [2, 512, 2048], P('section'), may hold values from -0.25 to 0.25
- expand_bias: bfloat16 [2, 2048], P('section'), may hold values from -1.796875 to 1.796875
- reduce_weight: bfloat16 [2, 2048, 512], P('section'), may hold values from -0.125 to 0.125
- reduce_bias: bfloat16 [2, 512], P('section'), may hold values from -1.796875 to 1.796875
- mlp_scale: bfloat16 [2, 512], P('section'), may hold values from 0.5 to 2
Outputs:
- block_outputs: bfloat16 [2, 2, 16, 16, 16, 512], P('section', None, 'dp')
- input_grads: float32 [2, 2, 16, 16, 16, 512], P('section', None, 'dp')
- norm1_gain_grad: float32 [2, 512], P('section')
- norm1_shift_grad: float32 [2, 512], P('section')
- input_weight_grad: float32 [2, 512, 1024], P('section')
- input_bias_grad: float32 [2, 1024], P('section')
- conv_kernel_grad: float32 [2, 49, 960], P('section')
- conv_bias_grad: float32 [2, 960], P('section')
- gate1_weight_grad: float32 [2, 64, 128], P('section')
- gate1_bias_grad: float32 [2, 128], P('section')
- gate2_weight_grad: float32 [2, 128, 256], P('section')
- gate2_bias_grad: float32 [2, 256], P('section')
- gate3_weight_grad: float32 [2, 256, 512], P('section')
- gate3_bias_grad: float32 [2, 512], P('section')
- output_weight_grad: float32 [2, 512, 512], P('section')
- output_bias_grad: float32 [2, 512], P('section')
- branch_scale_grad: float32 [2, 512], P('section')
- norm2_gain_grad: float32 [2, 512], P('section')
- norm2_shift_grad: float32 [2, 512], P('section')
- expand_weight_grad: float32 [2, 512, 2048], P('section')
- expand_bias_grad: float32 [2, 2048], P('section')
- reduce_weight_grad: float32 [2, 2048, 512], P('section')
- reduce_bias_grad: float32 [2, 512], P('section')
- mlp_scale_grad: float32 [2, 512], P('section')
The draws below stay inside these ranges and needn't reach their ends.
Inputs may be any that keep to these rules, and one draw needn't show every extreme that they name: `crop_class`: 0 stands for a crop of 8 pixels a side, 1 for 12, 2 for 16; an image's pixels outside its crop are ignored.
All inputs are finite; a program needn't handle non-finite values.
Results may differ from the reference program's by a relative error of at most 0.025.
Values may be sent and summed in bfloat16 or wider, within the bound.
No kernel may reach another device: no remote copies, remote signals or barrier semaphores. Data moves between devices by JAX's collectives and lax.ppermute only.
A program may use at most 192 MiB of HBM per device.

```python
import math
import jax
import jax.numpy as jnp
from jax import lax

C = 512
FF = 2048
DW = 960
M = 2
CANVAS = 16
SIDE_S = 8
SIDE_M = 12
IMAGES = 16


def plant(drawn, stream_key, low, high):
    shape = drawn.shape
    index_at = [jax.random.randint(jax.random.fold_in(stream_key, axis), (), 0, shape[axis]) for axis in range(len(shape))]
    drawn = drawn.at[tuple(index_at)].set(low)
    longest = shape.index(max(shape))
    index_at[longest] = (index_at[longest] + 1) % shape[longest]
    return drawn.at[tuple(index_at)].set(high)


def level_of(stream_key, shape, shards, smallest, top_value):
    level = 1.0
    for axis_at, parts in shards:
        heights = jax.random.uniform(jax.random.fold_in(jax.random.fold_in(stream_key, 6), axis_at), (parts,), jnp.float32, smallest / len(shards), top_value / len(shards))
        level = level * jnp.repeat(jnp.exp(heights), shape[axis_at] // parts).reshape((-1,) + (1,) * (len(shape) - 1 - axis_at))
    return level


def noise(key, shape, scale, bound, pieces=(), kind=jnp.bfloat16):
    array = scale * jax.random.normal(key, shape, jnp.float32)
    if pieces:
        array = array * level_of(key, shape, pieces, -0.22, 0.18)
    return jnp.clip(array, -bound, bound).astype(kind)


def setup_inputs(seed: int = 0) -> dict:
    seeds = jax.random.split(jax.random.key(seed), 26)
    return {
        "images": noise(seeds[0], (M, IMAGES, CANVAS, CANVAS, C), 1.0, 6.0, ((1, 16),)),
        "cotangent": noise(seeds[1], (M, IMAGES, CANVAS, CANVAS, C), 1.0, 6.0, ((1, 16),)),
        "crop_class": plant(jax.random.randint(seeds[2], (M, IMAGES), 0, 3), jax.random.fold_in(seeds[2], 1), 0, 2).astype(jnp.int32),
        "norm1_gain": jnp.clip(1.0 + 0.1 * jax.random.normal(seeds[3], (2, C), jnp.float32), 0.5, 1.5).astype(jnp.bfloat16),
        "norm1_shift": noise(seeds[4], (2, C), 0.3, 1.796875, ((0, 2),)),
        "input_weight": noise(seeds[5], (2, C, 2 * C), C ** -0.5, 0.25, ((0, 2),)),
        "input_bias": noise(seeds[6], (2, 2 * C), 0.3, 1.796875, ((0, 2),)),
        "conv_kernel": noise(seeds[7], (2, 49, DW), 0.43, 2.59375, ((0, 2),)),
        "conv_bias": noise(seeds[8], (2, DW), 0.3, 1.796875, ((0, 2),)),
        "gate1_weight": noise(seeds[9], (2, C // 8, C // 4), (C // 8) ** -0.5, 0.75, ((0, 2),)),
        "gate1_bias": noise(seeds[10], (2, C // 4), 0.3, 1.796875, ((0, 2),)),
        "gate2_weight": noise(seeds[11], (2, C // 4, C // 2), (C // 4) ** -0.5, 0.5, ((0, 2),)),
        "gate2_bias": noise(seeds[12], (2, C // 2), 0.3, 1.796875, ((0, 2),)),
        "gate3_weight": noise(seeds[13], (2, C // 2, C), (C // 2) ** -0.5, 0.375, ((0, 2),)),
        "gate3_bias": noise(seeds[14], (2, C), 0.3, 1.796875, ((0, 2),)),
        "output_weight": noise(seeds[15], (2, C, C), C ** -0.5, 0.25, ((0, 2),)),
        "output_bias": noise(seeds[16], (2, C), 0.3, 1.796875, ((0, 2),)),
        "branch_scale": jnp.clip(jnp.exp(math.log(2.0) - 1.3862944 * jax.random.uniform(seeds[17], (2, C), jnp.float32) ** level_of(seeds[17], (2, C), ((0, 2),), -0.2, 0.2)), 0.5, 2.0).astype(jnp.bfloat16),
        "norm2_gain": jnp.clip(1.0 + 0.1 * jax.random.normal(seeds[18], (2, C), jnp.float32), 0.5, 1.5).astype(jnp.bfloat16),
        "norm2_shift": noise(seeds[19], (2, C), 0.3, 1.796875, ((0, 2),)),
        "expand_weight": noise(seeds[20], (2, C, FF), C ** -0.5, 0.25, ((0, 2),)),
        "expand_bias": noise(seeds[21], (2, FF), 0.3, 1.796875, ((0, 2),)),
        "reduce_weight": noise(seeds[22], (2, FF, C), FF ** -0.5, 0.125, ((0, 2),)),
        "reduce_bias": noise(seeds[23], (2, C), 0.3, 1.796875, ((0, 2),)),
        "mlp_scale": jnp.clip(jnp.exp(math.log(2.0) - 1.3862944 * jax.random.uniform(seeds[24], (2, C), jnp.float32) ** level_of(seeds[24], (2, C), ((0, 2),), -0.2, 0.2)), 0.5, 2.0).astype(jnp.bfloat16),
    }


@jax.custom_vjp
def low(v):
    return lax.optimization_barrier(v.astype(jnp.bfloat16)).astype(jnp.float32)

@jax.custom_vjp
def low_back(v):
    return v

def low_keep(v):
    return (low(v), None)

def low_pass(kept, grad):
    return (grad,)

def back_keep(v):
    return (v, None)

def back_low(kept, grad):
    return (low(grad),)
low.defvjp(low_keep, low_pass)
low_back.defvjp(back_keep, back_low)
eps_norm = 1e-06
conv_scale = 1.0 / 3.0

def project(left, weight):
    return jnp.einsum('hwk,kn->hwn', left, weight, precision=lax.Precision.HIGHEST)

def layer_norm(values, gain, shift):
    average = lax.optimization_barrier(jnp.mean(values, axis=-1, keepdims=True))
    centered = values - average
    spread = lax.optimization_barrier(jnp.mean(centered * centered, axis=-1, keepdims=True))
    return centered * lax.rsqrt(spread + eps_norm) * gain + shift

def depthwise(source, kernel):
    extent = source.shape[0]
    padded = jnp.pad(source, ((3, 3), (3, 3), (0, 0)))
    total = jnp.zeros(source.shape, source.dtype)
    for tap_row in range(7):
        for tap_col in range(7):
            window = padded[tap_row:tap_row + extent, tap_col:tap_col + extent, :]
            total = total + window * kernel[tap_row * 7 + tap_col]
    return total

def block(field, region, params):
    norm1_gain, norm1_shift, input_weight, input_bias, conv_kernel, conv_bias, gate1_weight, gate1_bias, gate2_weight, gate2_bias, gate3_weight, gate3_bias, output_weight, output_bias, branch_scale, norm2_gain, norm2_shift, expand_weight, expand_bias, reduce_weight, reduce_bias, mlp_scale = params
    start = field * region
    normed = low(layer_norm(start, norm1_gain, norm1_shift))
    merged = low_back(project(normed, input_weight) + input_bias)
    first = gate1_weight.shape[0]
    conv_in = merged[..., first:] * region
    mixed = (depthwise(conv_in, conv_kernel) + conv_bias) * conv_scale
    gated = merged[..., :first] * mixed[..., :first]
    offset = first
    for weight, bias in ((gate1_weight, gate1_bias), (gate2_weight, gate2_bias), (gate3_weight, gate3_bias)):
        proj = low_back(project(low(gated), weight) + bias)
        width = weight.shape[1]
        gated = proj * mixed[..., offset:offset + width]
        offset = offset + width
    branch = low_back(project(low(gated), output_weight) + output_bias)
    middle = start + branch_scale * branch
    normed2 = low(layer_norm(middle, norm2_gain, norm2_shift))
    before = low_back(project(normed2, expand_weight) + expand_bias)
    active = low(jax.nn.gelu(before, approximate=False))
    output = low_back(project(active, reduce_weight) + reduce_bias)
    return region * (middle + mlp_scale * output)

def relay(field, first, second, probe, region):
    hidden = block(field, region, first)
    sent = low_back(low(hidden)) + probe
    final = block(sent, region, second)
    return (final, hidden)

def reference(images, cotangent, crop_class, norm1_gain, norm1_shift, input_weight, input_bias, conv_kernel, conv_bias, gate1_weight, gate1_bias, gate2_weight, gate2_bias, gate3_weight, gate3_bias, output_weight, output_bias, branch_scale, norm2_gain, norm2_shift, expand_weight, expand_bias, reduce_weight, reduce_bias, mlp_scale):
    stacked = (norm1_gain, norm1_shift, input_weight, input_bias, conv_kernel, conv_bias, gate1_weight, gate1_bias, gate2_weight, gate2_bias, gate3_weight, gate3_bias, output_weight, output_bias, branch_scale, norm2_gain, norm2_shift, expand_weight, expand_bias, reduce_weight, reduce_bias, mlp_scale)
    params = tuple((entry.astype(jnp.float32) for entry in stacked))
    first = tuple((entry[0] for entry in params))
    second = tuple((entry[1] for entry in params))
    side_of = jnp.where(crop_class == 0, SIDE_S, jnp.where(crop_class == 1, SIDE_M, CANVAS)).astype(jnp.int32)
    count = M * IMAGES
    flat_images = images.reshape(count, CANVAS, CANVAS, C)
    flat_cotangent = cotangent.reshape(count, CANVAS, CANVAS, C)
    flat_sides = side_of.reshape(count)
    places = jnp.arange(CANVAS, dtype=jnp.int32)

    def step(totals, item):
        image_field, image_grad, image_side = item
        inside = (places < image_side).astype(jnp.float32)
        region = (inside[:, None] * inside[None, :])[:, :, None]
        probe = jnp.zeros((CANVAS, CANVAS, C), jnp.float32)

        def whole(field, first_p, second_p, probe_p):
            return relay(field, first_p, second_p, probe_p, region)
        final, pull, hidden = jax.vjp(whole, image_field.astype(jnp.float32), first, second, probe, has_aux=True)
        field_grad, first_grad, second_grad, probe_grad = pull(image_grad.astype(jnp.float32))
        totals = jax.tree.map(lambda total, one, two: total + jnp.stack([one, two]), totals, first_grad, second_grad)
        return (totals, (hidden.astype(jnp.bfloat16), final.astype(jnp.bfloat16), field_grad, probe_grad))
    start_totals = tuple((jnp.zeros(entry.shape, entry.dtype) for entry in params))
    totals, (hidden_all, final_all, field_all, probe_all) = lax.scan(step, start_totals, (flat_images, flat_cotangent, flat_sides))
    block_outputs = jnp.stack([hidden_all, final_all]).reshape(2, M, IMAGES, CANVAS, CANVAS, C)
    input_grads = jnp.stack([field_all, probe_all]).reshape(2, M, IMAGES, CANVAS, CANVAS, C)
    return (block_outputs, input_grads, totals[0], totals[1], totals[2], totals[3], totals[4], totals[5], totals[6], totals[7], totals[8], totals[9], totals[10], totals[11], totals[12], totals[13], totals[14], totals[15], totals[16], totals[17], totals[18], totals[19], totals[20], totals[21])
```

```python
import functools

import jax
import jax.numpy as jnp
from jax import lax
from jax.experimental import pallas as pl
from jax.experimental.pallas import tpu as pltpu
from jax.sharding import PartitionSpec as P

SIDE_S = 8
SIDE_M = 12
CANVAS = 16
PIX = CANVAS * CANVAS
C = 512
FF = 2048
LANES = 128
GROUPS = 8
EPS = 1e-06
KS = 7
PAD_ROWS = (CANVAS + 6) * CANVAS
BF = jnp.bfloat16
F32 = jnp.float32
VMEM_BYTES = 56 * 1024 * 1024

V_N1G, V_N1S, V_BIN, V_CB, V_B1, V_B2, V_B3, V_BO, V_BS, V_N2G, V_N2S, V_BE, V_BR, V_MS = range(14)
VEC_ROWS = 16


def nn(a, b):
    return jnp.dot(a, b, preferred_element_type=F32)


def nt(a, b):
    return lax.dot_general(a, b, (((1,), (1,)), ((), ())), preferred_element_type=F32)


def tn(a, b):
    return lax.dot_general(a, b, (((0,), (0,)), ((), ())), preferred_element_type=F32)


def colsum(v):
    return jnp.sum(v, axis=0, keepdims=True)


def wide(m, n):
    return jnp.concatenate([m] * n, axis=1)


def fill_mask(mask_ref, side):
    r = lax.broadcasted_iota(jnp.int32, (PIX, LANES), 0)
    inside = ((r // CANVAS) < side) & ((r % CANVAS) < side)
    mask_ref[...] = inside.astype(F32)


def start_select(sel, pairs, sems):
    for i, (own, other, dst) in enumerate(pairs):

        @pl.when(sel == 0)
        def _():
            pltpu.make_async_copy(own, dst, sems.at[i]).start()

        @pl.when(sel != 0)
        def _():
            pltpu.make_async_copy(other, dst, sems.at[i]).start()


def wait_select(i, pairs, sems):
    own, other, dst = pairs[i]
    pltpu.make_async_copy(own, dst, sems.at[i]).wait()


def conv_rows(src_ref, taps_ref, flip, bias, store):
    def row(h, carry):
        accs = [bias] * CANVAS if bias is not None else [None] * CANVAS
        for a in range(KS):
            ks = []
            for e in range(KS):
                t = (KS - 1 - a) * KS + (KS - 1 - e) if flip else a * KS + e
                ks.append(taps_ref[t * GROUPS : (t + 1) * GROUPS, :])
            for w2 in range(CANVAS):
                x = src_ref[pl.ds(pl.multiple_of(((h + a) * CANVAS + w2) * GROUPS, GROUPS), GROUPS), :]
                for e in range(KS):
                    w = w2 + 3 - e
                    if 0 <= w < CANVAS:
                        term = x * ks[e]
                        accs[w] = term if accs[w] is None else accs[w] + term
        for w in range(CANVAS):
            store(h * CANVAS + w, accs[w])
        return carry

    lax.fori_loop(0, CANVAS, row, 0)


def zero_border(ref):
    zeros = jnp.zeros((3 * CANVAS * GROUPS, LANES), F32)
    ref[0 : 3 * CANVAS * GROUPS, :] = zeros
    ref[(PAD_ROWS - 3 * CANVAS) * GROUPS :, :] = zeros


def lane_group(ref, g, rows=PIX, base=0):
    return ref[pl.ds(base + g, rows, stride=GROUPS), :]


def forward_kernel(
    meta, x_ref, vec_ref, taps_ref, cbias_ref,
    win_a, win_b, w1_a, w1_b, w2_a, w2_b, w3_a, w3_b, wo_a, wo_b, we_a, we_b, wr_a, wr_b,
    n1_ref, cin_ref, mix_ref, p_ref, gl_ref, mid_ref, br_ref, n2_ref, act_ref, slope_ref, out_ref, res_ref,
    mask_ref, mx_ref, win, w1, w2, w3, wo, we, wr, sems,
):
    pairs = [
        (win_a, win_b, win), (w1_a, w1_b, w1.at[0:64]), (w2_a, w2_b, w2), (w3_a, w3_b, w3),
        (wo_a, wo_b, wo), (we_a, we_b, we), (wr_a, wr_b, wr),
    ]
    start_select(meta[0], pairs, sems)
    w1[64:128, :] = jnp.zeros((64, LANES), BF)
    fill_mask(mask_ref, meta[1])
    zero_border(cin_ref)

    def vec(row, lo, n):
        return vec_ref[row : row + 1, lo : lo + n]

    def norm_in(i, carry):
        r = pl.ds(pl.multiple_of(i * 32, 32), 32)
        start = x_ref[r, :].astype(F32) * wide(mask_ref[r, :], 4)
        cen = start - jnp.mean(start, axis=-1, keepdims=True)
        inv = lax.rsqrt(jnp.mean(cen * cen, axis=-1, keepdims=True) + EPS)
        n1_ref[r, :] = (cen * inv * vec(V_N1G, 0, C) + vec(V_N1S, 0, C)).astype(BF)
        return carry

    lax.fori_loop(0, PIX // 32, norm_in, 0)
    wait_select(0, pairs, sems)
    for n in range(4):
        m = nn(n1_ref[...], win[:, n * 256 : (n + 1) * 256]) + vec(V_BIN, n * 256, 256)
        for half in range(2):
            g = 2 * n + half
            v = m[:, half * LANES : (half + 1) * LANES] * mask_ref[...]
            cin_ref[pl.ds(3 * CANVAS * GROUPS + g, PIX, stride=GROUPS), :] = v
            if g == 0:
                p_ref[:, 0:LANES] = v
    bias = cbias_ref[...]

    def keep(pixel, acc):
        mx_ref[pl.ds(pl.multiple_of(pixel * GROUPS, GROUPS), GROUPS), :] = acc * (1.0 / 3.0)

    conv_rows(cin_ref, taps_ref, False, bias, keep)
    for g in range(GROUPS):
        mix_ref[:, g * LANES : (g + 1) * LANES] = lane_group(mx_ref, g)
    for i in (1, 2, 3, 4):
        wait_select(i, pairs, sems)
    gl_ref[:, 0:128] = (p_ref[:, 0:128] * pltpu.roll(mix_ref[:, 0:128], 64, 1)).astype(BF)
    p1 = nn(gl_ref[:, 0:128], w1[...]) + vec(V_B1, 0, 128)
    p_ref[:, 128:256] = p1
    gl_ref[:, 128:256] = (p1 * mix_ref[:, 128:256]).astype(BF)
    p2 = nn(gl_ref[:, 128:256], w2[...]) + vec(V_B2, 0, 256)
    p_ref[:, 256:512] = p2
    gl_ref[:, 256:512] = (p2 * mix_ref[:, 256:512]).astype(BF)
    for n in range(2):
        c = 256 * n
        p3 = nn(gl_ref[:, 256:512], w3[:, c : c + 256]) + vec(V_B3, c, 256)
        p_ref[:, 512 + c : 768 + c] = p3
        gl_ref[:, 512 + c : 768 + c] = (p3 * mix_ref[:, 512 + c : 768 + c]).astype(BF)
    for n in range(2):
        c = 256 * n
        br = nn(gl_ref[:, 512:1024], wo[:, c : c + 256]) + vec(V_BO, c, 256)
        br_ref[:, c : c + 256] = br.astype(BF)
        start = x_ref[:, c : c + 256].astype(F32) * wide(mask_ref[...], 2)
        mid_ref[:, c : c + 256] = start + vec(V_BS, c, 256) * br

    def norm_mid(i, carry):
        r = pl.ds(pl.multiple_of(i * 32, 32), 32)
        mid = mid_ref[r, :]
        cen = mid - jnp.mean(mid, axis=-1, keepdims=True)
        inv = lax.rsqrt(jnp.mean(cen * cen, axis=-1, keepdims=True) + EPS)
        n2_ref[r, :] = (cen * inv * vec(V_N2G, 0, C) + vec(V_N2S, 0, C)).astype(BF)
        return carry

    lax.fori_loop(0, PIX // 32, norm_mid, 0)
    wait_select(5, pairs, sems)
    wait_select(6, pairs, sems)
    for j in range(8):
        c = 256 * j
        pre = nn(n2_ref[...], we[:, c : c + 256]) + vec(V_BE, c, 256)
        cum = 0.5 * (1.0 + lax.erf(pre * 0.7071067811865476))
        act_ref[:, c : c + 256] = (pre * cum).astype(BF)
        slope = cum + pre * jnp.exp(-0.5 * pre * pre) * 0.3989422804014327
        slope_ref[:, c : c + 256] = slope.astype(BF)
    for n in range(2):
        c = 256 * n
        out = nn(act_ref[...], wr[:, c : c + 256]) + vec(V_BR, c, 256)
        out_ref[:, c : c + 256] = out.astype(BF)
        res = wide(mask_ref[...], 2) * (mid_ref[:, c : c + 256] + vec(V_MS, c, 256) * out)
        res_ref[:, c : c + 256] = res.astype(BF)


def piece_rows(meta, p, rows):
    mask = meta[2 + ((p >> 4) & 1)]
    return pl.multiple_of((p ^ mask) * rows, 32)


def mlp_kernel(
    meta, dy_ref, vec_ref, n2_ref, act_ref, slope_ref, out_ref, mid_ref, we_a, we_b, wr_a, wr_b,
    dmid_ref, mvec_ref, keep_ref, send_ref,
    mask_ref, dout_ref, dpre_ref, dn2_ref, bucket, we, wr, sems,
):
    pairs = [(wr_a, wr_b, wr), (we_a, we_b, we)]
    start_select(meta[0], pairs, sems)
    fill_mask(mask_ref, meta[1])
    mvec_ref[...] = jnp.zeros_like(mvec_ref)

    def vec(row, lo, n):
        return vec_ref[row : row + 1, lo : lo + n]

    for n in range(2):
        c = 256 * n
        dyr = dy_ref[:, c : c + 256].astype(F32) * wide(mask_ref[...], 2)
        dmid_ref[:, c : c + 256] = dyr
        dout = (vec(V_MS, c, 256) * dyr).astype(BF)
        dout_ref[:, c : c + 256] = dout
        mvec_ref[3:4, c : c + 256] = colsum(dout.astype(F32))
        mvec_ref[4:5, c : c + 256] = colsum(dyr * out_ref[:, c : c + 256].astype(F32))
    wait_select(0, pairs, sems)
    for j in range(8):
        c = 256 * j
        dw = tn(act_ref[:, c : c + 256], dout_ref[...]).astype(BF)
        for q in range(8):
            p = 8 * j + q
            bucket[pl.ds(piece_rows(meta, p, 64), 32), :] = dw[32 * q : 32 * q + 32, :]
        dact = nt(dout_ref[...], wr[c : c + 256, :])
        dpre = (dact * slope_ref[:, c : c + 256].astype(F32)).astype(BF)
        dpre_ref[:, c : c + 256] = dpre
        mvec_ref[2:3, c : c + 256] = colsum(dpre.astype(F32))
    wait_select(1, pairs, sems)
    for cb in range(4):
        dw = tn(n2_ref[...], dpre_ref[:, 512 * cb : 512 * cb + 512]).astype(BF)
        for q in range(16):
            p = 16 * cb + q
            bucket[pl.ds(pl.multiple_of(piece_rows(meta, p, 64) + 32, 32), 32), :] = dw[32 * q : 32 * q + 32, :]
    keep_copy = pltpu.make_async_copy(bucket.at[0:2048], keep_ref, sems.at[2])
    send_copy = pltpu.make_async_copy(bucket.at[2048:4096], send_ref, sems.at[3])
    send_copy.start()
    keep_copy.start()
    for n in range(2):
        c = 256 * n
        dn2_ref[:, c : c + 256] = nt(dpre_ref[...], we[c : c + 256, :])

    def norm_back(i, carry):
        dgain, dshift = carry
        r = pl.ds(pl.multiple_of(i * 32, 32), 32)
        mid = mid_ref[r, :]
        cen = mid - jnp.mean(mid, axis=-1, keepdims=True)
        inv = lax.rsqrt(jnp.mean(cen * cen, axis=-1, keepdims=True) + EPS)
        xhat = cen * inv
        up = dn2_ref[r, :]
        g = up * vec(V_N2G, 0, C)
        inner = g - jnp.mean(g, axis=-1, keepdims=True) - xhat * jnp.mean(g * xhat, axis=-1, keepdims=True)
        dmid_ref[r, :] = dmid_ref[r, :] + inv * inner
        return dgain + colsum(up * xhat), dshift + colsum(up)

    zero = jnp.zeros((1, C), F32)
    dgain, dshift = lax.fori_loop(0, PIX // 32, norm_back, (zero, zero))
    mvec_ref[0:1, 0:C] = dgain
    mvec_ref[1:2, 0:C] = dshift
    send_copy.wait()
    keep_copy.wait()


def gn_kernel(
    meta, x_ref, dmid_ref, mvec_ref, vec_ref, taps_ref, n1_ref, cin_ref, mix_ref, p_ref, gl_ref, br_ref,
    win_a, win_b, w1_a, w1_b, w2_a, w2_b, w3_a, w3_b, wo_a, wo_b,
    dv_ref, dvb_ref, keep_ref, send_ref,
    mask_ref, dbr_ref, dg_ref, dp_ref, dmix_ref, dcp_ref, ds_ref, dk_ref, dmg_ref, dn1_ref, bucket,
    win, w1, w2, w3, wo, sems,
):
    pairs = [
        (wo_a, wo_b, wo), (w3_a, w3_b, w3), (w2_a, w2_b, w2), (w1_a, w1_b, w1.at[0:64]), (win_a, win_b, win),
    ]
    start_select(meta[0], pairs, sems)
    w1[64:128, :] = jnp.zeros((64, LANES), BF)
    fill_mask(mask_ref, meta[1])
    zero_border(dcp_ref)

    def vec(row, lo, n):
        return vec_ref[row : row + 1, lo : lo + n]

    def put(p, val, sub=0):
        n = val.shape[0]
        bucket[pl.ds(pl.multiple_of(piece_rows(meta, p, 32) + sub, 16), n), :] = val

    tail = {}

    def vec_grad(row, val):
        tail[row] = val

    dbs, dbo = [], []
    for n in range(2):
        c = 256 * n
        dm = dmid_ref[:, c : c + 256]
        dbs.append(colsum(dm * br_ref[:, c : c + 256].astype(F32)))
        dbr = (vec(V_BS, c, 256) * dm).astype(BF)
        dbr_ref[:, c : c + 256] = dbr
        dbo.append(colsum(dbr.astype(F32)))
    wait_select(0, pairs, sems)
    dw = tn(gl_ref[:, 512:1024], dbr_ref[...]).astype(BF)
    for q in range(16):
        put(32 + q, dw[32 * q : 32 * q + 32, :])
    wait_select(1, pairs, sems)
    wait_select(2, pairs, sems)
    wait_select(3, pairs, sems)
    db3 = []
    for n in range(2):
        c = 256 * n
        dg = nt(dbr_ref[...], wo[c : c + 256, :])
        dp = (dg * mix_ref[:, 512 + c : 768 + c]).astype(BF)
        dmix_ref[:, 512 + c : 768 + c] = dg * p_ref[:, 512 + c : 768 + c] * (1.0 / 3.0)
        dp_ref[:, 512 + c : 768 + c] = dp
        db3.append(colsum(dp.astype(F32)))
    dw = tn(gl_ref[:, 256:512], dp_ref[:, 512:1024]).astype(BF)
    for q in range(8):
        put(48 + q, dw[32 * q : 32 * q + 32, :])
    dg = nt(dp_ref[:, 512:1024], w3[...])
    dp = (dg * mix_ref[:, 256:512]).astype(BF)
    dmix_ref[:, 256:512] = dg * p_ref[:, 256:512] * (1.0 / 3.0)
    dp_ref[:, 256:512] = dp
    db2 = colsum(dp.astype(F32))
    dw = tn(gl_ref[:, 128:256], dp_ref[:, 256:512]).astype(BF)
    dw = jnp.concatenate([dw[0:64, :], dw[64:128, :]], axis=1)
    put(56, dw[0:32, :])
    put(57, dw[32:64, :])
    dg = nt(dp_ref[:, 256:512], w2[...])
    dp = (dg * mix_ref[:, 128:256]).astype(BF)
    dmix_ref[:, 128:256] = dg * p_ref[:, 128:256] * (1.0 / 3.0)
    dp_ref[:, 128:256] = dp
    db1 = colsum(dp.astype(F32))
    dw1 = tn(gl_ref[:, 0:128], dp_ref[:, 128:256]).astype(BF)
    put(62, jnp.concatenate([dw1[16 * i : 16 * i + 16, :] for i in range(4)], axis=1))
    put(62, jnp.zeros((16, 512), BF), 16)
    dg = nt(dp_ref[:, 128:256], w1[...])
    dmix_ref[:, 0:128] = pltpu.roll(dg * p_ref[:, 0:128], 64, 1) * (1.0 / 3.0)
    dg_ref[...] = dg * pltpu.roll(mix_ref[:, 0:128], 64, 1)
    for g in range(GROUPS):
        dcp_ref[pl.ds(3 * CANVAS * GROUPS + g, PIX, stride=GROUPS), :] = dmix_ref[:, g * LANES : (g + 1) * LANES]

    def keep(pixel, acc):
        ds_ref[pl.ds(pl.multiple_of(pixel * GROUPS, GROUPS), GROUPS), :] = acc

    conv_rows(dcp_ref, taps_ref, True, None, keep)

    def vreg(ref, index):
        return ref[pl.ds(pl.multiple_of(index * GROUPS, GROUPS), GROUPS), :]

    dk_ref[...] = jnp.zeros_like(dk_ref)
    for taps in ((0, 1), (2, 3), (4, 5), (6,)):

        def row(h, accs):
            accs = list(accs)
            ds = [vreg(dcp_ref, (h + 3) * CANVAS + w) for w in range(CANVAS)]
            for i, a in enumerate(taps):
                for w2 in range(CANVAS):
                    x = vreg(cin_ref, (h + a) * CANVAS + w2)
                    for e in range(KS):
                        w = w2 + 3 - e
                        if 0 <= w < CANVAS:
                            accs[i * KS + e] = accs[i * KS + e] + x * ds[w]
            if len(taps) == 1:
                for w in range(CANVAS):
                    accs[KS] = accs[KS] + ds[w]
            return tuple(accs)

        count = len(taps) * KS + (1 if len(taps) == 1 else 0)
        accs = lax.fori_loop(0, CANVAS, row, tuple(jnp.zeros((GROUPS, LANES), F32) for _ in range(count)))
        for i in range(count):
            t = taps[0] * KS + i
            dk_ref[t * GROUPS : (t + 1) * GROUPS, :] = accs[i]
    for half in range(2):
        dk = jnp.concatenate([lane_group(dk_ref, 4 * half + i, 64) for i in range(4)], axis=1).astype(BF)
        put(58 + 2 * half, dk[0:32, :])
        put(59 + 2 * half, dk[32:64, :])
    dbin = []
    for g in range(GROUPS):
        d = lane_group(ds_ref, g) * mask_ref[...]
        if g == 0:
            d = d + dg_ref[...]
        d = d.astype(BF)
        dmg_ref[:, g * LANES : (g + 1) * LANES] = d
        dbin.append(colsum(d.astype(F32)))
    wait_select(4, pairs, sems)
    for cb in range(2):
        dw = tn(n1_ref[...], dmg_ref[:, 512 * cb : 512 * cb + 512]).astype(BF)
        for q in range(16):
            put(16 * cb + q, dw[32 * q : 32 * q + 32, :])
    for n in range(2):
        c = 256 * n
        dn1_ref[:, c : c + 256] = nt(dmg_ref[...], win[c : c + 256, :])

    def norm_back(i, carry):
        dgain, dshift = carry
        r = pl.ds(pl.multiple_of(i * 32, 32), 32)
        m = wide(mask_ref[r, :], 4)
        start = x_ref[r, :].astype(F32) * m
        cen = start - jnp.mean(start, axis=-1, keepdims=True)
        inv = lax.rsqrt(jnp.mean(cen * cen, axis=-1, keepdims=True) + EPS)
        xhat = cen * inv
        up = dn1_ref[r, :]
        g = up * vec(V_N1G, 0, C)
        inner = g - jnp.mean(g, axis=-1, keepdims=True) - xhat * jnp.mean(g * xhat, axis=-1, keepdims=True)
        dv = m * (dmid_ref[r, :] + inv * inner)
        dv_ref[r, :] = dv
        dvb_ref[r, :] = dv.astype(BF)
        return dgain + colsum(up * xhat), dshift + colsum(up)

    zero = jnp.zeros((1, C), F32)
    dgain, dshift = lax.fori_loop(0, PIX // 32, norm_back, (zero, zero))
    z = jnp.zeros((1, LANES), F32)
    rows = [
        dgain,
        dshift,
        jnp.concatenate(dbin[0:4], axis=1),
        jnp.concatenate(dbin[4:8], axis=1),
        jnp.concatenate([db1, z, z, z], axis=1),
        jnp.concatenate([db2, z, z], axis=1),
        jnp.concatenate(db3, axis=1),
        jnp.concatenate(dbo, axis=1),
        jnp.concatenate(dbs, axis=1),
        mvec_ref[0:1, 0:C],
        mvec_ref[1:2, 0:C],
        mvec_ref[2:3, 0:512],
        mvec_ref[2:3, 512:1024],
        mvec_ref[2:3, 1024:1536],
        mvec_ref[2:3, 1536:2048],
        mvec_ref[3:4, 0:C],
        mvec_ref[4:5, 0:C],
    ]
    rows.append(jnp.zeros((32 - len(rows), C), F32))
    put(63, jnp.concatenate(rows, axis=0).astype(BF))
    send_copy = pltpu.make_async_copy(bucket.at[1024:2048], send_ref, sems.at[5])
    keep_copy = pltpu.make_async_copy(bucket.at[0:1024], keep_ref, sems.at[6])
    send_copy.start()
    keep_copy.start()
    send_copy.wait()
    keep_copy.wait()


def start_pieces(meta, rows, own0, other0, own1, other1, buf, sems):
    for p in range(64):
        mask = meta[2 + ((p >> 4) & 1)]
        rel = p ^ mask
        off = pl.multiple_of((rel & 31) * rows, 32)
        far = rel >> 5
        dst = buf.at[p * rows : (p + 1) * rows]
        sem = sems.at[p // 8]
        for sec, own, other in ((0, own0, other0), (1, own1, other1)):

            @pl.when((meta[4] == sec) & (far == 0))
            def _():
                pltpu.make_async_copy(own.at[pl.ds(off, rows)], dst, sem).start()

            @pl.when((meta[4] == sec) & (far == 1))
            def _():
                pltpu.make_async_copy(other.at[pl.ds(off, rows)], dst, sem).start()


def wait_pieces(i, rows, own0, buf, sems):
    part = pl.ds(i * 8 * rows, 8 * rows)
    pltpu.make_async_copy(own0.at[pl.ds(0, 8 * rows)], buf.at[part], sems.at[i]).wait()


def mlp_finish(meta, own0, other0, own1, other1, wr_ref, we_ref, buf, sems):
    start_pieces(meta, 64, own0, other0, own1, other1, buf, sems)
    for i in range(8):
        wait_pieces(i, 64, own0, buf, sems)
        for q in range(8):
            p = 8 * i + q
            wr_ref[32 * p : 32 * p + 32, :] = buf[64 * p : 64 * p + 32, :].astype(F32)
            cb, r = p // 16, p % 16
            we_ref[32 * r : 32 * r + 32, 512 * cb : 512 * cb + 512] = buf[64 * p + 32 : 64 * p + 64, :].astype(F32)


def gn_finish(
    meta, own0, other0, own1, other1,
    n1g, n1s, win, bin_, conv, w1, b1, w2, b2, w3, b3, wo, bo, bs, n2g, n2s, be, br, ms,
    buf, sems,
):
    start_pieces(meta, 32, own0, other0, own1, other1, buf, sems)
    for i in range(8):
        wait_pieces(i, 32, own0, buf, sems)
    for cb in range(2):
        win[:, 512 * cb : 512 * cb + 512] = buf[512 * cb : 512 * cb + 512, :].astype(F32)
    wo[...] = buf[1024:1536, :].astype(F32)
    w3[...] = buf[1536:1792, :].astype(F32)
    for i in range(2):
        w2[64 * i : 64 * i + 64, :] = buf[1792:1856, 256 * i : 256 * i + 256].astype(F32)
        conv[:, 512 * i : 512 * i + 512] = buf[1856 + 64 * i : 1920 + 64 * i, :].astype(F32)
    for i in range(4):
        w1[16 * i : 16 * i + 16, :] = buf[1984:2000, 128 * i : 128 * i + 128].astype(F32)
    v = buf[2016:2048, :].astype(F32)
    n1g[...] = v[0:1]
    n1s[...] = v[1:2]
    bin_[:, 0:512] = v[2:3]
    bin_[:, 512:1024] = v[3:4]
    b1[...] = v[4:5, 0:128]
    b2[...] = v[5:6, 0:256]
    b3[...] = v[6:7]
    bo[...] = v[7:8]
    bs[...] = v[8:9]
    n2g[...] = v[9:10]
    n2s[...] = v[10:11]
    for i in range(4):
        be[:, 512 * i : 512 * i + 512] = v[11 + i : 12 + i]
    br[...] = v[15:16]
    ms[...] = v[16:17]


SMEM = pl.BlockSpec(memory_space=pltpu.SMEM)
VM = pl.BlockSpec(memory_space=pltpu.VMEM)
ANY = pl.BlockSpec(memory_space=pl.ANY)


def sds(shape, dtype):
    return jax.ShapeDtypeStruct(shape, dtype)


def params():
    return pltpu.CompilerParams(vmem_limit_bytes=VMEM_BYTES)


def cost(flops, bytes_accessed):
    return pl.CostEstimate(flops=flops, bytes_accessed=bytes_accessed, transcendentals=0)


def run_forward(meta, x, vec, taps, cbias, mats):
    outs = [
        sds((PIX, C), BF), sds((PAD_ROWS * GROUPS, LANES), F32), sds((PIX, 1024), F32), sds((PIX, 1024), F32),
        sds((PIX, 1024), BF), sds((PIX, C), F32), sds((PIX, C), BF), sds((PIX, C), BF), sds((PIX, FF), BF),
        sds((PIX, FF), BF), sds((PIX, C), BF), sds((PIX, C), BF),
    ]
    flat = [r for pair in mats for r in pair]
    return pl.pallas_call(
        forward_kernel,
        name="block_forward",
        out_shape=outs,
        in_specs=[SMEM, VM, VM, VM, VM] + [ANY] * 14,
        out_specs=[VM] * len(outs),
        scratch_shapes=[
            pltpu.VMEM((PIX, LANES), F32), pltpu.VMEM((PIX * GROUPS, LANES), F32),
            pltpu.VMEM((C, 1024), BF), pltpu.VMEM((128, 128), BF), pltpu.VMEM((128, 256), BF),
            pltpu.VMEM((256, 512), BF), pltpu.VMEM((512, 512), BF), pltpu.VMEM((C, FF), BF),
            pltpu.VMEM((FF, C), BF), pltpu.SemaphoreType.DMA((7,)),
        ],
        compiler_params=params(),
        cost_estimate=cost(5_000_000_000, 14_000_000),
    )(meta, x, vec, taps, cbias, *flat)


def run_mlp(meta, dy, vec, n2, act, slope, out, mid, mats):
    outs = [sds((PIX, C), F32), sds((8, FF), F32), sds((2048, 512), BF), sds((2048, 512), BF)]
    return pl.pallas_call(
        mlp_kernel,
        name="mlp_backward",
        out_shape=outs,
        in_specs=[SMEM] + [VM] * 7 + [ANY] * 4,
        out_specs=[VM, VM, ANY, ANY],
        scratch_shapes=[
            pltpu.VMEM((PIX, LANES), F32), pltpu.VMEM((PIX, C), BF), pltpu.VMEM((PIX, FF), BF),
            pltpu.VMEM((PIX, C), F32), pltpu.VMEM((4096, 512), BF),
            pltpu.VMEM((C, FF), BF), pltpu.VMEM((FF, C), BF), pltpu.SemaphoreType.DMA((4,)),
        ],
        compiler_params=params(),
        cost_estimate=cost(5_000_000_000, 14_000_000),
    )(meta, dy, vec, n2, act, slope, out, mid, *mats[5], *mats[6])


def run_gn(meta, x, dmid, mvec, vec, taps, n1, cin, mix, p, gl, br, mats):
    outs = [sds((PIX, C), F32), sds((PIX, C), BF), sds((1024, 512), BF), sds((1024, 512), BF)]
    flat = [r for pair in mats[:5] for r in pair]
    return pl.pallas_call(
        gn_kernel,
        name="gnconv_backward",
        out_shape=outs,
        in_specs=[SMEM] + [VM] * 11 + [ANY] * 10,
        out_specs=[VM, VM, ANY, ANY],
        scratch_shapes=[
            pltpu.VMEM((PIX, LANES), F32), pltpu.VMEM((PIX, C), BF), pltpu.VMEM((PIX, LANES), F32),
            pltpu.VMEM((PIX, 1024), BF), pltpu.VMEM((PIX, 1024), F32), pltpu.VMEM((PAD_ROWS * GROUPS, LANES), F32),
            pltpu.VMEM((PIX * GROUPS, LANES), F32), pltpu.VMEM((64 * GROUPS, LANES), F32),
            pltpu.VMEM((PIX, 1024), BF), pltpu.VMEM((PIX, C), F32), pltpu.VMEM((2048, 512), BF),
            pltpu.VMEM((C, 1024), BF), pltpu.VMEM((128, 128), BF), pltpu.VMEM((128, 256), BF),
            pltpu.VMEM((256, 512), BF), pltpu.VMEM((512, 512), BF), pltpu.SemaphoreType.DMA((7,)),
        ],
        compiler_params=params(),
        cost_estimate=cost(5_000_000_000, 14_000_000),
    )(meta, x, dmid, mvec, vec, taps, n1, cin, mix, p, gl, br, *flat)


def run_mlp_finish(meta, halves):
    outs = [sds((FF, C), F32), sds((C, FF), F32)]
    return pl.pallas_call(
        mlp_finish,
        name="mlp_finish",
        out_shape=outs,
        in_specs=[SMEM] + [ANY] * 4,
        out_specs=[VM] * 2,
        scratch_shapes=[pltpu.VMEM((4096, 512), BF), pltpu.SemaphoreType.DMA((8,))],
        compiler_params=params(),
        cost_estimate=cost(1_000_000, 12_000_000),
    )(meta, *halves)


def run_gn_finish(meta, halves):
    widths = [512, 512, (512, 1024), 1024, (64, 1024), (64, 128), 128, (128, 256), 256, (256, 512), 512,
              (512, 512), 512, 512, 512, 512, 2048, 512, 512]
    outs = [sds((1, w) if isinstance(w, int) else w, F32) for w in widths]
    return pl.pallas_call(
        gn_finish,
        name="gn_finish",
        out_shape=outs,
        in_specs=[SMEM] + [ANY] * 4,
        out_specs=[VM] * len(outs),
        scratch_shapes=[pltpu.VMEM((2048, 512), BF), pltpu.SemaphoreType.DMA((8,))],
        compiler_params=params(),
        cost_estimate=cost(1_000_000, 6_000_000),
    )(meta, *halves)


AXES = ("section", "dp")


class Links:
    def __init__(self, count):
        self.count = count

    def to(self, x, section_flip, dp_flip, only=None):
        n = self.count
        pairs = [
            (s * n + d, (s ^ section_flip) * n + (d ^ dp_flip))
            for s in range(2)
            for d in range(n)
            if only is None or s == only
        ]
        return lax.ppermute(x, AXES, pairs)


def reduce_bucket(links, keep, send):
    rows = keep.shape[0] // 32
    shape = (2, 2, 2, 4, rows, 512)
    half = keep.reshape(shape) + links.to(send, 1, 0).reshape(shape)
    got_a = links.to(half[0, 1], 0, 1)
    got_b = links.to(half[1, 1], 0, 2)
    part_a = half[0, 0] + got_a
    part_b = half[1, 0] + got_b
    got_a = links.to(part_a[1], 0, 2)
    got_b = links.to(part_b[1], 0, 1)
    parts = jnp.stack([part_a[0] + got_a, part_b[0] + got_b], axis=1)
    got = [links.to(parts[i], 0, 4 * i) for i in (1, 2, 3)]
    total = parts[0].astype(F32) + got[0].astype(F32) + got[1].astype(F32) + got[2].astype(F32)
    total = total.astype(BF)
    chips = links.count // 16
    if chips > 1:
        groups = [[g * 16 + r for g in range(chips)] for r in range(16)]
        total = lax.psum(total, "dp", axis_index_groups=groups)
    return total


def gather_bucket(links, total):
    got = [links.to(total, 0, 4 * i) for i in (1, 2, 3)]
    whole = jnp.stack([total] + got, axis=1)
    part_a, part_b = whole[0], whole[1]
    got_a = links.to(part_a, 0, 2)
    got_b = links.to(part_b, 0, 1)
    part_a = jnp.stack([part_a, got_a])
    part_b = jnp.stack([part_b, got_b])
    got_a = links.to(part_a, 0, 1)
    got_b = links.to(part_b, 0, 2)
    return jnp.stack([jnp.stack([part_a, got_a]), jnp.stack([part_b, got_b])]).reshape(-1, 512)


MATRIX = (2, 6, 8, 10, 12, 17, 19)
VECTORS = (0, 1, 3, 5, 7, 9, 11, 13, 14, 15, 16, 18, 20, 21)


def on_device(links, images, cotangent, crop_class, *stacked):
    section = lax.axis_index("section")
    place = lax.axis_index("dp") % 16
    x_bit, y_bit, z_at = place & 1, (place >> 1) & 1, place >> 2
    mask_a = section * 32 + x_bit * 8 + y_bit * 4 + z_at
    mask_b = section * 32 + y_bit * 8 + x_bit * 4 + z_at
    kind = lax.dynamic_index_in_dim(crop_class.reshape(-1), section, 0, keepdims=False)
    side = jnp.where(kind == 0, SIDE_S, jnp.where(kind == 1, SIDE_M, CANVAS))

    def meta_for(block):
        sel = section if block == 0 else 1 - section
        return jnp.stack([sel, side, mask_a, mask_b, section, 0, 0, 0]).astype(jnp.int32)

    metas = [meta_for(0), meta_for(1)]
    image = lax.dynamic_index_in_dim(images, section, 0, keepdims=False).reshape(PIX, C)
    cot = lax.dynamic_index_in_dim(cotangent, section, 0, keepdims=False).reshape(PIX, C)

    mats = [stacked[i][0] for i in MATRIX]
    lines = []
    for i in VECTORS:
        v = stacked[i][0]
        if i == 5:
            v = jnp.concatenate([jnp.zeros((64,), BF), v])
        lines.append(jnp.pad(v, (0, FF - v.shape[0])))
    lines += [jnp.zeros((FF,), BF)] * (VEC_ROWS - len(lines))
    vec = jnp.stack(lines)
    taps = jnp.pad(stacked[4][0], ((0, 0), (64, 0)))
    vec_other = links.to(vec, 1, 0)
    taps_other = links.to(taps, 1, 0)
    mats_other = [links.to(m, 1, 0) for m in mats]
    pairs = list(zip(mats, mats_other))
    is_first = section == 0

    def block_vec(block):
        use_own = is_first if block == 0 else jnp.logical_not(is_first)
        v = jnp.where(use_own, vec, vec_other).astype(F32)
        t = jnp.where(use_own, taps, taps_other).astype(F32)
        return v, t.reshape(49 * GROUPS, LANES), v[V_CB, :1024].reshape(GROUPS, LANES)

    small = [block_vec(0), block_vec(1)]
    field = image
    kept = []
    for block in (0, 1):
        v, t, cb = small[block]
        saved = run_forward(metas[block], field, v, t, cb, pairs)
        kept.append((field, saved))
        field = saved[-1]
    hidden, final = kept[0][1][-1], kept[1][1][-1]

    def to_sections(first, second):
        mine = jnp.where(is_first, first, second)
        other = links.to(jnp.where(is_first, second, first), 1, 0)
        low = jnp.where(is_first, mine, other)
        high = jnp.where(is_first, other, mine)
        return jnp.stack([low, high]).reshape(1, 2, 1, CANVAS, CANVAS, C)

    dy = cot
    dvs = [None, None]
    totals = [None, None]
    for block in (1, 0):
        v, t, cb = small[block]
        x, (n1, cin, mix, p, gl, mid, br, n2, act, slope, out, res) = kept[block]
        dmid, mvec, keep_m, send_m = run_mlp(metas[block], dy, v, n2, act, slope, out, mid, pairs)
        total_m = reduce_bucket(links, keep_m, send_m)
        dv, dvb, keep_g, send_g = run_gn(metas[block], x, dmid, mvec, v, t, n1, cin, mix, p, gl, br, pairs)
        total_g = reduce_bucket(links, keep_g, send_g)
        dvs[block] = dv
        dy = dvb
        totals[block] = (total_m, total_g)
    halves_m, halves_g = [None, None], [None, None]
    for block in (1, 0):
        own_m = gather_bucket(links, totals[block][0])
        halves_m[block] = (own_m, links.to(own_m, 1, 0, only=1 - block))
        own_g = gather_bucket(links, totals[block][1])
        halves_g[block] = (own_g, links.to(own_g, 1, 0, only=1 - block))
    wr, we = run_mlp_finish(metas[0], halves_m[0] + halves_m[1])
    (n1g, n1s, win, bin_, conv, w1, b1, w2, b2, w3, b3, wo, bo, bs, n2g, n2s, be, br, ms) = run_gn_finish(
        metas[0], halves_g[0] + halves_g[1]
    )
    block_outputs = to_sections(hidden, final)
    input_grads = to_sections(dvs[0], dvs[1])
    return (
        block_outputs, input_grads, n1g, n1s, win[None], bin_, conv[None, :49, 64:], conv[None, 49, 64:],
        w1[None], b1, w2[None], b2, w3[None], b3, wo[None], bo, bs, n2g, n2s, we[None], be, wr[None], br, ms,
    )


def solution(mesh):
    links = Links(mesh.shape["dp"])
    image = P(None, "dp", None, None, None)
    one, two = P("section", None), P("section", None, None)
    weights = (one, one, two, one, two, one, two, one, two, one, two, one, two, one, one, one, one, two, one, two,
               one, one)
    field = P("section", None, "dp", None, None, None)
    return jax.shard_map(
        functools.partial(on_device, links),
        mesh=mesh,
        in_specs=(image, image, P(None, "dp")) + weights,
        out_specs=(field, field) + weights,
        check_vma=False,
    )
```

```python
import functools

import jax
import jax.numpy as jnp
from jax import lax
from jax.experimental import pallas as pl
from jax.experimental.pallas import tpu as pltpu
from jax.sharding import PartitionSpec as P

SIDE_S = 8
SIDE_M = 12
CANVAS = 16
PIX = CANVAS * CANVAS
C = 512
FF = 2048
LANES = 128
GROUPS = 8
EPS = 1e-06
KS = 7
PAD_ROWS = (CANVAS + 6) * CANVAS
BF = jnp.bfloat16
F32 = jnp.float32
VMEM_BYTES = 56 * 1024 * 1024

V_N1G, V_N1S, V_BIN, V_CB, V_B1, V_B2, V_B3, V_BO, V_BS, V_N2G, V_N2S, V_BE, V_BR, V_MS = range(14)
VEC_ROWS = 16


def nn(a, b):
    return jnp.dot(a, b, preferred_element_type=F32)


def nt(a, b):
    return lax.dot_general(a, b, (((1,), (1,)), ((), ())), preferred_element_type=F32)


def tn(a, b):
    return lax.dot_general(a, b, (((0,), (0,)), ((), ())), preferred_element_type=F32)


def colsum(v):
    return jnp.sum(v, axis=0, keepdims=True)


def wide(m, n):
    return jnp.concatenate([m] * n, axis=1)


def place_of(block):
    section = lax.axis_index("section")
    place = lax.axis_index("dp") % 16
    x_bit, y_bit, z_at = place & 1, (place >> 1) & 1, place >> 2
    mask_a = section * 16 + x_bit * 8 + y_bit * 4 + z_at
    mask_b = section * 16 + y_bit * 8 + x_bit * 4 + z_at
    return section ^ block, section, (mask_a, mask_b)


def fill_mask(mask_ref, crop_ref, section):
    kind = crop_ref[section, 0]
    side = jnp.where(kind == 0, SIDE_S, jnp.where(kind == 1, SIDE_M, CANVAS))
    r = lax.broadcasted_iota(jnp.int32, (PIX, LANES), 0)
    inside = ((r // CANVAS) < side) & ((r % CANVAS) < side)
    mask_ref[...] = inside.astype(F32)


def start_select(sel, pairs, sems):
    for i, (own, other, dst) in enumerate(pairs):

        @pl.when(sel == 0)
        def _():
            pltpu.make_async_copy(own, dst, sems.at[i]).start()

        @pl.when(sel != 0)
        def _():
            pltpu.make_async_copy(other, dst, sems.at[i]).start()


def wait_select(i, pairs, sems):
    own, other, dst = pairs[i]
    pltpu.make_async_copy(own, dst, sems.at[i]).wait()


def conv_rows(src_ref, taps_ref, flip, bias, store):
    def row(h, carry):
        accs = [bias] * CANVAS if bias is not None else [None] * CANVAS
        for a in range(KS):
            ks = []
            for e in range(KS):
                t = (KS - 1 - a) * KS + (KS - 1 - e) if flip else a * KS + e
                ks.append(taps_ref[t * GROUPS : (t + 1) * GROUPS, :])
            for w2 in range(CANVAS):
                x = src_ref[pl.ds(pl.multiple_of(((h + a) * CANVAS + w2) * GROUPS, GROUPS), GROUPS), :]
                for e in range(KS):
                    w = w2 + 3 - e
                    if 0 <= w < CANVAS:
                        term = x * ks[e]
                        accs[w] = term if accs[w] is None else accs[w] + term
        for w in range(CANVAS):
            store(h * CANVAS + w, accs[w])
        return carry

    lax.fori_loop(0, CANVAS, row, 0)


def zero_border(ref):
    zeros = jnp.zeros((3 * CANVAS * GROUPS, LANES), F32)
    ref[0 : 3 * CANVAS * GROUPS, :] = zeros
    ref[(PAD_ROWS - 3 * CANVAS) * GROUPS :, :] = zeros


def lane_group(ref, g, rows=PIX, base=0):
    return ref[pl.ds(base + g, rows, stride=GROUPS), :]


def pack_kernel(*refs):
    vectors, taps_in, w1, w2, w3 = refs[:14], refs[14], refs[15], refs[16], refs[17]
    vec_ref, taps_ref, gates_ref = refs[18:]
    gates_ref[0:256, :] = w3[...]
    gates_ref[256:384, 0:256] = w2[...]
    gates_ref[256:384, 256:384] = jnp.concatenate([w1[...], jnp.zeros((64, 128), BF)], axis=0)
    gates_ref[256:384, 384:512] = jnp.zeros((128, 128), BF)
    vec_ref[...] = jnp.zeros_like(vec_ref)
    for row, ref in enumerate(vectors):
        n = ref.shape[1]
        vec_ref[row : row + 1, 0:n] = ref[...].astype(F32)
    taps = taps_in[...].astype(F32)
    bias = vectors[V_CB][...].astype(F32)
    for g in range(GROUPS):
        if g == 0:
            t = jnp.concatenate([jnp.zeros((49, 64), F32), taps[:, 0:64]], axis=1)
            b = jnp.concatenate([jnp.zeros((1, 64), F32), bias[:, 0:64]], axis=1)
        else:
            t = taps[:, g * LANES - 64 : g * LANES + 64]
            b = bias[:, g * LANES - 64 : g * LANES + 64]
        taps_ref[pl.ds(g, 49, stride=GROUPS), :] = t
        taps_ref[49 * GROUPS + g : 49 * GROUPS + g + 1, :] = b


def gn_forward_kernel(
    block, crop_ref, x_any, vec_a, vec_b, taps_a, taps_b,
    gates_a, gates_b, win_a, win_b, wo_a, wo_b,
    n1_ref, cin_ref, mix_ref, p_ref, gl_ref, mid_ref, br_ref,
    mask_ref, x_ref, vec_ref, taps_ref, mx_ref, gates, win, wo, sems,
):
    sel, section, _ = place_of(block)
    pairs = [
        (vec_a, vec_b, vec_ref), (win_a, win_b, win), (taps_a, taps_b, taps_ref), (gates_a, gates_b, gates),
        (wo_a, wo_b, wo),
    ]
    x_copy = pltpu.make_async_copy(x_any.at[section if block == 0 else 0], x_ref, sems.at[7])
    x_copy.start()
    start_select(sel, pairs, sems)
    fill_mask(mask_ref, crop_ref, section)
    zero_border(cin_ref)
    x_copy.wait()
    wait_select(0, pairs, sems)

    def vec(row, lo, n):
        return vec_ref[row : row + 1, lo : lo + n]

    def norm_in(i, carry):
        r = pl.ds(pl.multiple_of(i * 32, 32), 32)
        start = x_ref[r, :].astype(F32) * wide(mask_ref[r, :], 4)
        cen = start - jnp.mean(start, axis=-1, keepdims=True)
        inv = lax.rsqrt(jnp.mean(cen * cen, axis=-1, keepdims=True) + EPS)
        n1_ref[r, :] = (cen * inv * vec(V_N1G, 0, C) + vec(V_N1S, 0, C)).astype(BF)
        return carry

    lax.fori_loop(0, PIX // 32, norm_in, 0)
    wait_select(1, pairs, sems)
    for n in range(4):
        m = nn(n1_ref[...], win[:, n * 256 : (n + 1) * 256]) + vec(V_BIN, n * 256, 256)
        for half in range(2):
            g = 2 * n + half
            v = m[:, half * LANES : (half + 1) * LANES] * mask_ref[...]
            cin_ref[pl.ds(3 * CANVAS * GROUPS + g, PIX, stride=GROUPS), :] = v
            if g == 0:
                p_ref[:, 0:LANES] = v
    wait_select(2, pairs, sems)
    bias = taps_ref[49 * GROUPS : 50 * GROUPS, :]

    def keep(pixel, acc):
        mx_ref[pl.ds(pl.multiple_of(pixel * GROUPS, GROUPS), GROUPS), :] = acc * (1.0 / 3.0)

    conv_rows(cin_ref, taps_ref, False, bias, keep)
    for g in range(GROUPS):
        mix_ref[:, g * LANES : (g + 1) * LANES] = lane_group(mx_ref, g)
    wait_select(3, pairs, sems)
    wait_select(4, pairs, sems)
    gl_ref[:, 0:128] = (p_ref[:, 0:128] * pltpu.roll(mix_ref[:, 0:128], 64, 1)).astype(BF)
    p1 = nn(gl_ref[:, 0:128], gates[256:384, 256:384]) + vec(V_B1, 0, 128)
    p_ref[:, 128:256] = p1
    gl_ref[:, 128:256] = (p1 * mix_ref[:, 128:256]).astype(BF)
    p2 = nn(gl_ref[:, 128:256], gates[256:384, 0:256]) + vec(V_B2, 0, 256)
    p_ref[:, 256:512] = p2
    gl_ref[:, 256:512] = (p2 * mix_ref[:, 256:512]).astype(BF)
    for n in range(2):
        c = 256 * n
        p3 = nn(gl_ref[:, 256:512], gates[0:256, c : c + 256]) + vec(V_B3, c, 256)
        p_ref[:, 512 + c : 768 + c] = p3
        gl_ref[:, 512 + c : 768 + c] = (p3 * mix_ref[:, 512 + c : 768 + c]).astype(BF)
    for n in range(2):
        c = 256 * n
        br = nn(gl_ref[:, 512:1024], wo[:, c : c + 256]) + vec(V_BO, c, 256)
        br_ref[:, c : c + 256] = br.astype(BF)
        start = x_ref[:, c : c + 256].astype(F32) * wide(mask_ref[...], 2)
        mid_ref[:, c : c + 256] = start + vec(V_BS, c, 256) * br


def mlp_forward_kernel(
    block, crop_ref, field_ref, mid_ref, vec_a, vec_b, we_a, we_b, wr_a, wr_b,
    n2_ref, act_ref, slope_ref, out_ref, res_ref, swap_ref,
    mask_ref, vec_ref, we, wr, sems,
):
    sel, section, _ = place_of(block)
    pairs = [(vec_a, vec_b, vec_ref), (we_a, we_b, we), (wr_a, wr_b, wr)]
    start_select(sel, pairs, sems)
    fill_mask(mask_ref, crop_ref, section)
    wait_select(0, pairs, sems)

    def vec(row, lo, n):
        return vec_ref[row : row + 1, lo : lo + n]

    def norm_mid(i, carry):
        r = pl.ds(pl.multiple_of(i * 32, 32), 32)
        mid = mid_ref[r, :]
        cen = mid - jnp.mean(mid, axis=-1, keepdims=True)
        inv = lax.rsqrt(jnp.mean(cen * cen, axis=-1, keepdims=True) + EPS)
        n2_ref[r, :] = (cen * inv * vec(V_N2G, 0, C) + vec(V_N2S, 0, C)).astype(BF)
        return carry

    lax.fori_loop(0, PIX // 32, norm_mid, 0)
    wait_select(1, pairs, sems)
    for j in range(8):
        c = 256 * j
        pre = nn(n2_ref[...], we[:, c : c + 256]) + vec(V_BE, c, 256)
        cum = 0.5 * (1.0 + lax.erf(pre * 0.7071067811865476))
        act_ref[:, c : c + 256] = (pre * cum).astype(BF)
        slope = cum + pre * jnp.exp(-0.5 * pre * pre) * 0.3989422804014327
        slope_ref[:, c : c + 256] = slope.astype(BF)
    wait_select(2, pairs, sems)
    for n in range(2):
        c = 256 * n
        out = nn(act_ref[...], wr[:, c : c + 256]) + vec(V_BR, c, 256)
        out_ref[:, c : c + 256] = out.astype(BF)
        res = wide(mask_ref[...], 2) * (mid_ref[:, c : c + 256] + vec(V_MS, c, 256) * out)
        res_ref[:, c : c + 256] = res.astype(BF)
        if block == 1:
            swap_ref[:, c : c + 256] = jnp.where(section == 0, res.astype(BF), field_ref[0, :, c : c + 256])


def piece_rows(masks, p, rows):
    return pl.multiple_of((p ^ masks[p >> 4]) * rows, 64)


def mlp_kernel(
    block, crop_ref, dy_any, vec_a, vec_b, n2_ref, act_ref, slope_ref, out_ref, mid_ref, we_a, we_b, wr_a, wr_b, *rest,
):
    (dmid_ref, mvec_ref, keep_ref, send_ref,
     mask_ref, dy_ref, vec_ref, dout_ref, dpre_ref, dn2_ref, bucket, we, wr, sems) = rest[-14:]
    sel, section, masks = place_of(block)
    pairs = [(vec_a, vec_b, vec_ref), (wr_a, wr_b, wr), (we_a, we_b, we)]
    dy_copy = pltpu.make_async_copy(dy_any.at[section if block == 1 else 0], dy_ref, sems.at[3])
    dy_copy.start()
    start_select(sel, pairs, sems)
    fill_mask(mask_ref, crop_ref, section)
    mvec_ref[...] = jnp.zeros_like(mvec_ref)
    dy_copy.wait()
    wait_select(0, pairs, sems)

    def vec(row, lo, n):
        return vec_ref[row : row + 1, lo : lo + n]

    for n in range(2):
        c = 256 * n
        dyr = dy_ref[:, c : c + 256].astype(F32) * wide(mask_ref[...], 2)
        dmid_ref[:, c : c + 256] = dyr
        dout = (vec(V_MS, c, 256) * dyr).astype(BF)
        dout_ref[:, c : c + 256] = dout
        mvec_ref[3:4, c : c + 256] = colsum(dout.astype(F32))
        mvec_ref[4:5, c : c + 256] = colsum(dyr * out_ref[:, c : c + 256].astype(F32))
    wait_select(1, pairs, sems)
    for j in range(8):
        c = 256 * j
        dw = tn(act_ref[:, c : c + 256], dout_ref[...]).astype(BF)
        for q in range(4):
            bucket[pl.ds(piece_rows(masks, 4 * j + q, 128), 64), :] = dw[64 * q : 64 * q + 64, :]
        dact = nt(dout_ref[...], wr[c : c + 256, :])
        dpre = (dact * slope_ref[:, c : c + 256].astype(F32)).astype(BF)
        dpre_ref[:, c : c + 256] = dpre
        mvec_ref[2:3, c : c + 256] = colsum(dpre.astype(F32))
    wait_select(2, pairs, sems)
    for cb in range(4):
        dw = tn(n2_ref[...], dpre_ref[:, 512 * cb : 512 * cb + 512]).astype(BF)
        for q in range(8):
            rows = pl.multiple_of(piece_rows(masks, 8 * cb + q, 128) + 64, 64)
            bucket[pl.ds(rows, 64), :] = dw[64 * q : 64 * q + 64, :]
    keep_copy = pltpu.make_async_copy(bucket.at[0:2048], keep_ref, sems.at[4])
    send_copy = pltpu.make_async_copy(bucket.at[2048:4096], send_ref, sems.at[5])
    send_copy.start()
    keep_copy.start()
    for n in range(2):
        c = 256 * n
        dn2_ref[:, c : c + 256] = nt(dpre_ref[...], we[c : c + 256, :])

    def norm_back(i, carry):
        dgain, dshift = carry
        r = pl.ds(pl.multiple_of(i * 32, 32), 32)
        mid = mid_ref[r, :]
        cen = mid - jnp.mean(mid, axis=-1, keepdims=True)
        inv = lax.rsqrt(jnp.mean(cen * cen, axis=-1, keepdims=True) + EPS)
        xhat = cen * inv
        up = dn2_ref[r, :]
        g = up * vec(V_N2G, 0, C)
        inner = g - jnp.mean(g, axis=-1, keepdims=True) - xhat * jnp.mean(g * xhat, axis=-1, keepdims=True)
        dmid_ref[r, :] = dmid_ref[r, :] + inv * inner
        return dgain + colsum(up * xhat), dshift + colsum(up)

    zero = jnp.zeros((1, C), F32)
    dgain, dshift = lax.fori_loop(0, PIX // 32, norm_back, (zero, zero))
    mvec_ref[0:1, 0:C] = dgain
    mvec_ref[1:2, 0:C] = dshift
    send_copy.wait()
    keep_copy.wait()


def gn_back_kernel(
    block, crop_ref, x_any, next_any, dmid_ref, mvec_ref, vec_a, vec_b, taps_a, taps_b, gates_a, gates_b,
    mix_ref, p_ref, gl_ref, br_ref, win_a, win_b, wo_a, wo_b, *rest,
):
    (dv_ref, dvb_ref, dbr_ref, dp_ref, dmg_ref, dcp_ref, gvec_ref, swap_ref,
     mask_ref, x_ref, next_ref, vec_ref, taps_ref, dg_ref, dmix_ref, ds_ref, dn1_ref, gates, win, wo, sems) = rest[-21:]
    sel, section, _ = place_of(block)
    pairs = [
        (vec_a, vec_b, vec_ref), (wo_a, wo_b, wo), (gates_a, gates_b, gates), (taps_a, taps_b, taps_ref),
        (win_a, win_b, win),
    ]
    x_copy = pltpu.make_async_copy(x_any.at[section if block == 0 else 0], x_ref, sems.at[7])
    start_select(sel, pairs, sems)
    x_copy.start()
    if block == 0:
        next_copy = pltpu.make_async_copy(next_any, next_ref, sems.at[5])
        next_copy.start()
    fill_mask(mask_ref, crop_ref, section)
    zero_border(dcp_ref)
    wait_select(0, pairs, sems)

    def vec(row, lo, n):
        return vec_ref[row : row + 1, lo : lo + n]

    dbs, dbo = [], []
    for n in range(2):
        c = 256 * n
        dm = dmid_ref[:, c : c + 256]
        dbs.append(colsum(dm * br_ref[:, c : c + 256].astype(F32)))
        dbr = (vec(V_BS, c, 256) * dm).astype(BF)
        dbr_ref[:, c : c + 256] = dbr
        dbo.append(colsum(dbr.astype(F32)))
    wait_select(1, pairs, sems)
    wait_select(2, pairs, sems)
    db3 = []
    for n in range(2):
        c = 256 * n
        dg = nt(dbr_ref[...], wo[c : c + 256, :])
        dp = (dg * mix_ref[:, 512 + c : 768 + c]).astype(BF)
        dmix_ref[:, 512 + c : 768 + c] = dg * p_ref[:, 512 + c : 768 + c] * (1.0 / 3.0)
        dp_ref[:, 512 + c : 768 + c] = dp
        db3.append(colsum(dp.astype(F32)))
    dg = nt(dp_ref[:, 512:1024], gates[0:256, :])
    dp = (dg * mix_ref[:, 256:512]).astype(BF)
    dmix_ref[:, 256:512] = dg * p_ref[:, 256:512] * (1.0 / 3.0)
    dp_ref[:, 256:512] = dp
    db2 = colsum(dp.astype(F32))
    dg = nt(dp_ref[:, 256:512], gates[256:384, 0:256])
    dp = (dg * mix_ref[:, 128:256]).astype(BF)
    dmix_ref[:, 128:256] = dg * p_ref[:, 128:256] * (1.0 / 3.0)
    dp_ref[:, 128:256] = dp
    db1 = colsum(dp.astype(F32))
    dg = nt(dp_ref[:, 128:256], gates[256:384, 256:384])
    dmix_ref[:, 0:128] = pltpu.roll(dg * p_ref[:, 0:128], 64, 1) * (1.0 / 3.0)
    dg_ref[...] = dg * pltpu.roll(mix_ref[:, 0:128], 64, 1)
    dp_ref[:, 0:128] = jnp.zeros((PIX, LANES), BF)
    for g in range(GROUPS):
        dcp_ref[pl.ds(3 * CANVAS * GROUPS + g, PIX, stride=GROUPS), :] = dmix_ref[:, g * LANES : (g + 1) * LANES]
    wait_select(3, pairs, sems)

    def keep(pixel, acc):
        ds_ref[pl.ds(pl.multiple_of(pixel * GROUPS, GROUPS), GROUPS), :] = acc

    conv_rows(dcp_ref, taps_ref, True, None, keep)
    dbin = []
    for g in range(GROUPS):
        d = lane_group(ds_ref, g) * mask_ref[...]
        if g == 0:
            d = d + dg_ref[...]
        d = d.astype(BF)
        dmg_ref[:, g * LANES : (g + 1) * LANES] = d
        dbin.append(colsum(d.astype(F32)))
    wait_select(4, pairs, sems)
    x_copy.wait()
    if block == 0:
        next_copy.wait()
    for n in range(2):
        c = 256 * n
        dn1_ref[:, c : c + 256] = nt(dmg_ref[...], win[c : c + 256, :])

    def norm_back(i, carry):
        dgain, dshift = carry
        r = pl.ds(pl.multiple_of(i * 32, 32), 32)
        m = wide(mask_ref[r, :], 4)
        start = x_ref[r, :].astype(F32) * m
        cen = start - jnp.mean(start, axis=-1, keepdims=True)
        inv = lax.rsqrt(jnp.mean(cen * cen, axis=-1, keepdims=True) + EPS)
        xhat = cen * inv
        up = dn1_ref[r, :]
        g = up * vec(V_N1G, 0, C)
        inner = g - jnp.mean(g, axis=-1, keepdims=True) - xhat * jnp.mean(g * xhat, axis=-1, keepdims=True)
        dv = m * (dmid_ref[r, :] + inv * inner)
        dv_ref[r, :] = dv
        dvb_ref[r, :] = dv.astype(BF)
        if block == 0:
            swap_ref[r, :] = jnp.where(section == 0, next_ref[r, :], dv)
        return dgain + colsum(up * xhat), dshift + colsum(up)

    zero = jnp.zeros((1, C), F32)
    dgain, dshift = lax.fori_loop(0, PIX // 32, norm_back, (zero, zero))
    z = jnp.zeros((1, LANES), F32)
    rows = [
        dgain,
        dshift,
        jnp.concatenate(dbin[0:4], axis=1),
        jnp.concatenate(dbin[4:8], axis=1),
        jnp.concatenate([db1, z, z, z], axis=1),
        jnp.concatenate([db2, z, z], axis=1),
        jnp.concatenate(db3, axis=1),
        jnp.concatenate(dbo, axis=1),
        jnp.concatenate(dbs, axis=1),
        mvec_ref[0:1, 0:C],
        mvec_ref[1:2, 0:C],
        mvec_ref[2:3, 0:512],
        mvec_ref[2:3, 512:1024],
        mvec_ref[2:3, 1024:1536],
        mvec_ref[2:3, 1536:2048],
        mvec_ref[3:4, 0:C],
        mvec_ref[4:5, 0:C],
    ]
    rows.append(jnp.zeros((32 - len(rows), C), F32))
    gvec_ref[...] = jnp.concatenate(rows, axis=0).astype(BF)


def gn_weights_kernel(block, n1_ref, gl_ref, dbr_ref, dp_ref, dmg_ref, gvec_ref, cin_any, dcp_any, *rest):
    keep_ref, send_ref, dk_ref, cin_ref, dcp_ref, bucket, sems = rest[-7:]
    _, _, masks = place_of(block)
    cin_copy = pltpu.make_async_copy(cin_any, cin_ref, sems.at[0])
    dcp_copy = pltpu.make_async_copy(dcp_any, dcp_ref, sems.at[1])
    cin_copy.start()
    dcp_copy.start()

    def put(p, val, sub=0):
        n = val.shape[0]
        bucket[pl.ds(pl.multiple_of(piece_rows(masks, p, 64) + sub, 16), n), :] = val

    for cb in range(2):
        dw = tn(n1_ref[...], dmg_ref[:, 512 * cb : 512 * cb + 512]).astype(BF)
        for q in range(8):
            put(8 * cb + q, dw[64 * q : 64 * q + 64, :])
    dw = tn(gl_ref[:, 512:1024], dbr_ref[...]).astype(BF)
    for q in range(8):
        put(16 + q, dw[64 * q : 64 * q + 64, :])
    dw = tn(gl_ref[:, 256:512], dp_ref[:, 512:1024]).astype(BF)
    for q in range(4):
        put(24 + q, dw[64 * q : 64 * q + 64, :])
    dw = tn(gl_ref[:, 128:256], dp_ref[:, 256:512]).astype(BF)
    put(28, jnp.concatenate([dw[0:64, :], dw[64:128, :]], axis=1))
    dw1 = tn(gl_ref[:, 0:128], dp_ref[:, 128:256]).astype(BF)
    put(31, jnp.concatenate([dw1[16 * i : 16 * i + 16, :] for i in range(4)], axis=1))
    put(31, jnp.zeros((16, 512), BF), 16)
    put(31, gvec_ref[...], 32)
    cin_copy.wait()
    dcp_copy.wait()

    def vreg(ref, index):
        return ref[pl.ds(pl.multiple_of(index * GROUPS, GROUPS), GROUPS), :]

    dk_ref[...] = jnp.zeros_like(dk_ref)
    for taps in ((0, 1), (2, 3), (4, 5), (6,)):

        def row(h, accs):
            accs = list(accs)
            ds = [vreg(dcp_ref, (h + 3) * CANVAS + w) for w in range(CANVAS)]
            for i, a in enumerate(taps):
                for w2 in range(CANVAS):
                    x = vreg(cin_ref, (h + a) * CANVAS + w2)
                    for e in range(KS):
                        w = w2 + 3 - e
                        if 0 <= w < CANVAS:
                            accs[i * KS + e] = accs[i * KS + e] + x * ds[w]
            if len(taps) == 1:
                for w in range(CANVAS):
                    accs[KS] = accs[KS] + ds[w]
            return tuple(accs)

        count = len(taps) * KS + (1 if len(taps) == 1 else 0)
        accs = lax.fori_loop(0, CANVAS, row, tuple(jnp.zeros((GROUPS, LANES), F32) for _ in range(count)))
        for i in range(count):
            t = taps[0] * KS + i
            dk_ref[t * GROUPS : (t + 1) * GROUPS, :] = accs[i]
    for half in range(2):
        dk = jnp.concatenate([lane_group(dk_ref, 4 * half + i, 64) for i in range(4)], axis=1).astype(BF)
        put(29 + half, dk)
    send_copy = pltpu.make_async_copy(bucket.at[1024:2048], send_ref, sems.at[2])
    keep_copy = pltpu.make_async_copy(bucket.at[0:1024], keep_ref, sems.at[3])
    send_copy.start()
    keep_copy.start()
    send_copy.wait()
    keep_copy.wait()


def start_pieces(layout, rows, halves, buf, sems):
    _, section, masks = place_of(0)
    for p in range(32):
        rel = p ^ masks[p >> 4]
        far = rel >> 4
        dst = buf.at[p * rows : (p + 1) * rows]
        sem = sems.at[p // 4]
        for sec in range(2):
            stride, first = layout[sec]
            off = pl.multiple_of((rel & 15) * stride + first, 64)
            for side in range(2):

                @pl.when((section == sec) & (far == side))
                def _():
                    pltpu.make_async_copy(halves[2 * sec + side].at[pl.ds(off, rows)], dst, sem).start()


def wait_pieces(i, rows, halves, buf, sems):
    part = buf.at[pl.ds(i * 4 * rows, 4 * rows)]
    pltpu.make_async_copy(halves[0].at[pl.ds(0, 4 * rows)], part, sems.at[i]).wait()


def mlp_finish_kernel(layout, *refs):
    halves = refs[:4]
    wr_any, we_any, buf, wr_ref, we_ref, sems, out_sems = refs[-7:]
    start_pieces(layout, 128, halves, buf, sems)
    copies = []
    for i in range(8):
        wait_pieces(i, 128, halves, buf, sems)
        cb = i // 2
        for q in range(4):
            p = 4 * i + q
            r = p % 8
            wr_ref[64 * p : 64 * p + 64, :] = buf[128 * p : 128 * p + 64, :].astype(F32)
            we_ref[64 * r : 64 * r + 64, 512 * cb : 512 * cb + 512] = buf[128 * p + 64 : 128 * p + 128, :].astype(F32)
        rows = slice(256 * i, 256 * i + 256)
        copies.append(pltpu.make_async_copy(wr_ref.at[rows], wr_any.at[rows], out_sems.at[i]))
        half = slice(256 * (i % 2), 256 * (i % 2) + 256)
        cols = slice(512 * cb, 512 * cb + 512)
        copies.append(pltpu.make_async_copy(we_ref.at[half, cols], we_any.at[half, cols], out_sems.at[8 + i]))
        copies[-2].start()
        copies[-1].start()
    for copy in copies:
        copy.wait()


def gn_finish_kernel(layout, *refs):
    halves = refs[:4]
    (n1g, n1s, win, bin_, conv, cbias, w1, b1, w2, b2, w3, b3, wo, bo, bs, n2g, n2s, be, br, ms, buf, sems) = refs[-22:]
    start_pieces(layout, 64, halves, buf, sems)
    for i in range(8):
        wait_pieces(i, 64, halves, buf, sems)
    for cb in range(2):
        win[:, 512 * cb : 512 * cb + 512] = buf[512 * cb : 512 * cb + 512, :].astype(F32)
    wo[...] = buf[1024:1536, :].astype(F32)
    w3[...] = buf[1536:1792, :].astype(F32)
    for i in range(2):
        w2[64 * i : 64 * i + 64, :] = buf[1792:1856, 256 * i : 256 * i + 256].astype(F32)
    for i in range(4):
        w1[16 * i : 16 * i + 16, :] = buf[1984:2000, 128 * i : 128 * i + 128].astype(F32)
    taps = jnp.concatenate([buf[1856:1920, :], buf[1920:1984, :]], axis=1).astype(F32)
    conv[...] = taps[0:49, 64:1024]
    cbias[...] = taps[49:50, 64:1024]
    v = buf[2016:2048, :].astype(F32)
    n1g[...] = v[0:1]
    n1s[...] = v[1:2]
    bin_[:, 0:512] = v[2:3]
    bin_[:, 512:1024] = v[3:4]
    b1[...] = v[4:5, 0:128]
    b2[...] = v[5:6, 0:256]
    b3[...] = v[6:7]
    bo[...] = v[7:8]
    bs[...] = v[8:9]
    n2g[...] = v[9:10]
    n2s[...] = v[10:11]
    for i in range(4):
        be[:, 512 * i : 512 * i + 512] = v[11 + i : 12 + i]
    br[...] = v[15:16]
    ms[...] = v[16:17]


def place_kernel(first, second, got, out):
    section = lax.axis_index("section")

    @pl.when(section == 0)
    def _():
        out[0] = first[...]
        out[1] = got[...]

    @pl.when(section != 0)
    def _():
        out[0] = got[...]
        out[1] = second[...]


SMEM = pl.BlockSpec(memory_space=pltpu.SMEM)
VM = pl.BlockSpec(memory_space=pltpu.VMEM)
ANY = pl.BlockSpec(memory_space=pl.ANY)


def sds(shape, dtype):
    return jax.ShapeDtypeStruct(shape, dtype)


def vmem(rows, cols, dtype):
    return pltpu.VMEM((rows, cols), dtype)


def call(kernel, name, operands, outs, scratch, micros):
    return pl.pallas_call(
        kernel,
        name=name,
        out_shape=[shape for _, shape in outs],
        in_specs=[spec for spec, _ in operands],
        out_specs=[spec for spec, _ in outs],
        scratch_shapes=scratch,
        compiler_params=pltpu.CompilerParams(vmem_limit_bytes=VMEM_BYTES),
        cost_estimate=pl.CostEstimate(flops=int(micros * 1e9), bytes_accessed=int(micros * 3e6), transcendentals=0),
    )(*[array for _, array in operands])


def on(spec, *arrays):
    return [(spec, a) for a in arrays]


SMALL = [vmem(VEC_ROWS, FF, F32)]
TAPS = [vmem(50 * GROUPS, LANES, F32)]
GN_MATS = [vmem(384, 512, BF), vmem(C, 1024, BF), vmem(512, 512, BF)]
FIELD_F32, FIELD_BF = sds((PIX, C), F32), sds((PIX, C), BF)
CONV_F32 = sds((PAD_ROWS * GROUPS, LANES), F32)
WIDE_F32, WIDE_BF = sds((PIX, 1024), F32), sds((PIX, 1024), BF)


def run_pack(vectors, taps, gates):
    outs = on(VM, sds((VEC_ROWS, FF), F32), sds((50 * GROUPS, LANES), F32), sds((384, 512), BF))
    return call(pack_kernel, "pack", on(VM, *vectors, taps, *gates), outs, [], 2)


def run_gn_forward(block, crop, x, small, mats):
    flat = [r for pair in mats[:2] for r in pair]
    outs = on(VM, FIELD_BF, CONV_F32, WIDE_F32, WIDE_F32, WIDE_BF, FIELD_F32, FIELD_BF)
    scratch = [vmem(PIX, LANES, F32), vmem(PIX, C, BF)] + SMALL + TAPS + [vmem(PIX * GROUPS, LANES, F32)] + GN_MATS
    scratch += [pltpu.SemaphoreType.DMA((8,))]
    return call(functools.partial(gn_forward_kernel, block), "gnconv_forward",
                on(SMEM, crop) + on(ANY, x, *small, *flat), outs, scratch, 8)


def run_mlp_forward(block, crop, field, mid, small, mats):
    outs = on(VM, FIELD_BF, sds((PIX, FF), BF), sds((PIX, FF), BF), FIELD_BF, FIELD_BF)
    outs += on(VM, FIELD_BF) if block == 1 else on(ANY, FIELD_BF)
    scratch = [vmem(PIX, LANES, F32)] + SMALL + [vmem(C, FF, BF), vmem(FF, C, BF), pltpu.SemaphoreType.DMA((3,))]
    return call(functools.partial(mlp_forward_kernel, block), "mlp_forward",
                on(SMEM, crop) + on(VM if block == 1 else ANY, field) + on(VM, mid) + on(ANY, *small[:2], *mats[2], *mats[3]),
                outs, scratch, 5)


def run_mlp_back(block, crop, dy, small, n2, act, slope, out, mid, mats):
    outs = on(VM, FIELD_F32, sds((8, FF), F32)) + on(ANY, sds((2048, 512), BF), sds((2048, 512), BF))
    scratch = [vmem(PIX, LANES, F32), vmem(PIX, C, BF)] + SMALL + [
        vmem(PIX, C, BF), vmem(PIX, FF, BF), vmem(PIX, C, F32), vmem(4096, 512, BF), vmem(C, FF, BF), vmem(FF, C, BF),
        pltpu.SemaphoreType.DMA((6,)),
    ]
    operands = on(SMEM, crop) + on(ANY, dy, *small[:2]) + on(VM, n2, act, slope, out, mid)
    operands += on(ANY, *mats[2], *mats[3])
    return call(functools.partial(mlp_kernel, block), "mlp_backward", operands, outs, scratch, 2)


def run_gn_back(block, crop, x, following, dmid, mvec, small, mix, p, gl, br, mats):
    flat = [r for pair in mats[:2] for r in pair]
    outs = on(VM, FIELD_F32, FIELD_BF, FIELD_BF, WIDE_BF, WIDE_BF, CONV_F32, sds((32, 512), BF))
    outs += on(VM if block == 0 else ANY, FIELD_F32)
    scratch = [vmem(PIX, LANES, F32), vmem(PIX, C, BF), vmem(PIX, C, F32)] + SMALL + TAPS + [
        vmem(PIX, LANES, F32), vmem(PIX, 1024, F32), vmem(PIX * GROUPS, LANES, F32), vmem(PIX, C, F32),
    ] + GN_MATS + [pltpu.SemaphoreType.DMA((8,))]
    operands = on(SMEM, crop) + on(ANY, x, following) + on(VM, dmid, mvec) + on(ANY, *small) + on(VM, mix, p, gl, br)
    operands += on(ANY, *flat)
    return call(functools.partial(gn_back_kernel, block), "gnconv_backward", operands, outs, scratch, 2)


def run_gn_weights(block, n1, gl, dbr, dp, dmg, gvec, cin, dcp):
    outs = on(ANY, sds((1024, 512), BF), sds((1024, 512), BF))
    scratch = [vmem(64 * GROUPS, LANES, F32), vmem(PAD_ROWS * GROUPS, LANES, F32), vmem(PAD_ROWS * GROUPS, LANES, F32),
               vmem(2048, 512, BF), pltpu.SemaphoreType.DMA((4,))]
    operands = on(VM, n1, gl, dbr, dp, dmg, gvec) + on(ANY, cin, dcp)
    return call(functools.partial(gn_weights_kernel, block), "gnconv_weights", operands, outs, scratch, 2)


def turn_kernel(token, out):
    out[...] = jnp.zeros_like(out)


def run_turn(token):
    return call(turn_kernel, "turn", on(ANY, token), on(VM, sds((8, LANES), F32)), [], 0.1)[0]


def run_mlp_finish(layout, halves):
    outs = on(ANY, sds((FF, C), F32), sds((C, FF), F32))
    scratch = [vmem(4096, 512, BF), vmem(FF, C, F32), vmem(C, FF, F32), pltpu.SemaphoreType.DMA((8,)),
               pltpu.SemaphoreType.DMA((16,))]
    return call(functools.partial(mlp_finish_kernel, layout), "mlp_finish", on(ANY, *halves), outs, scratch, 20)


def run_gn_finish(layout, halves):
    widths = [512, 512, (512, 1024), 1024, (49, 960), 960, (64, 128), 128, (128, 256), 256, (256, 512), 512,
              (512, 512), 512, 512, 512, 512, 2048, 512, 512]
    outs = on(VM, *[sds((1, w) if isinstance(w, int) else w, F32) for w in widths])
    scratch = [vmem(2048, 512, BF), pltpu.SemaphoreType.DMA((8,))]
    return call(functools.partial(gn_finish_kernel, layout), "gn_finish", on(ANY, *halves), outs, scratch, 3)


def run_place(first, second, got):
    outs = on(VM, sds((2, PIX, C), first.dtype))
    return call(place_kernel, "place", on(VM, first, second, got), outs, [], 0.1)[0]


AXES = ("section", "dp")
X_BIT, Y_BIT, Z_LOW, Z_HIGH = 1, 2, 4, 8


def after(x, *others):
    return lax.optimization_barrier((x,) + others)[0]


class Links:
    def __init__(self, count):
        self.count = count
        self.token = None

    def send(self, x, section_flip, flips, only=None):
        n = self.count
        pairs = [
            (s * n + d, (s ^ section_flip) * n + (d ^ flips[s]))
            for s in range(2)
            for d in range(n)
            if only is None or s == only
        ]
        got = lax.ppermute(x, AXES, pairs)
        return got if self.token is None else after(got, self.token)

    def core(self, x, only=None):
        return self.send(x, 1, (0, 0), only)

    def first(self, x):
        return self.send(x, 0, (X_BIT, Y_BIT))

    def second(self, x):
        return self.send(x, 0, (Y_BIT, X_BIT))

    def low(self, x):
        return self.send(x, 0, (Z_LOW, Z_LOW))

    def high(self, x):
        return self.send(x, 0, (Z_HIGH, Z_HIGH))


def sum_core(links, keep, send):
    return (keep + links.core(send)).reshape(2, 2, 2, 2, keep.shape[0] // 16, 512)


def sum_first(links, parts):
    return parts[0] + links.first(parts[1])


def sum_second(links, parts):
    return parts[0] + links.second(parts[1])


def sum_low(links, parts):
    return parts[:, 0] + links.low(parts[:, 1])


def sum_high(links, parts):
    total = parts[0] + links.high(parts[1])
    chips = links.count // 16
    if chips > 1:
        groups = [[g * 16 + r for g in range(chips)] for r in range(16)]
        total = lax.psum(total, "dp", axis_index_groups=groups)
    return total


def gather_high(links, total):
    return jnp.stack([total, links.high(total)])


def gather_low(links, whole):
    return jnp.stack([whole, links.low(whole)], axis=1)


def gather_second(links, parts):
    return jnp.stack([parts, links.second(parts)])


def gather_first(links, parts):
    return jnp.stack([parts, links.first(parts)]).reshape(-1, 512)


VECTORS = (0, 1, 3, 5, 7, 9, 11, 13, 14, 15, 16, 18, 20, 21)


def on_device(links, images, cotangent, crop, *stacked):
    images = images.reshape(2, PIX, C)
    cotangent = cotangent.reshape(2, PIX, C)
    win, wo, we, wr = [stacked[i][0] for i in (2, 12, 17, 19)]
    vec, taps, gates = run_pack([stacked[i] for i in VECTORS], stacked[4][0], [stacked[i][0] for i in (6, 8, 10)])
    win_other, wo_other = links.core(win), links.core(wo)
    taps_other, vec_other, gates_other = links.core(taps), links.core(vec), links.core(gates)
    we, wr = after((we, wr), win_other, wo_other, taps_other, vec_other, gates_other)
    we_other, wr_other = links.core(we), links.core(wr)
    pairs = [(win, win_other), (wo, wo_other), (we, we_other), (wr, wr_other)]
    small = (vec, vec_other, taps, taps_other, gates, gates_other)

    field = images
    kept = []
    for block in (0, 1):
        gn = run_gn_forward(block, crop, field, small, pairs)
        mlp = run_mlp_forward(block, crop, field, gn[5], small, pairs)
        kept.append((field, gn, mlp))
        field = mlp[4].reshape(1, PIX, C)
    hidden, final, field_swap = kept[0][2][4], kept[1][2][4], kept[1][2][5]

    def mlp_back(block, dy):
        _, gn, (n2, act, slope, out, _, _) = kept[block]
        return run_mlp_back(block, crop, dy, small, n2, act, slope, out, gn[5], pairs)

    def gn_back(block, following, dmid, mvec):
        x, (_, _, mix, p, gl, _, br), _ = kept[block]
        return run_gn_back(block, crop, x, following, dmid, mvec, small, mix, p, gl, br, pairs)

    def gn_weights(block, back, gvec):
        _, (n1, cin, _, _, gl, _, _), _ = kept[block]
        _, _, dbr, dp, dmg, dcp, _, _ = back
        return run_gn_weights(block, n1, gl, dbr, dp, dmg, gvec, cin, dcp)

    together = lax.optimization_barrier
    dmid, mvec, keep_m, send_m = mlp_back(1, cotangent)

    keep_m, send_m, dmid = together((keep_m, send_m, dmid))
    back1 = gn_back(1, mvec, dmid, mvec)
    links.token = back1[6]
    m1 = sum_core(links, keep_m, send_m)

    m1, gvec = together((m1, back1[6]))
    keep_g, send_g = gn_weights(1, back1, gvec)
    links.token = keep_g
    m1 = sum_first(links, m1)

    m1, keep_g, send_g, dvb = together((m1, keep_g, send_g, back1[1]))
    dmid, mvec, keep_m, send_m = mlp_back(0, dvb.reshape(1, PIX, C))
    links.token = mvec
    m1 = sum_second(links, m1)
    g1 = sum_core(links, keep_g, send_g)

    m1, g1, keep_m, send_m, dmid = together((m1, g1, keep_m, send_m, dmid))
    back0 = gn_back(0, back1[0], dmid, mvec)
    links.token = back0[6]
    m1 = sum_low(links, m1)
    g1 = sum_first(links, g1)
    m0 = sum_core(links, keep_m, send_m)

    m1, g1, m0, gvec = together((m1, g1, m0, back0[6]))
    keep_g, send_g = gn_weights(0, back0, gvec)
    links.token = keep_g
    m1 = sum_high(links, m1)
    g1 = sum_second(links, g1)
    m0 = sum_first(links, m0)

    def turn(*values):
        *values, token = together(values + (links.token,))
        links.token = run_turn(token)
        return values

    m1, g1, m0, keep_g, send_g = turn(m1, g1, m0, keep_g, send_g)
    g0 = sum_core(links, keep_g, send_g)
    m0 = sum_second(links, m0)
    g1 = sum_low(links, g1)
    m1 = gather_high(links, m1)

    m1, g1, m0, g0, field_swap, grad_swap = turn(m1, g1, m0, g0, field_swap, back0[7])
    g0 = sum_first(links, g0)
    m1 = gather_low(links, m1)
    g1 = sum_high(links, g1)
    m0 = sum_low(links, m0)
    field_got, grad_got = links.core(field_swap), links.core(grad_swap)

    m1, g1, m0, g0, field_got, grad_got = together((m1, g1, m0, g0, field_got, grad_got))
    links.token = block_outputs = run_place(hidden, final, field_got)
    g0 = sum_second(links, g0)
    m1 = gather_second(links, m1)
    m0 = sum_high(links, m0)

    m1, m0, g0, grad_got, block_outputs = together((m1, m0, g0, grad_got, block_outputs))
    links.token = input_grads = run_place(back0[0], back1[0], grad_got)
    g0 = sum_low(links, g0)
    gm = gather_high(links, jnp.concatenate([m0, g1], axis=0))

    gm, g0, input_grads = turn(gm, g0, input_grads)
    all_m1 = gather_first(links, m1)
    g0 = sum_high(links, g0)
    gm = gather_low(links, gm)

    gm, g0, all_m1 = turn(gm, g0, all_m1)
    g0 = gather_high(links, g0)
    gm = gather_second(links, gm)
    got_m1 = links.core(all_m1, only=0)

    gm, g0, got_m1 = turn(gm, g0, got_m1)
    g0 = gather_low(links, g0)

    (g0,) = turn(g0)
    g0 = gather_second(links, g0)
    all_gm = gather_first(links, gm)

    all_gm, g0 = turn(all_gm, g0)
    all_g0 = gather_first(links, g0)
    got_gm = links.core(all_gm)

    got_gm, all_g0 = together((got_gm, all_g0))
    wr, we = run_mlp_finish(((192, 0), (128, 0)), (all_gm, got_gm, all_m1, got_m1))
    links.token = wr
    got_g0 = links.core(all_g0, only=1)
    (n1g, n1s, win, bin_, conv, cbias, w1, b1, w2, b2, w3, b3, wo, bo, bs, n2g, n2s, be, br, ms) = run_gn_finish(
        ((64, 0), (192, 128)), (all_g0, got_g0, all_gm, got_gm)
    )
    shape = (1, 2, 1, CANVAS, CANVAS, C)
    return (
        block_outputs.reshape(shape), input_grads.reshape(shape), n1g, n1s, win[None], bin_, conv[None], cbias,
        w1[None], b1, w2[None], b2, w3[None], b3, wo[None], bo, bs, n2g, n2s, we[None], be, wr[None], br, ms,
    )


def solution(mesh):
    links = Links(mesh.shape["dp"])
    image = P(None, "dp", None, None, None)
    one, two = P("section", None), P("section", None, None)
    weights = (one, one, two, one, two, one, two, one, two, one, two, one, two, one, one, one, one, two, one, two,
               one, one)
    field = P("section", None, "dp", None, None, None)
    return jax.shard_map(
        functools.partial(on_device, links),
        mesh=mesh,
        in_specs=(image, image, P(None, "dp")) + weights,
        out_specs=(field, field) + weights,
        check_vma=False,
    )
```

```python
import functools
import math

import jax
import jax.numpy as jnp
from jax import lax
from jax.experimental import pallas as pl
from jax.experimental.pallas import tpu as pltpu
from jax.sharding import PartitionSpec as P

SIDE_S = 8
SIDE_M = 12
CANVAS = 16
PIX = CANVAS * CANVAS
C = 512
FF = 2048
LANES = 128
GROUPS = 8
EPS = 1e-06
KS = 7
PAD_ROWS = (CANVAS + 6) * CANVAS
BF = jnp.bfloat16
F32 = jnp.float32
SPARE_VMEM = 8 * 1024 * 1024
MOST_VMEM = 58 * 1024 * 1024

V_N1G, V_N1S, V_BIN, V_CB, V_B1, V_B2, V_B3, V_BO, V_BS, V_N2G, V_N2S, V_BE, V_BR, V_MS = range(14)
VEC_ROWS = 16


class Slot:
    def __init__(self, ref, copy):
        self.ref, self.copy = ref, copy

    def get(self):
        if self.copy is not None:
            self.copy.wait()
            self.copy = None
        return self.ref


class Ship:
    def __init__(self, ref, copies):
        self.ref, self.copies, self.started = ref, copies, False

    def go(self):
        for copy in self.copies:
            copy.start()
        self.started = True


class Halves:
    def __init__(self, rows):
        self.shape, self.dtype = (rows, 512), BF


def load(array):
    return ("load", array)


def near(array):
    return ("near", array)


def image(array):
    return ("image", array)


def pick(block, pair):
    return (block, pair)


def smem(array):
    return ("smem", array)


def sds(shape, dtype):
    return jax.ShapeDtypeStruct(shape, dtype)


def vmem(rows, cols, dtype):
    return pltpu.VMEM((rows, cols), dtype)


def room(shapes, most):
    if most:
        return pltpu.CompilerParams(vmem_limit_bytes=MOST_VMEM)
    total = 0
    for shape in shapes:
        if len(getattr(shape, "shape", ())) >= 2 and jnp.issubdtype(shape.dtype, jnp.floating):
            total += math.prod(shape.shape) * jnp.dtype(shape.dtype).itemsize
    return pltpu.CompilerParams(vmem_limit_bytes=total + SPARE_VMEM)


SMEM = pl.BlockSpec(memory_space=pltpu.SMEM)
ANY = pl.BlockSpec(memory_space=pl.ANY)
HBM = pl.BlockSpec(memory_space=pltpu.HBM)


def call(kernel, name, operands, outs, scratch, most=False):
    specs, arrays, buffers = [], [], []
    for kind, value in operands:
        if kind == "smem":
            specs.append(SMEM)
            arrays.append(value)
            continue
        sources = value if isinstance(kind, int) else (value,)
        specs += [ANY if kind == "near" else HBM] * len(sources)
        arrays += list(sources)
        shape = value.shape[1:] if kind == "image" else sources[0].shape
        buffers.append(pltpu.VMEM(shape, sources[0].dtype))
    shapes = []
    for out in outs:
        half = sds((out.shape[0] // 2, out.shape[1]), out.dtype) if isinstance(out, Halves) else None
        shapes += [half, half] if half is not None else [out]
    n_in, n_out, n_load, n_ship = len(arrays), len(shapes), len(buffers), len(outs)
    buffers += [pltpu.VMEM(out.shape, out.dtype) for out in outs]

    def body(*refs):
        ins, results = refs[:n_in], refs[n_in : n_in + n_out]
        bufs = refs[n_in + n_out : n_in + n_out + n_load + n_ship]
        rest, sems = refs[n_in + n_out + n_load + n_ship : -1], refs[-1]
        section = lax.axis_index("section")
        slots, at, nth = [], 0, 0
        for kind, value in operands:
            if kind == "smem":
                slots.append(ins[at])
                at += 1
                continue
            dst, sem = bufs[nth], sems.at[nth]
            nth += 1
            if isinstance(kind, int):
                own, other = ins[at], ins[at + 1]
                at += 2

                @pl.when(section == kind)
                def _():
                    pltpu.make_async_copy(own, dst, sem).start()

                @pl.when(section != kind)
                def _():
                    pltpu.make_async_copy(other, dst, sem).start()

                copy = pltpu.make_async_copy(own, dst, sem)
            else:
                src = ins[at]
                at += 1
                if kind == "image":
                    src = src.at[section]
                copy = pltpu.make_async_copy(src, dst, sem)
                copy.start()
            slots.append(Slot(dst, copy))
        ships, at = [], 0
        for i, out in enumerate(outs):
            buf, copies = bufs[n_load + i], []
            if isinstance(out, Halves):
                rows = out.shape[0] // 2
                for half in (1, 0):
                    src = buf.at[half * rows : (half + 1) * rows]
                    copies.append(pltpu.make_async_copy(src, results[at + half], sems.at[n_load + at + half]))
            else:
                copies.append(pltpu.make_async_copy(buf, results[at], sems.at[n_load + at]))
            at += len(copies)
            ships.append(Ship(buf, copies))
        kernel(*slots, *ships, *rest)
        for slot in slots:
            if isinstance(slot, Slot):
                slot.get()
        for ship in ships:
            if not ship.started:
                ship.go()
        for ship in ships:
            for copy in ship.copies:
                copy.wait()

    return pl.pallas_call(
        body,
        name=name,
        out_shape=shapes,
        in_specs=specs,
        out_specs=[ANY] * n_out,
        scratch_shapes=buffers + list(scratch) + [pltpu.SemaphoreType.DMA((n_load + n_out,))],
        compiler_params=room(buffers + list(scratch), most),
        cost_estimate=pl.CostEstimate(flops=0, bytes_accessed=0, transcendentals=0),
    )(*arrays)


def nn(a, b):
    return jnp.dot(a, b, preferred_element_type=F32)


def nt(a, b):
    return lax.dot_general(a, b, (((1,), (1,)), ((), ())), preferred_element_type=F32)


def tn(a, b):
    return lax.dot_general(a, b, (((0,), (0,)), ((), ())), preferred_element_type=F32)


def colsum(v):
    return jnp.sum(v, axis=0, keepdims=True)


def wide(m, n):
    return jnp.concatenate([m] * n, axis=1)


def reader(vec_ref):
    return lambda row, lo, n: vec_ref[row : row + 1, lo : lo + n]


def piece_masks(section):
    place = lax.axis_index("dp") % 16
    x_bit, y_bit, z_at = place & 1, (place >> 1) & 1, place >> 2
    return section * 16 + x_bit * 8 + y_bit * 4 + z_at, section * 16 + y_bit * 8 + x_bit * 4 + z_at


def piece_rows(masks, p, rows):
    return pl.multiple_of((p ^ masks[p >> 4]) * rows, 64)


def fill_mask(mask_ref, crop_ref, section):
    kind = crop_ref[section, 0]
    side = jnp.where(kind == 0, SIDE_S, jnp.where(kind == 1, SIDE_M, CANVAS))
    r = lax.broadcasted_iota(jnp.int32, (PIX, LANES), 0)
    inside = ((r // CANVAS) < side) & ((r % CANVAS) < side)
    mask_ref[...] = inside.astype(F32)


def row_chunks(body, start):
    return lax.fori_loop(0, PIX // 32, lambda i, carry: body(pl.ds(pl.multiple_of(i * 32, 32), 32), carry), start,
                         unroll=True)


def normalized(v):
    cen = v - jnp.mean(v, axis=-1, keepdims=True)
    inv = lax.rsqrt(jnp.mean(cen * cen, axis=-1, keepdims=True) + EPS)
    return cen * inv, inv


def norm_gradient(up, xhat, inv, gain):
    g = up * gain
    return inv * (g - jnp.mean(g, axis=-1, keepdims=True) - xhat * jnp.mean(g * xhat, axis=-1, keepdims=True))


def conv_rows(src_ref, taps_ref, flip, bias, store):
    def row(h, carry):
        accs = [bias] * CANVAS if bias is not None else [None] * CANVAS
        for a in range(KS):
            ks = []
            for e in range(KS):
                t = (KS - 1 - a) * KS + (KS - 1 - e) if flip else a * KS + e
                ks.append(taps_ref[t * GROUPS : (t + 1) * GROUPS, :])
            for w2 in range(CANVAS):
                x = vreg(src_ref, (h + a) * CANVAS + w2)
                for e in range(KS):
                    w = w2 + 3 - e
                    if 0 <= w < CANVAS:
                        term = x * ks[e]
                        accs[w] = term if accs[w] is None else accs[w] + term
        for w in range(CANVAS):
            store(h * CANVAS + w, accs[w])
        return carry

    lax.fori_loop(0, CANVAS, row, 0)


def vreg(ref, index):
    return ref[pl.ds(pl.multiple_of(index * GROUPS, GROUPS), GROUPS), :]


def zero_border(ref):
    zeros = jnp.zeros((3 * CANVAS * GROUPS, LANES), F32)
    ref[0 : 3 * CANVAS * GROUPS, :] = zeros
    ref[(PAD_ROWS - 3 * CANVAS) * GROUPS :, :] = zeros


def lane_group(ref, g, rows=PIX, base=0):
    return ref[pl.ds(base + g, rows, stride=GROUPS), :]


def gn_forward_part(mask, x_ref, vec, taps, gates, win, wo, n1, cin, mix, p, gl, mid, br, mx_ref):
    zero_border(cin.ref)

    def norm_in(r, carry):
        xhat, _ = normalized(x_ref[r, :].astype(F32) * wide(mask[r, :], 4))
        n1.ref[r, :] = (xhat * vec(V_N1G, 0, C) + vec(V_N1S, 0, C)).astype(BF)
        return carry

    row_chunks(norm_in, 0)
    n1.go()
    win_ref = win.get()
    for n in range(4):
        m = nn(n1.ref[...], win_ref[:, n * 256 : (n + 1) * 256]) + vec(V_BIN, n * 256, 256)
        for half in range(2):
            g = 2 * n + half
            v = m[:, half * LANES : (half + 1) * LANES] * mask[...]
            cin.ref[pl.ds(3 * CANVAS * GROUPS + g, PIX, stride=GROUPS), :] = v
            if g == 0:
                p.ref[:, 0:LANES] = v
    cin.go()
    taps_ref = taps.get()
    bias = taps_ref[49 * GROUPS : 50 * GROUPS, :]

    def keep(pixel, acc):
        mx_ref[pl.ds(pl.multiple_of(pixel * GROUPS, GROUPS), GROUPS), :] = acc * (1.0 / 3.0)

    conv_rows(cin.ref, taps_ref, False, bias, keep)
    for g in range(GROUPS):
        mix.ref[:, g * LANES : (g + 1) * LANES] = lane_group(mx_ref, g)
    mix.go()
    gates_ref, wo_ref = gates.get(), wo.get()
    gl.ref[:, 0:128] = (p.ref[:, 0:128] * pltpu.roll(mix.ref[:, 0:128], 64, 1)).astype(BF)
    p1 = nn(gl.ref[:, 0:128], gates_ref[256:384, 256:384]) + vec(V_B1, 0, 128)
    p.ref[:, 128:256] = p1
    gl.ref[:, 128:256] = (p1 * mix.ref[:, 128:256]).astype(BF)
    p2 = nn(gl.ref[:, 128:256], gates_ref[256:384, 0:256]) + vec(V_B2, 0, 256)
    p.ref[:, 256:512] = p2
    gl.ref[:, 256:512] = (p2 * mix.ref[:, 256:512]).astype(BF)
    for n in range(2):
        c = 256 * n
        p3 = nn(gl.ref[:, 256:512], gates_ref[0:256, c : c + 256]) + vec(V_B3, c, 256)
        p.ref[:, 512 + c : 768 + c] = p3
        gl.ref[:, 512 + c : 768 + c] = (p3 * mix.ref[:, 512 + c : 768 + c]).astype(BF)
    p.go()
    gl.go()
    for n in range(2):
        c = 256 * n
        b = nn(gl.ref[:, 512:1024], wo_ref[:, c : c + 256]) + vec(V_BO, c, 256)
        br.ref[:, c : c + 256] = b.astype(BF)
        start = x_ref[:, c : c + 256].astype(F32) * wide(mask[...], 2)
        mid.ref[:, c : c + 256] = start + vec(V_BS, c, 256) * b
    br.go()
    if isinstance(mid, Ship):
        mid.go()


def mlp_forward_part(mask, mid_ref, vec, we, wr, n2_ref, act_ref, slope_ref, out_ref, res_ref):
    def norm_mid(r, carry):
        xhat, _ = normalized(mid_ref[r, :])
        n2_ref[r, :] = (xhat * vec(V_N2G, 0, C) + vec(V_N2S, 0, C)).astype(BF)
        return carry

    row_chunks(norm_mid, 0)
    we_ref = we.get()
    for j in range(8):
        c = 256 * j
        pre = nn(n2_ref[...], we_ref[:, c : c + 256]) + vec(V_BE, c, 256)
        cum = 0.5 * (1.0 + lax.erf(pre * 0.7071067811865476))
        act_ref[:, c : c + 256] = (pre * cum).astype(BF)
        slope = cum + pre * jnp.exp(-0.5 * pre * pre) * 0.3989422804014327
        slope_ref[:, c : c + 256] = slope.astype(BF)
    wr_ref = wr.get()
    for n in range(2):
        c = 256 * n
        out = nn(act_ref[...], wr_ref[:, c : c + 256]) + vec(V_BR, c, 256)
        out_ref[:, c : c + 256] = out.astype(BF)
        res = wide(mask[...], 2) * (mid_ref[:, c : c + 256] + vec(V_MS, c, 256) * out)
        res_ref[:, c : c + 256] = res.astype(BF)


def mlp_back_part(mask, masks, dy_ref, vec, n2_ref, act_ref, slope_ref, out_ref, mid_ref, we, wr,
                  dmid, mvec, bucket, dout_ref, dpre_ref, dn2_ref):
    mvec.ref[...] = jnp.zeros_like(mvec.ref)
    for n in range(2):
        c = 256 * n
        dyr = dy_ref[:, c : c + 256].astype(F32) * wide(mask[...], 2)
        dmid.ref[:, c : c + 256] = dyr
        dout = (vec(V_MS, c, 256) * dyr).astype(BF)
        dout_ref[:, c : c + 256] = dout
        mvec.ref[3:4, c : c + 256] = colsum(dout.astype(F32))
        mvec.ref[4:5, c : c + 256] = colsum(dyr * out_ref[:, c : c + 256].astype(F32))
    wr_ref = wr.get()
    for j in range(8):
        c = 256 * j
        dw = tn(act_ref[:, c : c + 256], dout_ref[...]).astype(BF)
        for q in range(4):
            bucket.ref[pl.ds(piece_rows(masks, 4 * j + q, 128), 64), :] = dw[64 * q : 64 * q + 64, :]
        dact = nt(dout_ref[...], wr_ref[c : c + 256, :])
        dpre = (dact * slope_ref[:, c : c + 256].astype(F32)).astype(BF)
        dpre_ref[:, c : c + 256] = dpre
        mvec.ref[2:3, c : c + 256] = colsum(dpre.astype(F32))
    we_ref = we.get()
    for cb in range(4):
        dw = tn(n2_ref[...], dpre_ref[:, 512 * cb : 512 * cb + 512]).astype(BF)
        for q in range(8):
            rows = pl.multiple_of(piece_rows(masks, 8 * cb + q, 128) + 64, 64)
            bucket.ref[pl.ds(rows, 64), :] = dw[64 * q : 64 * q + 64, :]
    bucket.go()
    for n in range(2):
        c = 256 * n
        dn2_ref[:, c : c + 256] = nt(dpre_ref[...], we_ref[c : c + 256, :])

    def norm_back(r, carry):
        dgain, dshift = carry
        xhat, inv = normalized(mid_ref[r, :])
        up = dn2_ref[r, :]
        dmid.ref[r, :] = dmid.ref[r, :] + norm_gradient(up, xhat, inv, vec(V_N2G, 0, C))
        return dgain + colsum(up * xhat), dshift + colsum(up)

    zero = jnp.zeros((1, C), F32)
    dgain, dshift = row_chunks(norm_back, (zero, zero))
    mvec.ref[0:1, 0:C] = dgain
    mvec.ref[1:2, 0:C] = dshift


def pack_kernel(*refs):
    vectors, taps_in, w1, w2, w3 = refs[:14], refs[14], refs[15], refs[16], refs[17]
    vec_ref, taps_ref, gates_ref = refs[18:]
    gates_ref[0:256, :] = w3[...]
    gates_ref[256:384, 0:256] = w2[...]
    gates_ref[256:384, 256:384] = jnp.concatenate([w1[...], jnp.zeros((64, 128), BF)], axis=0)
    gates_ref[256:384, 384:512] = jnp.zeros((128, 128), BF)
    vec_ref[...] = jnp.zeros_like(vec_ref)
    for row, ref in enumerate(vectors):
        n = ref.shape[1]
        vec_ref[row : row + 1, 0:n] = ref[...].astype(F32)
    taps = taps_in[...].astype(F32)
    bias = vectors[V_CB][...].astype(F32)
    for g in range(GROUPS):
        if g == 0:
            t = jnp.concatenate([jnp.zeros((49, 64), F32), taps[:, 0:64]], axis=1)
            b = jnp.concatenate([jnp.zeros((1, 64), F32), bias[:, 0:64]], axis=1)
        else:
            t = taps[:, g * LANES - 64 : g * LANES + 64]
            b = bias[:, g * LANES - 64 : g * LANES + 64]
        taps_ref[pl.ds(g, 49, stride=GROUPS), :] = t
        taps_ref[49 * GROUPS + g : 49 * GROUPS + g + 1, :] = b


def gn_forward_kernel(crop, x, vec, win, taps, gates, wo, n1, cin, mix, p, gl, mid, br, mask, mx_ref):
    fill_mask(mask, crop, lax.axis_index("section"))
    x_ref = x.get()
    gn_forward_part(mask, x_ref, reader(vec.get()), taps, gates, win, wo, n1, cin, mix, p, gl, mid, br, mx_ref)


def middle_kernel(crop, mid0, vec0, we0, wr0, vec1, win, taps, gates, wo, we1, wr1, dy,
                  hidden, n2, act, slope, out, n1, cin, mix, p, gl, br, final, swap, dmid, mvec, bucket,
                  mask, mx_ref, mid1, n2_1, act1, slope1, out1, dout_ref, dpre_ref, dn2_ref):
    section = lax.axis_index("section")
    masks = piece_masks(section)
    fill_mask(mask, crop, section)
    mid0_ref = mid0.get()
    mlp_forward_part(mask, mid0_ref, reader(vec0.get()), we0, wr0, n2.ref, act.ref, slope.ref, out.ref, hidden.ref)
    for ship in (hidden, n2, act, slope, out):
        ship.go()
    vec = reader(vec1.get())
    gn_forward_part(mask, hidden.ref, vec, taps, gates, win, wo, n1, cin, mix, p, gl, Slot(mid1, None), br, mx_ref)
    mlp_forward_part(mask, mid1, vec, we1, wr1, n2_1, act1, slope1, out1, final.ref)
    final.go()
    swap.ref[...] = jnp.where(section == 0, final.ref[...], hidden.ref[...])
    swap.go()
    mlp_back_part(mask, masks, dy.get(), vec, n2_1, act1, slope1, out1, mid1, we1, wr1,
                  dmid, mvec, bucket, dout_ref, dpre_ref, dn2_ref)


def mlp_back_kernel(crop, dy, vec, n2, act, slope, out, mid, wr, we, dmid, mvec, bucket,
                    mask, dout_ref, dpre_ref, dn2_ref):
    section = lax.axis_index("section")
    fill_mask(mask, crop, section)
    mlp_back_part(mask, piece_masks(section), dy.get(), reader(vec.get()), n2.get(), act.get(), slope.get(), out.get(),
                  mid.get(), we, wr, dmid, mvec, bucket, dout_ref, dpre_ref, dn2_ref)


def gn_back_kernel(block, crop, dmid, br, vec, wo, mix, p, gates, mvec, taps, win, x, *rest):
    if block == 0:
        following, dv, swap, dbr, dp, dmg, dcp, gvec = rest[:8]
    else:
        dv, dvb, dbr, dp, dmg, dcp, gvec = rest[:7]
    mask, dg_ref, dmix_ref, ds_ref, dn1_ref = rest[-5:]
    section = lax.axis_index("section")
    fill_mask(mask, crop, section)
    zero_border(dcp.ref)
    dmid_ref, br_ref = dmid.get(), br.get()
    vec = reader(vec.get())
    dbs, dbo = [], []
    for n in range(2):
        c = 256 * n
        dm = dmid_ref[:, c : c + 256]
        dbs.append(colsum(dm * br_ref[:, c : c + 256].astype(F32)))
        d = (vec(V_BS, c, 256) * dm).astype(BF)
        dbr.ref[:, c : c + 256] = d
        dbo.append(colsum(d.astype(F32)))
    dbr.go()
    wo_ref, mix_ref, p_ref = wo.get(), mix.get(), p.get()
    db3 = []
    for n in range(2):
        c = 256 * n
        dg = nt(dbr.ref[...], wo_ref[c : c + 256, :])
        d = (dg * mix_ref[:, 512 + c : 768 + c]).astype(BF)
        dmix_ref[:, 512 + c : 768 + c] = dg * p_ref[:, 512 + c : 768 + c] * (1.0 / 3.0)
        dp.ref[:, 512 + c : 768 + c] = d
        db3.append(colsum(d.astype(F32)))
    gates_ref = gates.get()
    dg = nt(dp.ref[:, 512:1024], gates_ref[0:256, :])
    d = (dg * mix_ref[:, 256:512]).astype(BF)
    dmix_ref[:, 256:512] = dg * p_ref[:, 256:512] * (1.0 / 3.0)
    dp.ref[:, 256:512] = d
    db2 = colsum(d.astype(F32))
    dg = nt(dp.ref[:, 256:512], gates_ref[256:384, 0:256])
    d = (dg * mix_ref[:, 128:256]).astype(BF)
    dmix_ref[:, 128:256] = dg * p_ref[:, 128:256] * (1.0 / 3.0)
    dp.ref[:, 128:256] = d
    db1 = colsum(d.astype(F32))
    dg = nt(dp.ref[:, 128:256], gates_ref[256:384, 256:384])
    dmix_ref[:, 0:128] = pltpu.roll(dg * p_ref[:, 0:128], 64, 1) * (1.0 / 3.0)
    dg_ref[...] = dg * pltpu.roll(mix_ref[:, 0:128], 64, 1)
    dp.ref[:, 0:128] = jnp.zeros((PIX, LANES), BF)
    dp.go()
    for g in range(GROUPS):
        dcp.ref[pl.ds(3 * CANVAS * GROUPS + g, PIX, stride=GROUPS), :] = dmix_ref[:, g * LANES : (g + 1) * LANES]
    dcp.go()

    def keep(pixel, acc):
        ds_ref[pl.ds(pl.multiple_of(pixel * GROUPS, GROUPS), GROUPS), :] = acc

    conv_rows(dcp.ref, taps.get(), True, None, keep)
    dbin = []
    for g in range(GROUPS):
        d = lane_group(ds_ref, g) * mask[...]
        if g == 0:
            d = d + dg_ref[...]
        d = d.astype(BF)
        dmg.ref[:, g * LANES : (g + 1) * LANES] = d
        dbin.append(colsum(d.astype(F32)))
    dmg.go()
    win_ref, x_ref = win.get(), x.get()
    next_ref = following.get() if block == 0 else None
    for n in range(2):
        c = 256 * n
        dn1_ref[:, c : c + 256] = nt(dmg.ref[...], win_ref[c : c + 256, :])

    def norm_back(r, carry):
        dgain, dshift = carry
        m = wide(mask[r, :], 4)
        xhat, inv = normalized(x_ref[r, :].astype(F32) * m)
        up = dn1_ref[r, :]
        d = m * (dmid_ref[r, :] + norm_gradient(up, xhat, inv, vec(V_N1G, 0, C)))
        dv.ref[r, :] = d
        if block == 0:
            swap.ref[r, :] = jnp.where(section == 0, next_ref[r, :], d)
        else:
            dvb.ref[r, :] = d.astype(BF)
        return dgain + colsum(up * xhat), dshift + colsum(up)

    zero = jnp.zeros((1, C), F32)
    dgain, dshift = row_chunks(norm_back, (zero, zero))
    z = jnp.zeros((1, LANES), F32)
    mvec_ref = mvec.get()
    rows = [
        dgain,
        dshift,
        jnp.concatenate(dbin[0:4], axis=1),
        jnp.concatenate(dbin[4:8], axis=1),
        jnp.concatenate([db1, z, z, z], axis=1),
        jnp.concatenate([db2, z, z], axis=1),
        jnp.concatenate(db3, axis=1),
        jnp.concatenate(dbo, axis=1),
        jnp.concatenate(dbs, axis=1),
        mvec_ref[0:1, 0:C],
        mvec_ref[1:2, 0:C],
        mvec_ref[2:3, 0:512],
        mvec_ref[2:3, 512:1024],
        mvec_ref[2:3, 1024:1536],
        mvec_ref[2:3, 1536:2048],
        mvec_ref[3:4, 0:C],
        mvec_ref[4:5, 0:C],
    ]
    rows.append(jnp.zeros((32 - len(rows), C), F32))
    gvec.ref[...] = jnp.concatenate(rows, axis=0).astype(BF)


def gn_weights_kernel(n1, dmg, gl, dbr, dp, gvec, cin, dcp, bucket, dk_ref):
    masks = piece_masks(lax.axis_index("section"))

    def put(p, val, sub=0):
        n = val.shape[0]
        bucket.ref[pl.ds(pl.multiple_of(piece_rows(masks, p, 64) + sub, 16), n), :] = val

    n1_ref, dmg_ref = n1.get(), dmg.get()
    for cb in range(2):
        dw = tn(n1_ref[...], dmg_ref[:, 512 * cb : 512 * cb + 512]).astype(BF)
        for q in range(8):
            put(8 * cb + q, dw[64 * q : 64 * q + 64, :])
    gl_ref, dbr_ref, dp_ref = gl.get(), dbr.get(), dp.get()
    dw = tn(gl_ref[:, 512:1024], dbr_ref[...]).astype(BF)
    for q in range(8):
        put(16 + q, dw[64 * q : 64 * q + 64, :])
    dw = tn(gl_ref[:, 256:512], dp_ref[:, 512:1024]).astype(BF)
    for q in range(4):
        put(24 + q, dw[64 * q : 64 * q + 64, :])
    dw = tn(gl_ref[:, 128:256], dp_ref[:, 256:512]).astype(BF)
    put(28, jnp.concatenate([dw[0:64, :], dw[64:128, :]], axis=1))
    dw1 = tn(gl_ref[:, 0:128], dp_ref[:, 128:256]).astype(BF)
    put(31, jnp.concatenate([dw1[16 * i : 16 * i + 16, :] for i in range(4)], axis=1))
    put(31, jnp.zeros((16, 512), BF), 16)
    put(31, gvec.get()[...], 32)
    cin_ref, dcp_ref = cin.get(), dcp.get()
    dk_ref[...] = jnp.zeros_like(dk_ref)
    for taps in ((0, 1), (2, 3), (4, 5), (6,)):

        def row(h, accs):
            accs = list(accs)
            ds = [vreg(dcp_ref, (h + 3) * CANVAS + w) for w in range(CANVAS)]
            for i, a in enumerate(taps):
                for w2 in range(CANVAS):
                    x = vreg(cin_ref, (h + a) * CANVAS + w2)
                    for e in range(KS):
                        w = w2 + 3 - e
                        if 0 <= w < CANVAS:
                            accs[i * KS + e] = accs[i * KS + e] + x * ds[w]
            if len(taps) == 1:
                for w in range(CANVAS):
                    accs[KS] = accs[KS] + ds[w]
            return tuple(accs)

        count = len(taps) * KS + (1 if len(taps) == 1 else 0)
        accs = lax.fori_loop(0, CANVAS, row, tuple(jnp.zeros((GROUPS, LANES), F32) for _ in range(count)))
        for i in range(count):
            t = taps[0] * KS + i
            dk_ref[t * GROUPS : (t + 1) * GROUPS, :] = accs[i]
    for half in range(2):
        put(29 + half, jnp.concatenate([lane_group(dk_ref, 4 * half + i, 64) for i in range(4)], axis=1).astype(BF))


def start_pieces(layout, rows, halves, buf, sems):
    section = lax.axis_index("section")
    masks = piece_masks(section)
    for p in range(32):
        rel = p ^ masks[p >> 4]
        far = rel >> 4
        dst = buf.at[p * rows : (p + 1) * rows]
        sem = sems.at[p // 4]
        for sec in range(2):
            stride, first = layout[sec]
            off = pl.multiple_of((rel & 15) * stride + first, 64)
            for side in range(2):

                @pl.when((section == sec) & (far == side))
                def _():
                    pltpu.make_async_copy(halves[2 * sec + side].at[pl.ds(off, rows)], dst, sem).start()


def wait_pieces(i, rows, halves, buf, sems):
    part = buf.at[pl.ds(i * 4 * rows, 4 * rows)]
    pltpu.make_async_copy(halves[0].at[pl.ds(0, 4 * rows)], part, sems.at[i]).wait()


def mlp_finish_kernel(layout, *refs):
    halves = refs[:4]
    wr_any, we_any, buf, wr_ref, we_ref, sems, out_sems = refs[-7:]
    start_pieces(layout, 128, halves, buf, sems)
    copies = []
    for i in range(8):
        wait_pieces(i, 128, halves, buf, sems)
        cb = i // 2
        for q in range(4):
            p = 4 * i + q
            r = p % 8
            wr_ref[64 * p : 64 * p + 64, :] = buf[128 * p : 128 * p + 64, :].astype(F32)
            we_ref[64 * r : 64 * r + 64, 512 * cb : 512 * cb + 512] = buf[128 * p + 64 : 128 * p + 128, :].astype(F32)
        rows = slice(256 * i, 256 * i + 256)
        copies.append(pltpu.make_async_copy(wr_ref.at[rows], wr_any.at[rows], out_sems.at[i]))
        half = slice(256 * (i % 2), 256 * (i % 2) + 256)
        cols = slice(512 * cb, 512 * cb + 512)
        copies.append(pltpu.make_async_copy(we_ref.at[half, cols], we_any.at[half, cols], out_sems.at[8 + i]))
        copies[-2].start()
        copies[-1].start()
    for copy in copies:
        copy.wait()


def gn_finish_kernel(layout, *refs):
    halves = refs[:4]
    (n1g, n1s, win_any, bin_, conv, cbias, w1, b1, w2, b2, w3, b3, wo_any, bo, bs, n2g, n2s, be, br, ms,
     buf, win, wo, sems, out_sems) = refs[-25:]
    start_pieces(layout, 64, halves, buf, sems)
    copies = []
    for cb in range(2):
        cols = slice(512 * cb, 512 * cb + 512)
        for i in range(2):
            wait_pieces(2 * cb + i, 64, halves, buf, sems)
        win[:, cols] = buf[cols, :].astype(F32)
        copies.append(pltpu.make_async_copy(win.at[:, cols], win_any.at[:, cols], out_sems.at[cb]))
        copies[-1].start()
    for i in (4, 5):
        wait_pieces(i, 64, halves, buf, sems)
    wo[...] = buf[1024:1536, :].astype(F32)
    copies.append(pltpu.make_async_copy(wo, wo_any, out_sems.at[2]))
    copies[-1].start()
    for i in (6, 7):
        wait_pieces(i, 64, halves, buf, sems)
    w3[...] = buf[1536:1792, :].astype(F32)
    for i in range(2):
        w2[64 * i : 64 * i + 64, :] = buf[1792:1856, 256 * i : 256 * i + 256].astype(F32)
    for i in range(4):
        w1[16 * i : 16 * i + 16, :] = buf[1984:2000, 128 * i : 128 * i + 128].astype(F32)
    taps = jnp.concatenate([buf[1856:1920, :], buf[1920:1984, :]], axis=1).astype(F32)
    for i in range(49):
        conv[i] = taps[i : i + 1, 64:1024]
    cbias[...] = taps[49:50, 64:1024]
    v = buf[2016:2048, :].astype(F32)
    n1g[...] = v[0:1]
    n1s[...] = v[1:2]
    bin_[:, 0:512] = v[2:3]
    bin_[:, 512:1024] = v[3:4]
    b1[...] = v[4:5, 0:128]
    b2[...] = v[5:6, 0:256]
    b3[...] = v[6:7]
    bo[...] = v[7:8]
    bs[...] = v[8:9]
    n2g[...] = v[9:10]
    n2s[...] = v[10:11]
    for i in range(4):
        be[:, 512 * i : 512 * i + 512] = v[11 + i : 12 + i]
    br[...] = v[15:16]
    ms[...] = v[16:17]
    for copy in copies:
        copy.wait()


def place_kernel(first, second, got, out):
    section = lax.axis_index("section")

    @pl.when(section == 0)
    def _():
        out[0] = first[...]
        out[1] = got[...]

    @pl.when(section != 0)
    def _():
        out[0] = got[...]
        out[1] = second[...]


VM = pl.BlockSpec(memory_space=pltpu.VMEM)


def plain_call(kernel, name, operands, outs, scratch, most=False):
    return pl.pallas_call(
        kernel,
        name=name,
        out_shape=[shape for _, shape in outs],
        in_specs=[spec for spec, _ in operands],
        out_specs=[spec for spec, _ in outs],
        scratch_shapes=scratch,
        compiler_params=room([a for spec, a in operands + outs if spec is VM] + scratch, most),
        cost_estimate=pl.CostEstimate(flops=0, bytes_accessed=0, transcendentals=0),
    )(*[array for _, array in operands])


def on(spec, *arrays):
    return [(spec, a) for a in arrays]


MASK = vmem(PIX, LANES, F32)
PIXEL_CHANNELS = vmem(PIX * GROUPS, LANES, F32)
FIELD_F32, FIELD_BF = sds((PIX, C), F32), sds((PIX, C), BF)
CONV_F32 = sds((PAD_ROWS * GROUPS, LANES), F32)
WIDE_F32, WIDE_BF = sds((PIX, 1024), F32), sds((PIX, 1024), BF)
HIDE_BF = sds((PIX, FF), BF)
GN_SAVED = [FIELD_BF, CONV_F32, WIDE_F32, WIDE_F32, WIDE_BF]


def run_pack(vectors, taps, gates):
    outs = on(VM, sds((VEC_ROWS, FF), F32), sds((50 * GROUPS, LANES), F32), sds((384, 512), BF))
    return plain_call(pack_kernel, "pack", on(VM, *vectors, taps, *gates), outs, [], True)


def run_gn_forward(crop, images, w):
    operands = [smem(crop), image(images)] + [pick(0, w[k]) for k in ("vec", "win", "taps", "gates", "wo")]
    return call(gn_forward_kernel, "gnconv_forward", operands, GN_SAVED + [FIELD_F32, FIELD_BF],
                [MASK, PIXEL_CHANNELS], True)


def run_middle(crop, mid, cotangent, w):
    operands = [smem(crop), load(mid)] + [pick(0, w[k]) for k in ("vec", "we", "wr")]
    operands += [pick(1, w[k]) for k in ("vec", "win", "taps", "gates", "wo", "we", "wr")] + [image(cotangent)]
    outs = [FIELD_BF, FIELD_BF, HIDE_BF, HIDE_BF, FIELD_BF] + GN_SAVED + [FIELD_BF, FIELD_BF, FIELD_BF, FIELD_F32]
    outs += [sds((8, FF), F32), Halves(4096)]
    scratch = [MASK, PIXEL_CHANNELS, vmem(PIX, C, F32), vmem(PIX, C, BF), vmem(PIX, FF, BF), vmem(PIX, FF, BF),
               vmem(PIX, C, BF), vmem(PIX, C, BF), vmem(PIX, FF, BF), vmem(PIX, C, F32)]
    return call(middle_kernel, "middle", operands, outs, scratch, True)


def run_mlp_back(crop, dy, n2, act, slope, out, mid, w):
    operands = [smem(crop), near(dy), pick(0, w["vec"]), load(n2), load(act), load(slope), load(out), load(mid),
                pick(0, w["wr"]), pick(0, w["we"])]
    outs = [FIELD_F32, sds((8, FF), F32), Halves(4096)]
    scratch = [MASK, vmem(PIX, C, BF), vmem(PIX, FF, BF), vmem(PIX, C, F32)]
    return call(mlp_back_kernel, "mlp_backward", operands, outs, scratch, True)


def run_gn_back(block, crop, x, following, dmid, mvec, mix, p, br, w):
    far = load if block == 1 else near
    operands = [smem(crop), far(dmid), load(br), pick(block, w["vec"]), pick(block, w["wo"]), load(mix), load(p),
                pick(block, w["gates"]), far(mvec), pick(block, w["taps"]), pick(block, w["win"])]
    operands += [image(x), near(following)] if block == 0 else [load(x)]
    outs = [FIELD_F32, FIELD_F32 if block == 0 else FIELD_BF, FIELD_BF, WIDE_BF, WIDE_BF, CONV_F32, sds((32, 512), BF)]
    scratch = [MASK, vmem(PIX, LANES, F32), vmem(PIX, 1024, F32), PIXEL_CHANNELS, vmem(PIX, C, F32)]
    return call(functools.partial(gn_back_kernel, block), "gnconv_backward", operands, outs, scratch, block == 1)


def run_gn_weights(block, n1, dmg, gl, dbr, dp, gvec, cin, dcp):
    operands = [load(n1), near(dmg), load(gl), near(dbr), near(dp), near(gvec), load(cin), near(dcp)]
    return call(gn_weights_kernel, "gnconv_weights", operands, [Halves(2048)], [vmem(64 * GROUPS, LANES, F32)],
                block == 1)


def turn_kernel(token, out):
    out[...] = jnp.zeros_like(out)


def run_turn(token):
    return plain_call(turn_kernel, "turn", on(ANY, token), on(VM, sds((8, LANES), F32)), [])[0]


def run_mlp_finish(layout, halves):
    outs = on(ANY, sds((FF, C), F32), sds((C, FF), F32))
    scratch = [vmem(4096, 512, BF), vmem(FF, C, F32), vmem(C, FF, F32), pltpu.SemaphoreType.DMA((8,)),
               pltpu.SemaphoreType.DMA((16,))]
    return plain_call(functools.partial(mlp_finish_kernel, layout), "mlp_finish", on(ANY, *halves), outs, scratch, True)


def run_gn_finish(layout, halves):
    widths = [512, 512, (512, 1024), 1024, (49, 1, 960), 960, (64, 128), 128, (128, 256), 256, (256, 512), 512,
              (512, 512), 512, 512, 512, 512, 2048, 512, 512]
    large = ((512, 1024), (512, 512))
    outs = [(ANY if w in large else VM, sds((1, w) if isinstance(w, int) else w, F32)) for w in widths]
    scratch = [vmem(2048, 512, BF), vmem(512, 1024, F32), vmem(512, 512, F32), pltpu.SemaphoreType.DMA((8,)),
               pltpu.SemaphoreType.DMA((3,))]
    return plain_call(functools.partial(gn_finish_kernel, layout), "gn_finish", on(ANY, *halves), outs, scratch, True)


def run_place(first, second, got):
    outs = on(VM, sds((2, PIX, C), first.dtype))
    return plain_call(place_kernel, "place", on(VM, first, second, got), outs, [])[0]


AXES = ("section", "dp")
X_BIT, Y_BIT, Z_LOW, Z_HIGH = 1, 2, 4, 8

FIRST, SECOND, LOW, HIGH = (X_BIT, Y_BIT), (Y_BIT, X_BIT), (Z_LOW, Z_LOW), (Z_HIGH, Z_HIGH)

ORDER = (
    "+m1.core", "K1", "-m1.core", "+m1.x1", "K2", "+g1.core", "K3", "-g1.core", "+g1.x1", "-m1.x1", "+m1.x2",
    "+m0.core", "K4", "-g1.x1", "+g1.x2", "-m1.x2", "+m1.zl", "-m0.core", "+m0.x1", "-g1.x2", "+g1.zl", "-m1.zl",
    "+m1.zh", "-g1.zl", "+g1.zh", "K5", "-m0.x1", "+m0.x2", "-m1.zh", "-g1.zh", "+b1.ZH", "+g0.core", "-m0.x2",
    "+m0.zl", "-g0.core", "+g0.x1", "-b1.ZH", "+b1.ZL", "-m0.zl", "+m0.zh", "-g0.x1", "+g0.x2", "-b1.ZL", "+b1.X2",
    "+go", "-go", "-g0.x2", "+g0.zl", "-m0.zh", "+m0.ZH", "-b1.X2", "+b1.X1", "-g0.zl", "+g0.zh", "-m0.ZH", "+m0.ZL",
    "P2", "-g0.zh", "+g0.ZH", "-m0.ZL", "+m0.X2", "-g0.ZH", "+g0.ZL", "-g0.ZL", "+g0.X2", "-m0.X2", "+m0.X1",
    "-b1.X1", "+fo", "-fo", "P1", "-g0.X2", "+g0.X1", "+b1.Core", "-b1.Core", "-m0.X1", "+m0.Core", "-m0.Core",
    "-g0.X1", "+g0.Core", "MF", "-g0.Core", "GF",
)


def after(x, *others):
    return lax.optimization_barrier((x,) + others)[0]


class Flow:
    def __init__(self, count):
        self.count = count
        self.token = None
        self.flying = {}

    def exchange(self, x, flips=None, only=None):
        n = self.count
        other, bits = (1, (0, 0)) if flips is None else (0, flips)
        pairs = [
            (s * n + d, (s ^ other) * n + (d ^ bits[s])) for s in range(2) for d in range(n) if only is None or s == only
        ]
        return lax.ppermute(x, AXES, pairs)

    def start(self, name, x, flips=None, only=None):
        self.flying[name] = self.exchange(after(x, self.token), flips, only)

    def end(self, name):
        got, token = lax.optimization_barrier((self.flying.pop(name), self.token))
        self.token = run_turn(token)
        return got

    def tie(self, x):
        return after(x, self.token)


VECTORS = (0, 1, 3, 5, 7, 9, 11, 13, 14, 15, 16, 18, 20, 21)


def on_device(flow, images, cotangent, crop, *stacked):
    images = images.reshape(2, PIX, C)
    cotangent = cotangent.reshape(2, PIX, C)
    win, wo, we, wr = [stacked[i][0] for i in (2, 12, 17, 19)]
    vec, taps, gates = run_pack([stacked[i] for i in VECTORS], stacked[4][0], [stacked[i][0] for i in (6, 8, 10)])
    swap = flow.exchange
    win_other, wo_other = swap(win), swap(wo)
    taps_other, vec_other, gates_other = swap(taps), swap(vec), swap(gates)
    we, wr = after((we, wr), win_other, wo_other, taps_other, vec_other, gates_other)
    we_other, wr_other = swap(we), swap(wr)
    w = {
        "win": (win, win_other), "wo": (wo, wo_other), "we": (we, we_other), "wr": (wr, wr_other),
        "vec": (vec, vec_other), "taps": (taps, taps_other), "gates": (gates, gates_other),
    }

    n1_0, cin_0, mix_0, p_0, gl_0, mid_0, br_0 = run_gn_forward(crop, images, w)
    (hidden, n2_0, act_0, slope_0, out_0, n1_1, cin_1, mix_1, p_1, gl_1, br_1, final, field_swap, dmid_1, mvec_1,
     keep, send) = run_middle(crop, mid_0, cotangent, w)
    flow.token = mvec_1
    value = {"m1.core": (keep, send)}
    chips = flow.count // 16

    def sum_all(total):
        if chips > 1:
            groups = [[g * 16 + r for g in range(chips)] for r in range(16)]
            total = lax.psum(total, "dp", axis_index_groups=groups)
        return total

    def begin(name):
        bucket, step = name.split(".")
        only = {"b1": 0, "m0": 1, "g0": 1}.get(bucket)
        if step == "core":
            flow.start(name, value[name][1])
        elif step == "Core":
            flow.start(name, value[name], None, only)
        elif step in ("x1", "x2", "zh"):
            flow.start(name, value[name][1], {"x1": FIRST, "x2": SECOND, "zh": HIGH}[step])
        elif step == "zl":
            flow.start(name, value[name][:, 1], LOW)
        else:
            flow.start(name, value[name], {"ZH": HIGH, "ZL": LOW, "X2": SECOND, "X1": FIRST}[step])

    def finish(name):
        bucket, step = name.split(".")
        got = flow.end(name)
        mine = value.pop(name)
        if step == "core":
            half = mine[0] + got
            value[bucket + ".x1"] = half.reshape(2, 2, 2, 2, half.shape[0] // 16, 512)
        elif step in ("x1", "x2"):
            value[bucket + (".x2" if step == "x1" else ".zl")] = mine[0] + got
        elif step == "zl":
            value[bucket + ".zh"] = mine[:, 0] + got
        elif step == "zh":
            value[bucket] = sum_all(mine[0] + got)
            if bucket in ("m0", "g0"):
                value[bucket + ".ZH"] = value[bucket]
            elif "m1" in value and "g1" in value:
                value["b1.ZH"] = jnp.concatenate([value["m1"], value["g1"]], axis=0)
        elif step == "ZH":
            value[bucket + ".ZL"] = jnp.stack([mine, got])
        elif step == "ZL":
            value[bucket + ".X2"] = jnp.stack([mine, got], axis=1)
        elif step == "X2":
            value[bucket + ".X1"] = jnp.stack([mine, got])
        elif step == "X1":
            value[bucket + ".Core"] = jnp.stack([mine, got]).reshape(-1, 512)
        else:
            value[bucket] = (mine, got)

    for event in ORDER:
        if event in ("+fo", "+go"):
            flow.start(event[1:], field_swap if event == "+fo" else grad_swap)
        elif event in ("-fo", "-go"):
            value[event[1:]] = flow.end(event[1:])
        elif event[0] == "+":
            begin(event[1:])
        elif event[0] == "-":
            finish(event[1:])
        elif event == "K1":
            back = run_gn_back(1, crop, hidden, None, flow.tie(dmid_1), mvec_1, mix_1, p_1, br_1, w)
            dv_1, dvb, dbr_1, dp_1, dmg_1, dcp_1, gvec_1 = back
            flow.token = gvec_1
        elif event == "K2":
            value["g1.core"] = run_gn_weights(1, n1_1, dmg_1, gl_1, dbr_1, dp_1, flow.tie(gvec_1), cin_1, dcp_1)
            flow.token = value["g1.core"][0]
        elif event == "K3":
            dmid_0, mvec_0, *value["m0.core"] = run_mlp_back(crop, flow.tie(dvb), n2_0, act_0, slope_0, out_0, mid_0, w)
            flow.token = mvec_0
        elif event == "K4":
            back = run_gn_back(0, crop, images, dv_1, flow.tie(dmid_0), mvec_0, mix_0, p_0, br_0, w)
            dv_0, grad_swap, dbr_0, dp_0, dmg_0, dcp_0, gvec_0 = back
            flow.token = gvec_0
        elif event == "K5":
            value["g0.core"] = run_gn_weights(0, n1_0, dmg_0, gl_0, dbr_0, dp_0, flow.tie(gvec_0), cin_0, dcp_0)
            flow.token = value["g0.core"][0]
        elif event == "P1":
            flow.token = block_outputs = run_place(hidden, final, flow.tie(value["fo"]))
        elif event == "P2":
            flow.token = input_grads = run_place(dv_0, dv_1, flow.tie(value["go"]))
        elif event == "MF":
            own, got = value["m0"]
            wr, we = run_mlp_finish(((128, 0), (192, 0)), (flow.tie(own), got) + value["b1"])
            flow.token = wr
        elif event == "GF":
            own, got = value["g0"]
            grads = run_gn_finish(((64, 0), (192, 128)), (flow.tie(own), got) + value["b1"])
    (n1g, n1s, win, bin_, conv, cbias, w1, b1, w2, b2, w3, b3, wo, bo, bs, n2g, n2s, be, br, ms) = grads
    shape = (1, 2, 1, CANVAS, CANVAS, C)
    return (
        block_outputs.reshape(shape), input_grads.reshape(shape), n1g, n1s, win[None], bin_, conv.reshape(1, 49, 960), cbias,
        w1[None], b1, w2[None], b2, w3[None], b3, wo[None], bo, bs, n2g, n2s, we[None], be, wr[None], br, ms,
    )


def solution(mesh):
    count = mesh.shape["dp"]
    image = P(None, "dp", None, None, None)
    one, two = P("section", None), P("section", None, None)
    weights = (one, one, two, one, two, one, two, one, two, one, two, one, two, one, one, one, one, two, one, two,
               one, one)
    field = P("section", None, "dp", None, None, None)
    return jax.shard_map(
        lambda *arrays: on_device(Flow(count), *arrays),
        mesh=mesh,
        in_specs=(image, image, P(None, "dp")) + weights,
        out_specs=(field, field) + weights,
        check_vma=False,
    )
```

```python
import functools
import math

import jax
import jax.numpy as jnp
from jax import lax
from jax.experimental import pallas as pl
from jax.experimental.pallas import tpu as pltpu
from jax.sharding import PartitionSpec as P

SIDE_S = 8
SIDE_M = 12
CANVAS = 16
PIX = CANVAS * CANVAS
C = 512
FF = 2048
LANES = 128
GROUPS = 8
EPS = 1e-06
KS = 7
PAD_ROWS = (CANVAS + 6) * CANVAS
BF = jnp.bfloat16
F32 = jnp.float32
SPARE_VMEM = 8 * 1024 * 1024
MOST_VMEM = 58 * 1024 * 1024

V_N1G, V_N1S, V_BIN, V_CB, V_B1, V_B2, V_B3, V_BO, V_BS, V_N2G, V_N2S, V_BE, V_BR, V_MS = range(14)
VEC_ROWS = 16


class Slot:
    def __init__(self, ref, copy, start=None):
        self.ref, self.copy, self.start = ref, copy, start

    def begin(self):
        if self.start is not None:
            self.start()
            self.start = None

    def get(self):
        self.begin()
        if self.copy is not None:
            self.copy.wait()
            self.copy = None
        return self.ref


class Ship:
    def __init__(self, ref, copies):
        self.ref, self.copies, self.started = ref, copies, False

    def go(self):
        for copy in self.copies:
            copy.start()
        self.started = True


class Halves:
    def __init__(self, rows):
        self.shape, self.dtype = (rows, 512), BF


def load(array):
    return ("load", array)


def near(array):
    return ("near", array)


def image(array):
    return ("image", array)


def pick(block, pair):
    return (block, pair)


def smem(array):
    return ("smem", array)


def sds(shape, dtype):
    return jax.ShapeDtypeStruct(shape, dtype)


def vmem(rows, cols, dtype):
    return pltpu.VMEM((rows, cols), dtype)


def room(shapes, most):
    if most:
        return pltpu.CompilerParams(vmem_limit_bytes=MOST_VMEM)
    total = 0
    for shape in shapes:
        if len(getattr(shape, "shape", ())) >= 2 and jnp.issubdtype(shape.dtype, jnp.floating):
            total += math.prod(shape.shape) * jnp.dtype(shape.dtype).itemsize
    return pltpu.CompilerParams(vmem_limit_bytes=total + SPARE_VMEM)


SMEM = pl.BlockSpec(memory_space=pltpu.SMEM)
ANY = pl.BlockSpec(memory_space=pl.ANY)
HBM = pl.BlockSpec(memory_space=pltpu.HBM)


def start_pick(is_own, own, other, dst, sem):
    @pl.when(is_own)
    def _():
        pltpu.make_async_copy(own, dst, sem).start()

    @pl.when(jnp.logical_not(is_own))
    def _():
        pltpu.make_async_copy(other, dst, sem).start()


def call(kernel, name, operands, outs, scratch, most=False, early=99):
    specs, arrays, buffers = [], [], []
    for kind, value in operands:
        if kind == "smem":
            specs.append(SMEM)
            arrays.append(value)
            continue
        sources = value if isinstance(kind, int) else (value,)
        specs += [ANY if kind == "near" else HBM] * len(sources)
        arrays += list(sources)
        shape = value.shape[1:] if kind == "image" else sources[0].shape
        buffers.append(pltpu.VMEM(shape, sources[0].dtype))
    shapes = []
    for out in outs:
        half = sds((out.shape[0] // 2, out.shape[1]), out.dtype) if isinstance(out, Halves) else None
        shapes += [half, half] if half is not None else [out]
    n_in, n_out, n_load, n_ship = len(arrays), len(shapes), len(buffers), len(outs)
    buffers += [pltpu.VMEM(out.shape, out.dtype) for out in outs]

    def body(*refs):
        ins, results = refs[:n_in], refs[n_in : n_in + n_out]
        bufs = refs[n_in + n_out : n_in + n_out + n_load + n_ship]
        rest, sems = refs[n_in + n_out + n_load + n_ship : -1], refs[-1]
        section = lax.axis_index("section")
        slots, at, nth = [], 0, 0
        for kind, value in operands:
            if kind == "smem":
                slots.append(ins[at])
                at += 1
                continue
            dst, sem = bufs[nth], sems.at[nth]
            nth += 1
            if isinstance(kind, int):
                own, other = ins[at], ins[at + 1]
                at += 2
                copy = pltpu.make_async_copy(own, dst, sem)
                start = functools.partial(start_pick, section == kind, own, other, dst, sem)
            else:
                src = ins[at]
                at += 1
                if kind == "image":
                    src = src.at[section]
                copy = pltpu.make_async_copy(src, dst, sem)
                start = copy.start
            slots.append(Slot(dst, copy, start))
            if len(slots) <= early:
                slots[-1].begin()
        ships, at = [], 0
        for i, out in enumerate(outs):
            buf, copies = bufs[n_load + i], []
            if isinstance(out, Halves):
                rows = out.shape[0] // 2
                for half in (1, 0):
                    src = buf.at[half * rows : (half + 1) * rows]
                    copies.append(pltpu.make_async_copy(src, results[at + half], sems.at[n_load + at + half]))
            else:
                copies.append(pltpu.make_async_copy(buf, results[at], sems.at[n_load + at]))
            at += len(copies)
            ships.append(Ship(buf, copies))
        kernel(*slots, *ships, *rest)
        for slot in slots:
            if isinstance(slot, Slot):
                slot.get()
        for ship in ships:
            if not ship.started:
                ship.go()
        for ship in ships:
            for copy in ship.copies:
                copy.wait()

    return pl.pallas_call(
        body,
        name=name,
        out_shape=shapes,
        in_specs=specs,
        out_specs=[ANY] * n_out,
        scratch_shapes=buffers + list(scratch) + [pltpu.SemaphoreType.DMA((n_load + n_out,))],
        compiler_params=room(buffers + list(scratch), most),
        cost_estimate=pl.CostEstimate(flops=0, bytes_accessed=0, transcendentals=0),
    )(*arrays)


def nn(a, b):
    return jnp.dot(a, b, preferred_element_type=F32)


def nt(a, b):
    return lax.dot_general(a, b, (((1,), (1,)), ((), ())), preferred_element_type=F32)


def tn(a, b):
    return lax.dot_general(a, b, (((0,), (0,)), ((), ())), preferred_element_type=F32)


def colsum(v):
    return jnp.sum(v, axis=0, keepdims=True)


def wide(m, n):
    return jnp.concatenate([m] * n, axis=1)


def reader(vec_ref):
    return lambda row, lo, n: vec_ref[row : row + 1, lo : lo + n]


def piece_masks(section, over_z):
    place = lax.axis_index("dp") % 16
    x_bit, y_bit, low, high = place & 1, (place >> 1) & 1, (place >> 2) & 1, place >> 3
    rest = section * 16 + (low * 2 + high if over_z else 0)
    return rest + x_bit * 8 + y_bit * 4, rest + y_bit * 8 + x_bit * 4


def piece_rows(masks, p, rows):
    return pl.multiple_of((p ^ masks[p >> 4]) * rows, 64)


def row_chunks(body, start):
    return lax.fori_loop(0, PIX // 32, lambda i, carry: body(pl.ds(pl.multiple_of(i * 32, 32), 32), carry), start,
                         unroll=True)


def normalized(v):
    cen = v - jnp.mean(v, axis=-1, keepdims=True)
    inv = lax.rsqrt(jnp.mean(cen * cen, axis=-1, keepdims=True) + EPS)
    return cen * inv, inv


def norm_gradient(up, xhat, inv, gain):
    g = up * gain
    return inv * (g - jnp.mean(g, axis=-1, keepdims=True) - xhat * jnp.mean(g * xhat, axis=-1, keepdims=True))


def conv_rows(src_ref, taps_ref, flip, bias, store):
    def row(h, carry):
        accs = [bias] * CANVAS if bias is not None else [None] * CANVAS
        for a in range(KS):
            ks = []
            for e in range(KS):
                t = (KS - 1 - a) * KS + (KS - 1 - e) if flip else a * KS + e
                ks.append(taps_ref[t * GROUPS : (t + 1) * GROUPS, :])
            for w2 in range(CANVAS):
                x = vreg(src_ref, (h + a) * CANVAS + w2)
                for e in range(KS):
                    w = w2 + 3 - e
                    if 0 <= w < CANVAS:
                        term = x * ks[e]
                        accs[w] = term if accs[w] is None else accs[w] + term
        for w in range(CANVAS):
            store(h * CANVAS + w, accs[w])
        return carry

    lax.fori_loop(0, CANVAS, row, 0)


def vreg(ref, index):
    return ref[pl.ds(pl.multiple_of(index * GROUPS, GROUPS), GROUPS), :]


def zero_border(ref):
    zeros = jnp.zeros((3 * CANVAS * GROUPS, LANES), F32)
    ref[0 : 3 * CANVAS * GROUPS, :] = zeros
    ref[(PAD_ROWS - 3 * CANVAS) * GROUPS :, :] = zeros


def lane_group(ref, g, rows=PIX, base=0):
    return ref[pl.ds(base + g, rows, stride=GROUPS), :]


def gn_forward_part(mask, x_ref, vec, taps, gates, win, wo, n1, cin, mix, p, gl, mid, br, mx_ref):
    zero_border(cin.ref)

    def norm_in(r, carry):
        xhat, _ = normalized(x_ref[r, :].astype(F32) * wide(mask[r, :], 4))
        n1.ref[r, :] = (xhat * vec(V_N1G, 0, C) + vec(V_N1S, 0, C)).astype(BF)
        return carry

    row_chunks(norm_in, 0)
    n1.go()
    win_ref = win.get()
    for n in range(4):
        m = nn(n1.ref[...], win_ref[:, n * 256 : (n + 1) * 256]) + vec(V_BIN, n * 256, 256)
        for half in range(2):
            g = 2 * n + half
            v = m[:, half * LANES : (half + 1) * LANES] * mask[...]
            cin.ref[pl.ds(3 * CANVAS * GROUPS + g, PIX, stride=GROUPS), :] = v
            if g == 0:
                p.ref[:, 0:LANES] = v
    cin.go()
    taps_ref = taps.get()
    bias = taps_ref[49 * GROUPS : 50 * GROUPS, :]

    def keep(pixel, acc):
        mx_ref[pl.ds(pl.multiple_of(pixel * GROUPS, GROUPS), GROUPS), :] = acc * (1.0 / 3.0)

    conv_rows(cin.ref, taps_ref, False, bias, keep)
    for g in range(GROUPS):
        mix.ref[:, g * LANES : (g + 1) * LANES] = lane_group(mx_ref, g)
    mix.go()
    gates_ref, wo_ref = gates.get(), wo.get()
    gl.ref[:, 0:128] = (p.ref[:, 0:128] * pltpu.roll(mix.ref[:, 0:128], 64, 1)).astype(BF)
    p1 = nn(gl.ref[:, 0:128], gates_ref[256:384, 256:384]) + vec(V_B1, 0, 128)
    p.ref[:, 128:256] = p1
    gl.ref[:, 128:256] = (p1 * mix.ref[:, 128:256]).astype(BF)
    p2 = nn(gl.ref[:, 128:256], gates_ref[256:384, 0:256]) + vec(V_B2, 0, 256)
    p.ref[:, 256:512] = p2
    gl.ref[:, 256:512] = (p2 * mix.ref[:, 256:512]).astype(BF)
    for n in range(2):
        c = 256 * n
        p3 = nn(gl.ref[:, 256:512], gates_ref[0:256, c : c + 256]) + vec(V_B3, c, 256)
        p.ref[:, 512 + c : 768 + c] = p3
        gl.ref[:, 512 + c : 768 + c] = (p3 * mix.ref[:, 512 + c : 768 + c]).astype(BF)
    p.go()
    gl.go()
    for n in range(2):
        c = 256 * n
        b = nn(gl.ref[:, 512:1024], wo_ref[:, c : c + 256]) + vec(V_BO, c, 256)
        br.ref[:, c : c + 256] = b.astype(BF)
        start = x_ref[:, c : c + 256].astype(F32) * wide(mask[...], 2)
        mid.ref[:, c : c + 256] = start + vec(V_BS, c, 256) * b
    br.go()
    if isinstance(mid, Ship):
        mid.go()


def mlp_forward_part(mask, mid_ref, vec, we, wr, n2_ref, act_ref, slope_ref, out_ref, res_ref):
    def norm_mid(r, carry):
        xhat, _ = normalized(mid_ref[r, :])
        n2_ref[r, :] = (xhat * vec(V_N2G, 0, C) + vec(V_N2S, 0, C)).astype(BF)
        return carry

    row_chunks(norm_mid, 0)
    we_ref = we.get()
    for j in range(8):
        c = 256 * j
        pre = nn(n2_ref[...], we_ref[:, c : c + 256]) + vec(V_BE, c, 256)
        cum = 0.5 * (1.0 + lax.erf(pre * 0.7071067811865476))
        act_ref[:, c : c + 256] = (pre * cum).astype(BF)
        slope = cum + pre * jnp.exp(-0.5 * pre * pre) * 0.3989422804014327
        slope_ref[:, c : c + 256] = slope.astype(BF)
    wr_ref = wr.get()
    for n in range(2):
        c = 256 * n
        out = nn(act_ref[...], wr_ref[:, c : c + 256]) + vec(V_BR, c, 256)
        out_ref[:, c : c + 256] = out.astype(BF)
        res = wide(mask[...], 2) * (mid_ref[:, c : c + 256] + vec(V_MS, c, 256) * out)
        res_ref[:, c : c + 256] = res.astype(BF)


def mlp_back_part(mask, masks, dy_ref, vec, n2_ref, act_ref, slope_ref, out_ref, mid_ref, we, wr,
                  dmid, mvec, bucket, dout_ref, dpre_ref, dn2_ref):
    mvec.ref[...] = jnp.zeros_like(mvec.ref)
    for n in range(2):
        c = 256 * n
        dyr = dy_ref[:, c : c + 256].astype(F32) * wide(mask[...], 2)
        dmid.ref[:, c : c + 256] = dyr
        dout = (vec(V_MS, c, 256) * dyr).astype(BF)
        dout_ref[:, c : c + 256] = dout
        mvec.ref[3:4, c : c + 256] = colsum(dout.astype(F32))
        mvec.ref[4:5, c : c + 256] = colsum(dyr * out_ref[:, c : c + 256].astype(F32))
    wr_ref = wr.get()
    for j in range(8):
        c = 256 * j
        dw = tn(act_ref[:, c : c + 256], dout_ref[...]).astype(BF)
        for q in range(4):
            bucket.ref[pl.ds(piece_rows(masks, 4 * j + q, 128), 64), :] = dw[64 * q : 64 * q + 64, :]
        dact = nt(dout_ref[...], wr_ref[c : c + 256, :])
        dpre = (dact * slope_ref[:, c : c + 256].astype(F32)).astype(BF)
        dpre_ref[:, c : c + 256] = dpre
        mvec.ref[2:3, c : c + 256] = colsum(dpre.astype(F32))
    we_ref = we.get()
    for cb in range(4):
        dw = tn(n2_ref[...], dpre_ref[:, 512 * cb : 512 * cb + 512]).astype(BF)
        for q in range(8):
            rows = pl.multiple_of(piece_rows(masks, 8 * cb + q, 128) + 64, 64)
            bucket.ref[pl.ds(rows, 64), :] = dw[64 * q : 64 * q + 64, :]
    bucket.go()
    for n in range(2):
        c = 256 * n
        dn2_ref[:, c : c + 256] = nt(dpre_ref[...], we_ref[c : c + 256, :])

    def norm_back(r, carry):
        dgain, dshift = carry
        xhat, inv = normalized(mid_ref[r, :])
        up = dn2_ref[r, :]
        dmid.ref[r, :] = dmid.ref[r, :] + norm_gradient(up, xhat, inv, vec(V_N2G, 0, C))
        return dgain + colsum(up * xhat), dshift + colsum(up)

    zero = jnp.zeros((1, C), F32)
    dgain, dshift = row_chunks(norm_back, (zero, zero))
    mvec.ref[0:1, 0:C] = dgain
    mvec.ref[1:2, 0:C] = dshift


def pack_kernel(*refs):
    vectors, taps_in, w1, w2, w3, crop_ref = refs[:14], refs[14], refs[15], refs[16], refs[17], refs[18]
    vec_ref, taps_ref, gates_ref, mask_ref = refs[19:]
    crops = crop_ref[...]
    kind = jnp.where(lax.axis_index("section") == 0, crops[:, 0:1], crops[:, 1:2])
    side = jnp.where(kind == 0, SIDE_S, jnp.where(kind == 1, SIDE_M, CANVAS))
    r = lax.broadcasted_iota(jnp.int32, (PIX, LANES), 0)
    inside = ((r // CANVAS) < side) & ((r % CANVAS) < side)
    mask_ref[...] = inside.astype(F32)
    gates_ref[0:256, :] = w3[...]
    gates_ref[256:384, 0:256] = w2[...]
    gates_ref[256:384, 256:384] = jnp.concatenate([w1[...], jnp.zeros((64, 128), BF)], axis=0)
    gates_ref[256:384, 384:512] = jnp.zeros((128, 128), BF)
    vec_ref[...] = jnp.zeros_like(vec_ref)
    for row, ref in enumerate(vectors):
        n = ref.shape[1]
        vec_ref[row : row + 1, 0:n] = ref[...].astype(F32)
    taps = taps_in[...].astype(F32)
    bias = vectors[V_CB][...].astype(F32)
    for g in range(GROUPS):
        if g == 0:
            t = jnp.concatenate([jnp.zeros((49, 64), F32), taps[:, 0:64]], axis=1)
            b = jnp.concatenate([jnp.zeros((1, 64), F32), bias[:, 0:64]], axis=1)
        else:
            t = taps[:, g * LANES - 64 : g * LANES + 64]
            b = bias[:, g * LANES - 64 : g * LANES + 64]
        taps_ref[pl.ds(g, 49, stride=GROUPS), :] = t
        taps_ref[49 * GROUPS + g : 49 * GROUPS + g + 1, :] = b


def gn_forward_kernel(mask, x, vec, win, taps, gates, wo, n1, cin, mix, p, gl, mid, br, mx_ref):
    x_ref = x.get()
    gn_forward_part(mask.get(), x_ref, reader(vec.get()), taps, gates, win, wo, n1, cin, mix, p, gl, mid, br, mx_ref)


def middle_kernel(mask, mid0, vec0, we0, wr0, vec1, win, taps, gates, wo, we1, wr1, dy,
                  hidden, n2, act, slope, out, n1, cin, mix, p, gl, br, final, swap, dmid, mvec, bucket,
                  mx_ref, mid1, n2_1, act1, slope1, out1, dout_ref, dpre_ref, dn2_ref):
    section = lax.axis_index("section")
    masks = piece_masks(section, True)
    mask = mask.get()
    mid0_ref = mid0.get()
    vec0_ref = vec0.get()
    wr0.begin()
    for slot in (vec1, win, taps, gates, wo, we1, wr1, dy):
        slot.begin()
    mlp_forward_part(mask, mid0_ref, reader(vec0_ref), we0, wr0, n2.ref, act.ref, slope.ref, out.ref, hidden.ref)
    for ship in (hidden, n2, act, slope, out):
        ship.go()
    vec = reader(vec1.get())
    gn_forward_part(mask, hidden.ref, vec, taps, gates, win, wo, n1, cin, mix, p, gl, Slot(mid1, None), br, mx_ref)
    mlp_forward_part(mask, mid1, vec, we1, wr1, n2_1, act1, slope1, out1, final.ref)
    final.go()
    swap.ref[...] = jnp.where(section == 0, final.ref[...], hidden.ref[...])
    swap.go()
    mlp_back_part(mask, masks, dy.get(), vec, n2_1, act1, slope1, out1, mid1, we1, wr1,
                  dmid, mvec, bucket, dout_ref, dpre_ref, dn2_ref)


def mlp_back_kernel(mask, dy, vec, n2, act, slope, out, mid, wr, we, dmid, mvec, bucket,
                    dout_ref, dpre_ref, dn2_ref):
    mlp_back_part(mask.get(), piece_masks(lax.axis_index("section"), True), dy.get(), reader(vec.get()), n2.get(), act.get(), slope.get(), out.get(),
                  mid.get(), we, wr, dmid, mvec, bucket, dout_ref, dpre_ref, dn2_ref)


def gn_back_kernel(block, mask, dmid, br, vec, wo, mix, p, gates, mvec, taps, win, x, *rest):
    if block == 0:
        following, dv, swap, dbr, dp, dmg, dcp, gvec = rest[:8]
    else:
        dv, dvb, dbr, dp, dmg, dcp, gvec = rest[:7]
    dg_ref, dmix_ref, ds_ref, dn1_ref = rest[-4:]
    section = lax.axis_index("section")
    mask = mask.get()
    zero_border(dcp.ref)
    dmid_ref, br_ref = dmid.get(), br.get()
    vec = reader(vec.get())
    dbs, dbo = [], []
    for n in range(2):
        c = 256 * n
        dm = dmid_ref[:, c : c + 256]
        dbs.append(colsum(dm * br_ref[:, c : c + 256].astype(F32)))
        d = (vec(V_BS, c, 256) * dm).astype(BF)
        dbr.ref[:, c : c + 256] = d
        dbo.append(colsum(d.astype(F32)))
    dbr.go()
    wo_ref, mix_ref, p_ref = wo.get(), mix.get(), p.get()
    db3 = []
    for n in range(2):
        c = 256 * n
        dg = nt(dbr.ref[...], wo_ref[c : c + 256, :])
        d = (dg * mix_ref[:, 512 + c : 768 + c]).astype(BF)
        dmix_ref[:, 512 + c : 768 + c] = dg * p_ref[:, 512 + c : 768 + c] * (1.0 / 3.0)
        dp.ref[:, 512 + c : 768 + c] = d
        db3.append(colsum(d.astype(F32)))
    gates_ref = gates.get()
    dg = nt(dp.ref[:, 512:1024], gates_ref[0:256, :])
    d = (dg * mix_ref[:, 256:512]).astype(BF)
    dmix_ref[:, 256:512] = dg * p_ref[:, 256:512] * (1.0 / 3.0)
    dp.ref[:, 256:512] = d
    db2 = colsum(d.astype(F32))
    dg = nt(dp.ref[:, 256:512], gates_ref[256:384, 0:256])
    d = (dg * mix_ref[:, 128:256]).astype(BF)
    dmix_ref[:, 128:256] = dg * p_ref[:, 128:256] * (1.0 / 3.0)
    dp.ref[:, 128:256] = d
    db1 = colsum(d.astype(F32))
    dg = nt(dp.ref[:, 128:256], gates_ref[256:384, 256:384])
    dmix_ref[:, 0:128] = pltpu.roll(dg * p_ref[:, 0:128], 64, 1) * (1.0 / 3.0)
    dg_ref[...] = dg * pltpu.roll(mix_ref[:, 0:128], 64, 1)
    dp.ref[:, 0:128] = jnp.zeros((PIX, LANES), BF)
    dp.go()
    for g in range(GROUPS):
        dcp.ref[pl.ds(3 * CANVAS * GROUPS + g, PIX, stride=GROUPS), :] = dmix_ref[:, g * LANES : (g + 1) * LANES]
    dcp.go()

    def keep(pixel, acc):
        ds_ref[pl.ds(pl.multiple_of(pixel * GROUPS, GROUPS), GROUPS), :] = acc

    conv_rows(dcp.ref, taps.get(), True, None, keep)
    dbin = []
    for g in range(GROUPS):
        d = lane_group(ds_ref, g) * mask[...]
        if g == 0:
            d = d + dg_ref[...]
        d = d.astype(BF)
        dmg.ref[:, g * LANES : (g + 1) * LANES] = d
        dbin.append(colsum(d.astype(F32)))
    dmg.go()
    win_ref, x_ref = win.get(), x.get()
    next_ref = following.get() if block == 0 else None
    for n in range(2):
        c = 256 * n
        dn1_ref[:, c : c + 256] = nt(dmg.ref[...], win_ref[c : c + 256, :])

    def norm_back(r, carry):
        dgain, dshift = carry
        m = wide(mask[r, :], 4)
        xhat, inv = normalized(x_ref[r, :].astype(F32) * m)
        up = dn1_ref[r, :]
        d = m * (dmid_ref[r, :] + norm_gradient(up, xhat, inv, vec(V_N1G, 0, C)))
        dv.ref[r, :] = d
        if block == 0:
            swap.ref[r, :] = jnp.where(section == 0, next_ref[r, :], d)
        else:
            dvb.ref[r, :] = d.astype(BF)
        return dgain + colsum(up * xhat), dshift + colsum(up)

    zero = jnp.zeros((1, C), F32)
    dgain, dshift = row_chunks(norm_back, (zero, zero))
    z = jnp.zeros((1, LANES), F32)
    mvec_ref = mvec.get()
    rows = [
        dgain,
        dshift,
        jnp.concatenate(dbin[0:4], axis=1),
        jnp.concatenate(dbin[4:8], axis=1),
        jnp.concatenate([db1, z, z, z], axis=1),
        jnp.concatenate([db2, z, z], axis=1),
        jnp.concatenate(db3, axis=1),
        jnp.concatenate(dbo, axis=1),
        jnp.concatenate(dbs, axis=1),
        mvec_ref[0:1, 0:C],
        mvec_ref[1:2, 0:C],
        mvec_ref[2:3, 0:512],
        mvec_ref[2:3, 512:1024],
        mvec_ref[2:3, 1024:1536],
        mvec_ref[2:3, 1536:2048],
        mvec_ref[3:4, 0:C],
        mvec_ref[4:5, 0:C],
    ]
    rows.append(jnp.zeros((32 - len(rows), C), F32))
    gvec.ref[...] = jnp.concatenate(rows, axis=0).astype(BF)


def gn_weights_kernel(n1, dmg, gl, dbr, dp, gvec, cin, dcp, bucket, dk_ref):
    masks = piece_masks(lax.axis_index("section"), False)

    def put(p, val, sub=0):
        n = val.shape[0]
        bucket.ref[pl.ds(pl.multiple_of(piece_rows(masks, p, 64) + sub, 16), n), :] = val

    n1_ref, dmg_ref = n1.get(), dmg.get()
    for cb in range(2):
        dw = tn(n1_ref[...], dmg_ref[:, 512 * cb : 512 * cb + 512]).astype(BF)
        for q in range(8):
            put(8 * cb + q, dw[64 * q : 64 * q + 64, :])
    gl_ref, dbr_ref, dp_ref = gl.get(), dbr.get(), dp.get()
    dw = tn(gl_ref[:, 512:1024], dbr_ref[...]).astype(BF)
    for q in range(8):
        put(16 + q, dw[64 * q : 64 * q + 64, :])
    dw = tn(gl_ref[:, 256:512], dp_ref[:, 512:1024]).astype(BF)
    for q in range(4):
        put(24 + q, dw[64 * q : 64 * q + 64, :])
    dw = tn(gl_ref[:, 128:256], dp_ref[:, 256:512]).astype(BF)
    put(28, jnp.concatenate([dw[0:64, :], dw[64:128, :]], axis=1))
    dw1 = tn(gl_ref[:, 0:128], dp_ref[:, 128:256]).astype(BF)
    put(31, jnp.concatenate([dw1[16 * i : 16 * i + 16, :] for i in range(4)], axis=1))
    put(31, jnp.zeros((16, 512), BF), 16)
    put(31, gvec.get()[...], 32)
    cin_ref, dcp_ref = cin.get(), dcp.get()
    dk_ref[...] = jnp.zeros_like(dk_ref)
    for taps in ((0, 1), (2, 3), (4, 5), (6,)):

        def row(h, accs):
            accs = list(accs)
            ds = [vreg(dcp_ref, (h + 3) * CANVAS + w) for w in range(CANVAS)]
            for i, a in enumerate(taps):
                for w2 in range(CANVAS):
                    x = vreg(cin_ref, (h + a) * CANVAS + w2)
                    for e in range(KS):
                        w = w2 + 3 - e
                        if 0 <= w < CANVAS:
                            accs[i * KS + e] = accs[i * KS + e] + x * ds[w]
            if len(taps) == 1:
                for w in range(CANVAS):
                    accs[KS] = accs[KS] + ds[w]
            return tuple(accs)

        count = len(taps) * KS + (1 if len(taps) == 1 else 0)
        accs = lax.fori_loop(0, CANVAS, row, tuple(jnp.zeros((GROUPS, LANES), F32) for _ in range(count)))
        for i in range(count):
            t = taps[0] * KS + i
            dk_ref[t * GROUPS : (t + 1) * GROUPS, :] = accs[i]
    for half in range(2):
        put(29 + half, jnp.concatenate([lane_group(dk_ref, 4 * half + i, 64) for i in range(4)], axis=1).astype(BF))


def start_half(far, rows, sources, buf, sems, over_z):
    section = lax.axis_index("section")
    half = 1 - section if far else section
    masks = piece_masks(section, over_z)
    mask = jnp.where(half == 0, masks[0], masks[1]) & 15
    for p in range(16):
        off = pl.multiple_of((p ^ mask) * rows, 64)
        dst = buf.at[p * rows : (p + 1) * rows]
        for sec in range(2):

            @pl.when(section == sec)
            def _():
                pltpu.make_async_copy(sources[sec].at[pl.ds(off, rows)], dst, sems.at[p // 4]).start()

    return half


def wait_quarter(i, rows, sources, buf, sems):
    part = buf.at[pl.ds(i * 4 * rows, 4 * rows)]
    pltpu.make_async_copy(sources[0].at[pl.ds(0, 4 * rows)], part, sems.at[i]).wait()


def mlp_finish_kernel(far, *refs):
    sources = refs[:2]
    wr_any, we_any, buf, wr_ref, we_ref, sems, out_sems = refs[-7:]
    half = start_half(far, 128, sources, buf, sems, True)
    copies = []
    for i in range(4):
        wait_quarter(i, 128, sources, buf, sems)
        cb = i // 2
        for q in range(4):
            p = 4 * i + q
            r = p % 8
            wr_ref[64 * p : 64 * p + 64, :] = buf[128 * p : 128 * p + 64, :].astype(F32)
            we_ref[64 * r : 64 * r + 64, 512 * cb : 512 * cb + 512] = buf[128 * p + 64 : 128 * p + 128, :].astype(F32)
        rows = pl.ds(pl.multiple_of(half * 1024 + 256 * i, 256), 256)
        copies.append(pltpu.make_async_copy(wr_ref.at[256 * i : 256 * i + 256], wr_any.at[rows], out_sems.at[i]))
        part = slice(256 * (i % 2), 256 * (i % 2) + 256)
        cols = pl.ds(pl.multiple_of(half * 1024 + 512 * cb, 512), 512)
        src = we_ref.at[part, 512 * cb : 512 * cb + 512]
        copies.append(pltpu.make_async_copy(src, we_any.at[part, cols], out_sems.at[4 + i]))
        copies[-2].start()
        copies[-1].start()
    for copy in copies:
        copy.wait()


def gn_finish_kernel(far, *refs):
    sources = refs[:2]
    count = len(GN_OUTS)
    results, buf, vals, sems, out_sems = refs[-2 * count - 3 : -count - 3], refs[-count - 3], refs[-count - 2 : -2], refs[-2], refs[-1]
    (n1g, n1s, win, bin_, conv, cbias, w1, b1, w2, b2, w3, b3, wo, bo, bs, n2g, n2s, be, br, ms) = vals
    half = start_half(far, 64, sources, buf, sems, False)
    for i in range(4):
        wait_quarter(i, 64, sources, buf, sems)

    def out(i):
        return pltpu.make_async_copy(vals[i], results[i], out_sems.at[i])

    @pl.when(half == 0)
    def _():
        for cb in range(2):
            win[:, 512 * cb : 512 * cb + 512] = buf[512 * cb : 512 * cb + 512, :].astype(F32)
        out(2).start()
        out(2).wait()

    @pl.when(half == 1)
    def _():
        wo[...] = buf[0:512, :].astype(F32)
        out(12).start()
        w3[...] = buf[512:768, :].astype(F32)
        out(10).start()
        for i in range(2):
            w2[64 * i : 64 * i + 64, :] = buf[768:832, 256 * i : 256 * i + 256].astype(F32)
        for i in range(4):
            w1[16 * i : 16 * i + 16, :] = buf[960:976, 128 * i : 128 * i + 128].astype(F32)
        taps = jnp.concatenate([buf[832:896, :], buf[896:960, :]], axis=1).astype(F32)
        for i in range(49):
            conv[i] = taps[i : i + 1, 64:1024]
        cbias[...] = taps[49:50, 64:1024]
        v = buf[992:1024, :].astype(F32)
        n1g[...] = v[0:1]
        n1s[...] = v[1:2]
        bin_[:, 0:512] = v[2:3]
        bin_[:, 512:1024] = v[3:4]
        b1[...] = v[4:5, 0:128]
        b2[...] = v[5:6, 0:256]
        b3[...] = v[6:7]
        bo[...] = v[7:8]
        bs[...] = v[8:9]
        n2g[...] = v[9:10]
        n2s[...] = v[10:11]
        for i in range(4):
            be[:, 512 * i : 512 * i + 512] = v[11 + i : 12 + i]
        br[...] = v[15:16]
        ms[...] = v[16:17]
        rest = [i for i in range(count) if i not in (2, 10, 12)]
        for i in rest:
            out(i).start()
        for i in rest + [10, 12]:
            out(i).wait()


def place_kernel(first, second, got, out):
    section = lax.axis_index("section")

    @pl.when(section == 0)
    def _():
        out[0] = first[...]
        out[1] = got[...]

    @pl.when(section != 0)
    def _():
        out[0] = got[...]
        out[1] = second[...]


VM = pl.BlockSpec(memory_space=pltpu.VMEM)


def plain_call(kernel, name, operands, outs, scratch, most=False, aliases={}):
    return pl.pallas_call(
        kernel,
        name=name,
        out_shape=[shape for _, shape in outs],
        in_specs=[spec for spec, _ in operands],
        out_specs=[spec for spec, _ in outs],
        scratch_shapes=scratch,
        compiler_params=room([a for spec, a in operands + outs if spec is VM] + scratch, most),
        input_output_aliases=aliases,
        cost_estimate=pl.CostEstimate(flops=0, bytes_accessed=0, transcendentals=0),
    )(*[array for _, array in operands])


def on(spec, *arrays):
    return [(spec, a) for a in arrays]


PIXEL_CHANNELS = vmem(PIX * GROUPS, LANES, F32)
FIELD_F32, FIELD_BF = sds((PIX, C), F32), sds((PIX, C), BF)
CONV_F32 = sds((PAD_ROWS * GROUPS, LANES), F32)
WIDE_F32, WIDE_BF = sds((PIX, 1024), F32), sds((PIX, 1024), BF)
HIDE_BF = sds((PIX, FF), BF)
GN_SAVED = [FIELD_BF, CONV_F32, WIDE_F32, WIDE_F32, WIDE_BF]


def run_pack(vectors, taps, gates, crop):
    outs = on(VM, sds((VEC_ROWS, FF), F32), sds((50 * GROUPS, LANES), F32), sds((384, 512), BF), sds((PIX, LANES), F32))
    return plain_call(pack_kernel, "pack", on(VM, *vectors, taps, *gates, crop), outs, [], True)


def run_gn_forward(mask, images, w):
    operands = [load(mask), image(images)] + [pick(0, w[k]) for k in ("vec", "win", "taps", "gates", "wo")]
    return call(gn_forward_kernel, "gnconv_forward", operands, GN_SAVED + [FIELD_F32, FIELD_BF],
                [PIXEL_CHANNELS], True)


def run_middle(mask, mid, cotangent, w):
    operands = [load(mask), load(mid)] + [pick(0, w[k]) for k in ("vec", "we", "wr")]
    operands += [pick(1, w[k]) for k in ("vec", "win", "taps", "gates", "wo", "we", "wr")] + [image(cotangent)]
    outs = [FIELD_BF, FIELD_BF, HIDE_BF, HIDE_BF, FIELD_BF] + GN_SAVED + [FIELD_BF, FIELD_BF, FIELD_BF, FIELD_F32]
    outs += [sds((8, FF), F32), Halves(4096)]
    scratch = [PIXEL_CHANNELS, vmem(PIX, C, F32), vmem(PIX, C, BF), vmem(PIX, FF, BF), vmem(PIX, FF, BF),
               vmem(PIX, C, BF), vmem(PIX, C, BF), vmem(PIX, FF, BF), vmem(PIX, C, F32)]
    return call(middle_kernel, "middle", operands, outs, scratch, True, 4)


def run_mlp_back(mask, dy, n2, act, slope, out, mid, w):
    operands = [load(mask), near(dy), pick(0, w["vec"]), load(n2), load(act), load(slope), load(out), load(mid),
                pick(0, w["wr"]), pick(0, w["we"])]
    outs = [FIELD_F32, sds((8, FF), F32), Halves(4096)]
    scratch = [vmem(PIX, C, BF), vmem(PIX, FF, BF), vmem(PIX, C, F32)]
    return call(mlp_back_kernel, "mlp_backward", operands, outs, scratch, True)


def run_gn_back(block, mask, x, following, dmid, mvec, mix, p, br, w):
    far = load if block == 1 else near
    operands = [load(mask), far(dmid), load(br), pick(block, w["vec"]), pick(block, w["wo"]), load(mix), load(p),
                pick(block, w["gates"]), far(mvec), pick(block, w["taps"]), pick(block, w["win"])]
    operands += [image(x), near(following)] if block == 0 else [load(x)]
    outs = [FIELD_F32, FIELD_F32 if block == 0 else FIELD_BF, FIELD_BF, WIDE_BF, WIDE_BF, CONV_F32, sds((32, 512), BF)]
    scratch = [vmem(PIX, LANES, F32), vmem(PIX, 1024, F32), PIXEL_CHANNELS, vmem(PIX, C, F32)]
    return call(functools.partial(gn_back_kernel, block), "gnconv_backward", operands, outs, scratch, block == 1)


def run_gn_weights(block, n1, dmg, gl, dbr, dp, gvec, cin, dcp):
    operands = [load(n1), near(dmg), load(gl), near(dbr), near(dp), near(gvec), load(cin), near(dcp)]
    return call(gn_weights_kernel, "gnconv_weights", operands, [Halves(2048)], [vmem(64 * GROUPS, LANES, F32)],
                block == 1)


def turn_kernel(token, out):
    out[...] = jnp.zeros_like(out)


def run_turn(token):
    return plain_call(turn_kernel, "turn", on(ANY, token), on(VM, sds((8, LANES), F32)), [])[0]


def run_mlp_finish(far, sources, earlier=()):
    outs = on(ANY, sds((FF, C), F32), sds((C, FF), F32))
    scratch = [vmem(2048, 512, BF), vmem(1024, C, F32), vmem(C, 1024, F32), pltpu.SemaphoreType.DMA((4,)),
               pltpu.SemaphoreType.DMA((8,))]
    return plain_call(functools.partial(mlp_finish_kernel, far), "mlp_finish", on(ANY, *sources, *earlier), outs, scratch,
                      True, {2: 0, 3: 1} if far else {})


GN_OUTS = [sds((1, w) if isinstance(w, int) else w, F32) for w in (
    512, 512, (512, 1024), 1024, (49, 1, 960), 960, (64, 128), 128, (128, 256), 256, (256, 512), 512, (512, 512), 512,
    512, 512, 512, 2048, 512, 512)]


def run_gn_finish(far, sources, earlier=()):
    scratch = [vmem(1024, 512, BF)] + [pltpu.VMEM(o.shape, F32) for o in GN_OUTS]
    scratch += [pltpu.SemaphoreType.DMA((4,)), pltpu.SemaphoreType.DMA((len(GN_OUTS),))]
    return plain_call(functools.partial(gn_finish_kernel, far), "gn_finish", on(ANY, *sources, *earlier),
                      on(ANY, *GN_OUTS), scratch, True, {2 + i: i for i in range(len(GN_OUTS))} if far else {})


def run_place(first, second, got):
    outs = on(VM, sds((2, PIX, C), first.dtype))
    return plain_call(place_kernel, "place", on(VM, first, second, got), outs, [])[0]


AXES = ("section", "dp")
X_BIT, Y_BIT, Z_LOW, Z_HIGH = 1, 2, 4, 8

FIRST, SECOND, LOW, HIGH = (X_BIT, Y_BIT), (Y_BIT, X_BIT), (Z_LOW, Z_LOW), (Z_HIGH, Z_HIGH)

BUCKETS = ("m1", "g1", "m0", "g0")
STEPS = ("core", "x1", "x2", "zl", "zh", "fl", "fh", "ZH", "ZL", "X2", "X1", "Core")
OTHERS = ("fo", "go")
KERNELS = ("K1", "K2", "K3", "K4", "K5", "MF1", "MF2", "GF1", "GF2", "P1", "P2")

ORDER = (
    1, 60, 49, -1, 2, 62, 61, 13, -2, 3, 25, -25, 26, 63, -3, 4, 50, -13, 14, 64, -4, 5, -26, 27, 37, -37, 38, -27,
    28, -5, 8, -28, 29, -8, 9, -49, 69, -14, 15, -29, 32, -38, 39, -9, 10, -15, 18, -39, 42, -32, 33, -33, 34, -18,
    19, -10, 11, -42, 43, -34, 35, -50, 70, -19, 22, -43, 46, -22, 23, -11, 12, -35, 36, 65, -12, -46, 47, -23, 24,
    -36, 66, -47, 48, 67, -24, -48, 68,
)


def event_name(number):
    at = abs(number) - 1
    if at >= 59:
        return KERNELS[at - 59]
    sign = "+" if number > 0 else "-"
    return sign + (OTHERS[at - 48] if at >= 48 else BUCKETS[at // 12] + "." + STEPS[at % 12])


GROUPED = (("m1", ("m1",)), ("m0", ("m0",)), ("g1", ("g1",)), ("g0", ("g0",)))


def after(x, *others):
    return lax.optimization_barrier((x,) + others)[0]


class Flow:
    def __init__(self, count):
        self.count = count
        self.token = None
        self.flying = {}

    def exchange(self, x, flips=None, only=None):
        n = self.count
        other, bits = (1, (0, 0)) if flips is None else (0, flips)
        pairs = [
            (s * n + d, (s ^ other) * n + (d ^ bits[s])) for s in range(2) for d in range(n) if only is None or s == only
        ]
        return lax.ppermute(x, AXES, pairs)

    def start(self, name, x, flips=None, only=None):
        with jax.named_scope("transfer_" + name.replace(".", "_")):
            self.flying[name] = self.exchange(after(x, self.token), flips, only)

    def end(self, name):
        got, token = lax.optimization_barrier((self.flying.pop(name), self.token))
        self.token = run_turn(token)
        return got

    def tie(self, x):
        return after(x, self.token)


VECTORS = (0, 1, 3, 5, 7, 9, 11, 13, 14, 15, 16, 18, 20, 21)


def on_device(flow, images, cotangent, crop, *stacked):
    images = images.reshape(2, PIX, C)
    cotangent = cotangent.reshape(2, PIX, C)
    win, wo, we, wr = [stacked[i][0] for i in (2, 12, 17, 19)]
    vec, taps, gates, mask = run_pack(
        [stacked[i] for i in VECTORS], stacked[4][0], [stacked[i][0] for i in (6, 8, 10)], crop.reshape(1, 2)
    )
    swap = flow.exchange
    win_other, wo_other = swap(win), swap(wo)
    taps_other, vec_other, gates_other = swap(taps), swap(vec), swap(gates)
    we, wr = after((we, wr), win_other, wo_other, taps_other, vec_other, gates_other)
    we_other, wr_other = swap(we), swap(wr)
    w = {
        "win": (win, win_other), "wo": (wo, wo_other), "we": (we, we_other), "wr": (wr, wr_other),
        "vec": (vec, vec_other), "taps": (taps, taps_other), "gates": (gates, gates_other),
    }

    n1_0, cin_0, mix_0, p_0, gl_0, mid_0, br_0 = run_gn_forward(mask, images, w)
    (hidden, n2_0, act_0, slope_0, out_0, n1_1, cin_1, mix_1, p_1, gl_1, br_1, final, field_swap, dmid_1, mvec_1,
     keep, send) = run_middle(mask, mid_0, cotangent, w)
    flow.token = mvec_1
    value = {"m1.core": (keep, send)}
    chips = flow.count // 16

    def sum_all(total):
        if chips > 1:
            groups = [[g * 16 + r for g in range(chips)] for r in range(16)]
            total = lax.psum(total, "dp", axis_index_groups=groups)
        return total

    def begin(name):
        bucket, step = name.split(".")
        only = {"m1": 0, "g1": 0, "m0": 1, "g0": 1}.get(bucket)
        flips = {"x1": FIRST, "x2": SECOND, "zl": LOW, "zh": HIGH, "fl": LOW, "fh": HIGH}.get(step.lower())
        whole = step.isupper() or step in ("Core", "fl", "fh")
        flow.start(name, value[name] if whole else value[name][1], flips, only if step == "Core" else None)

    def finish(name):
        bucket, step = name.split(".")
        got = flow.end(name)
        mine = value[name]
        after_step = {"core": "x1", "x1": "x2", "x2": "zl" if bucket[0] == "m" else "fl", "zl": "zh", "fl": "fh",
                      "ZH": "ZL", "ZL": "X2", "X2": "X1", "X1": "Core"}
        if step == "Core":
            value[bucket] = (mine, got)
            return
        if step.isupper():
            total = jnp.stack([mine, got])
            value[bucket + "." + after_step[step]] = total.reshape(-1, 512) if step == "X1" else total
            return
        if step in ("fl", "fh"):
            total = mine + got
        else:
            mine = mine[0]
            if step == "core":
                shape = (2, 2, 2, 2, mine.shape[0] // 16, 512)
                mine, got = mine.reshape(shape), got.reshape(shape)
            if step in ("core", "x1", "zl"):
                total = (mine[0] + got[0], mine[1] + got[1])
            else:
                total = mine + got
        if step == "x2" and bucket[0] == "m":
            total = (total[0], total[1])
        if step in ("zh", "fh"):
            total = sum_all(total)
            for group, members in GROUPED:
                if bucket in members:
                    value["sum of " + bucket] = total
                    sums = [value.get("sum of " + m) for m in members]
                    if all(v is not None for v in sums):
                        value[group + (".ZH" if step == "zh" else ".X2")] = jnp.concatenate(sums, axis=-2)
        else:
            value[bucket + "." + after_step[step]] = total

    for event in map(event_name, ORDER):
        if event in ("+fo", "+go"):
            flow.start(event[1:], field_swap if event == "+fo" else grad_swap)
        elif event in ("-fo", "-go"):
            value[event[1:]] = flow.end(event[1:])
        elif event[0] == "+":
            begin(event[1:])
        elif event[0] == "-":
            finish(event[1:])
        elif event == "K1":
            back = run_gn_back(1, mask, hidden, None, flow.tie(dmid_1), mvec_1, mix_1, p_1, br_1, w)
            dv_1, dvb, dbr_1, dp_1, dmg_1, dcp_1, gvec_1 = back
            flow.token = gvec_1
        elif event == "K2":
            value["g1.core"] = run_gn_weights(1, n1_1, dmg_1, gl_1, dbr_1, dp_1, flow.tie(gvec_1), cin_1, dcp_1)
            flow.token = value["g1.core"][0]
        elif event == "K3":
            dmid_0, mvec_0, *value["m0.core"] = run_mlp_back(mask, flow.tie(dvb), n2_0, act_0, slope_0, out_0, mid_0, w)
            flow.token = mvec_0
        elif event == "K4":
            back = run_gn_back(0, mask, images, dv_1, flow.tie(dmid_0), mvec_0, mix_0, p_0, br_0, w)
            dv_0, grad_swap, dbr_0, dp_0, dmg_0, dcp_0, gvec_0 = back
            flow.token = gvec_0
        elif event == "K5":
            value["g0.core"] = run_gn_weights(0, n1_0, dmg_0, gl_0, dbr_0, dp_0, flow.tie(gvec_0), cin_0, dcp_0)
            flow.token = value["g0.core"][0]
        elif event == "P1":
            flow.token = block_outputs = run_place(hidden, final, flow.tie(value["fo"]))
        elif event == "P2":
            flow.token = input_grads = run_place(dv_0, dv_1, flow.tie(value["go"]))
        elif event in ("MF1", "MF2"):
            far = event == "MF2"
            one, two = (value[b][1] if far else value[b + ".Core"] for b in ("m0", "m1"))
            wr, we = mlp_grads = run_mlp_finish(far, (flow.tie(one), two), mlp_grads if far else ())
            flow.token = wr
        elif event in ("GF1", "GF2"):
            far = event == "GF2"
            one, two = (value[b][1] if far else value[b + ".Core"] for b in ("g0", "g1"))
            grads = run_gn_finish(far, (flow.tie(one), two), grads if far else ())
            flow.token = grads[0]
    (n1g, n1s, win, bin_, conv, cbias, w1, b1, w2, b2, w3, b3, wo, bo, bs, n2g, n2s, be, br, ms) = grads
    shape = (1, 2, 1, CANVAS, CANVAS, C)
    return (
        block_outputs.reshape(shape), input_grads.reshape(shape), n1g, n1s, win[None], bin_, conv.reshape(1, 49, 960), cbias,
        w1[None], b1, w2[None], b2, w3[None], b3, wo[None], bo, bs, n2g, n2s, we[None], be, wr[None], br, ms,
    )


def solution(mesh):
    count = mesh.shape["dp"]
    image = P(None, "dp", None, None, None)
    one, two = P("section", None), P("section", None, None)
    weights = (one, one, two, one, two, one, two, one, two, one, two, one, two, one, one, one, one, two, one, two,
               one, one)
    field = P("section", None, "dp", None, None, None)
    return jax.shard_map(
        lambda *arrays: on_device(Flow(count), *arrays),
        mesh=mesh,
        in_specs=(image, image, P(None, "dp")) + weights,
        out_specs=(field, field) + weights,
        check_vma=False,
    )
```

```python
import functools
import math

import jax
import jax.numpy as jnp
from jax import lax
from jax.experimental import pallas as pl
from jax.experimental.pallas import tpu as pltpu
from jax.sharding import PartitionSpec as P

SIDE_S = 8
SIDE_M = 12
CANVAS = 16
PIX = CANVAS * CANVAS
C = 512
FF = 2048
LANES = 128
GROUPS = 8
EPS = 1e-06
KS = 7
PAD_ROWS = (CANVAS + 6) * CANVAS
BF = jnp.bfloat16
F32 = jnp.float32
SPARE_VMEM = 8 * 1024 * 1024
MOST_VMEM = 58 * 1024 * 1024

V_N1G, V_N1S, V_BIN, V_CB, V_B1, V_B2, V_B3, V_BO, V_BS, V_N2G, V_N2S, V_BE, V_BR, V_MS = range(14)
VEC_ROWS = 16


class Slot:
    def __init__(self, ref, copy, start=None):
        self.ref, self.copy, self.start = ref, copy, start

    def begin(self):
        if self.start is not None:
            self.start()
            self.start = None

    def get(self):
        self.begin()
        if self.copy is not None:
            self.copy.wait()
            self.copy = None
        return self.ref


class Ship:
    def __init__(self, ref, copies):
        self.ref, self.copies, self.started = ref, copies, False

    def go(self):
        for copy in self.copies:
            copy.start()
        self.started = True


class Halves:
    def __init__(self, rows):
        self.shape, self.dtype = (rows, 512), BF


def load(array):
    return ("load", array)


def near(array):
    return ("near", array)


def image(array):
    return ("image", array)


def pick(block, pair):
    return (block, pair)


def smem(array):
    return ("smem", array)


def sds(shape, dtype):
    return jax.ShapeDtypeStruct(shape, dtype)


def vmem(rows, cols, dtype):
    return pltpu.VMEM((rows, cols), dtype)


def room(shapes, most):
    if most:
        return pltpu.CompilerParams(vmem_limit_bytes=MOST_VMEM)
    total = 0
    for shape in shapes:
        if len(getattr(shape, "shape", ())) >= 2 and jnp.issubdtype(shape.dtype, jnp.floating):
            total += math.prod(shape.shape) * jnp.dtype(shape.dtype).itemsize
    return pltpu.CompilerParams(vmem_limit_bytes=total + SPARE_VMEM)


SMEM = pl.BlockSpec(memory_space=pltpu.SMEM)
ANY = pl.BlockSpec(memory_space=pl.ANY)
HBM = pl.BlockSpec(memory_space=pltpu.HBM)


def start_pick(is_own, own, other, dst, sem):
    @pl.when(is_own)
    def _():
        pltpu.make_async_copy(own, dst, sem).start()

    @pl.when(jnp.logical_not(is_own))
    def _():
        pltpu.make_async_copy(other, dst, sem).start()


def call(kernel, name, operands, outs, scratch, most=False, early=99):
    specs, arrays, buffers = [], [], []
    for kind, value in operands:
        if kind == "smem":
            specs.append(SMEM)
            arrays.append(value)
            continue
        sources = value if isinstance(kind, int) else (value,)
        specs += [ANY if kind == "near" else HBM] * len(sources)
        arrays += list(sources)
        shape = value.shape[1:] if kind == "image" else sources[0].shape
        buffers.append(pltpu.VMEM(shape, sources[0].dtype))
    shapes = []
    for out in outs:
        half = sds((out.shape[0] // 2, out.shape[1]), out.dtype) if isinstance(out, Halves) else None
        shapes += [half, half] if half is not None else [out]
    n_in, n_out, n_load, n_ship = len(arrays), len(shapes), len(buffers), len(outs)
    buffers += [pltpu.VMEM(out.shape, out.dtype) for out in outs]

    def body(*refs):
        ins, results = refs[:n_in], refs[n_in : n_in + n_out]
        bufs = refs[n_in + n_out : n_in + n_out + n_load + n_ship]
        rest, sems = refs[n_in + n_out + n_load + n_ship : -1], refs[-1]
        section = lax.axis_index("section")
        slots, at, nth = [], 0, 0
        for kind, value in operands:
            if kind == "smem":
                slots.append(ins[at])
                at += 1
                continue
            dst, sem = bufs[nth], sems.at[nth]
            nth += 1
            if isinstance(kind, int):
                own, other = ins[at], ins[at + 1]
                at += 2
                copy = pltpu.make_async_copy(own, dst, sem)
                start = functools.partial(start_pick, section == kind, own, other, dst, sem)
            else:
                src = ins[at]
                at += 1
                if kind == "image":
                    src = src.at[section]
                copy = pltpu.make_async_copy(src, dst, sem)
                start = copy.start
            slots.append(Slot(dst, copy, start))
            if len(slots) <= early:
                slots[-1].begin()
        ships, at = [], 0
        for i, out in enumerate(outs):
            buf, copies = bufs[n_load + i], []
            if isinstance(out, Halves):
                rows = out.shape[0] // 2
                for half in (1, 0):
                    src = buf.at[half * rows : (half + 1) * rows]
                    copies.append(pltpu.make_async_copy(src, results[at + half], sems.at[n_load + at + half]))
            else:
                copies.append(pltpu.make_async_copy(buf, results[at], sems.at[n_load + at]))
            at += len(copies)
            ships.append(Ship(buf, copies))
        kernel(*slots, *ships, *rest)
        for slot in slots:
            if isinstance(slot, Slot):
                slot.get()
        for ship in ships:
            if not ship.started:
                ship.go()
        for ship in ships:
            for copy in ship.copies:
                copy.wait()

    return pl.pallas_call(
        body,
        name=name,
        out_shape=shapes,
        in_specs=specs,
        out_specs=[ANY] * n_out,
        scratch_shapes=buffers + list(scratch) + [pltpu.SemaphoreType.DMA((n_load + n_out,))],
        compiler_params=room(buffers + list(scratch), most),
        cost_estimate=pl.CostEstimate(flops=0, bytes_accessed=0, transcendentals=0),
    )(*arrays)


def nn(a, b):
    return jnp.dot(a, b, preferred_element_type=F32)


def nt(a, b):
    return lax.dot_general(a, b, (((1,), (1,)), ((), ())), preferred_element_type=F32)


def tn(a, b):
    return lax.dot_general(a, b, (((0,), (0,)), ((), ())), preferred_element_type=F32)


def colsum(v):
    return jnp.sum(v, axis=0, keepdims=True)


def wide(m, n):
    return jnp.concatenate([m] * n, axis=1)


def reader(vec_ref):
    return lambda row, lo, n: vec_ref[row : row + 1, lo : lo + n]


def piece_masks(section, over_z):
    place = lax.axis_index("dp") % 16
    x_bit, y_bit, low, high = place & 1, (place >> 1) & 1, (place >> 2) & 1, place >> 3
    rest = section * 16 + (low * 2 + high if over_z else 0)
    return rest + x_bit * 8 + y_bit * 4, rest + y_bit * 8 + x_bit * 4


def piece_rows(masks, p, rows):
    return pl.multiple_of((p ^ masks[p >> 4]) * rows, 64)


def row_chunks(body, start):
    return lax.fori_loop(0, PIX // 32, lambda i, carry: body(pl.ds(pl.multiple_of(i * 32, 32), 32), carry), start,
                         unroll=True)


def normalized(v):
    cen = v - jnp.mean(v, axis=-1, keepdims=True)
    inv = lax.rsqrt(jnp.mean(cen * cen, axis=-1, keepdims=True) + EPS)
    return cen * inv, inv


def norm_gradient(up, xhat, inv, gain):
    g = up * gain
    return inv * (g - jnp.mean(g, axis=-1, keepdims=True) - xhat * jnp.mean(g * xhat, axis=-1, keepdims=True))


def conv_rows(src_ref, taps_ref, flip, bias, store):
    def row(h, carry):
        accs = [bias] * CANVAS if bias is not None else [None] * CANVAS
        for a in range(KS):
            ks = []
            for e in range(KS):
                t = (KS - 1 - a) * KS + (KS - 1 - e) if flip else a * KS + e
                ks.append(taps_ref[t * GROUPS : (t + 1) * GROUPS, :])
            for w2 in range(CANVAS):
                x = vreg(src_ref, (h + a) * CANVAS + w2)
                for e in range(KS):
                    w = w2 + 3 - e
                    if 0 <= w < CANVAS:
                        term = x * ks[e]
                        accs[w] = term if accs[w] is None else accs[w] + term
        for w in range(CANVAS):
            store(h * CANVAS + w, accs[w])
        return carry

    lax.fori_loop(0, CANVAS, row, 0)


def vreg(ref, index):
    return ref[pl.ds(pl.multiple_of(index * GROUPS, GROUPS), GROUPS), :]


def zero_border(ref):
    zeros = jnp.zeros((3 * CANVAS * GROUPS, LANES), F32)
    ref[0 : 3 * CANVAS * GROUPS, :] = zeros
    ref[(PAD_ROWS - 3 * CANVAS) * GROUPS :, :] = zeros


def lane_group(ref, g, rows=PIX, base=0):
    return ref[pl.ds(base + g, rows, stride=GROUPS), :]


def gn_forward_part(mask, x_ref, vec, taps, gates, win, wo, n1, cin, mix, p, gl, mid, br, mx_ref):
    zero_border(cin.ref)

    def norm_in(r, carry):
        xhat, _ = normalized(x_ref[r, :].astype(F32) * wide(mask[r, :], 4))
        n1.ref[r, :] = (xhat * vec(V_N1G, 0, C) + vec(V_N1S, 0, C)).astype(BF)
        return carry

    row_chunks(norm_in, 0)
    n1.go()
    win_ref = win.get()
    for n in range(4):
        m = nn(n1.ref[...], win_ref[:, n * 256 : (n + 1) * 256]) + vec(V_BIN, n * 256, 256)
        for half in range(2):
            g = 2 * n + half
            v = m[:, half * LANES : (half + 1) * LANES] * mask[...]
            cin.ref[pl.ds(3 * CANVAS * GROUPS + g, PIX, stride=GROUPS), :] = v
            if g == 0:
                p.ref[:, 0:LANES] = v
    cin.go()
    taps_ref = taps.get()
    bias = taps_ref[49 * GROUPS : 50 * GROUPS, :]

    def keep(pixel, acc):
        mx_ref[pl.ds(pl.multiple_of(pixel * GROUPS, GROUPS), GROUPS), :] = acc * (1.0 / 3.0)

    conv_rows(cin.ref, taps_ref, False, bias, keep)
    for g in range(GROUPS):
        mix.ref[:, g * LANES : (g + 1) * LANES] = lane_group(mx_ref, g)
    mix.go()
    gates_ref, wo_ref = gates.get(), wo.get()
    gl.ref[:, 0:128] = (p.ref[:, 0:128] * pltpu.roll(mix.ref[:, 0:128], 64, 1)).astype(BF)
    p1 = nn(gl.ref[:, 0:128], gates_ref[256:384, 256:384]) + vec(V_B1, 0, 128)
    p.ref[:, 128:256] = p1
    gl.ref[:, 128:256] = (p1 * mix.ref[:, 128:256]).astype(BF)
    p2 = nn(gl.ref[:, 128:256], gates_ref[256:384, 0:256]) + vec(V_B2, 0, 256)
    p.ref[:, 256:512] = p2
    gl.ref[:, 256:512] = (p2 * mix.ref[:, 256:512]).astype(BF)
    for n in range(2):
        c = 256 * n
        p3 = nn(gl.ref[:, 256:512], gates_ref[0:256, c : c + 256]) + vec(V_B3, c, 256)
        p.ref[:, 512 + c : 768 + c] = p3
        gl.ref[:, 512 + c : 768 + c] = (p3 * mix.ref[:, 512 + c : 768 + c]).astype(BF)
    p.go()
    gl.go()
    for n in range(2):
        c = 256 * n
        b = nn(gl.ref[:, 512:1024], wo_ref[:, c : c + 256]) + vec(V_BO, c, 256)
        br.ref[:, c : c + 256] = b.astype(BF)
        start = x_ref[:, c : c + 256].astype(F32) * wide(mask[...], 2)
        mid.ref[:, c : c + 256] = start + vec(V_BS, c, 256) * b
    br.go()
    if isinstance(mid, Ship):
        mid.go()


def mlp_forward_part(mask, mid_ref, vec, we, wr, n2_ref, act_ref, slope_ref, out_ref, res_ref):
    def norm_mid(r, carry):
        xhat, _ = normalized(mid_ref[r, :])
        n2_ref[r, :] = (xhat * vec(V_N2G, 0, C) + vec(V_N2S, 0, C)).astype(BF)
        return carry

    row_chunks(norm_mid, 0)
    we_ref = we.get()
    for j in range(8):
        c = 256 * j
        pre = nn(n2_ref[...], we_ref[:, c : c + 256]) + vec(V_BE, c, 256)
        cum = 0.5 * (1.0 + lax.erf(pre * 0.7071067811865476))
        act_ref[:, c : c + 256] = (pre * cum).astype(BF)
        slope = cum + pre * jnp.exp(-0.5 * pre * pre) * 0.3989422804014327
        slope_ref[:, c : c + 256] = slope.astype(BF)
    wr_ref = wr.get()
    for n in range(2):
        c = 256 * n
        out = nn(act_ref[...], wr_ref[:, c : c + 256]) + vec(V_BR, c, 256)
        out_ref[:, c : c + 256] = out.astype(BF)
        res = wide(mask[...], 2) * (mid_ref[:, c : c + 256] + vec(V_MS, c, 256) * out)
        res_ref[:, c : c + 256] = res.astype(BF)


def mlp_back_part(mask, masks, dy_ref, vec, n2_ref, act_ref, slope_ref, out_ref, mid_ref, we, wr,
                  dmid, mvec, bucket, dout_ref, dpre_ref, dn2_ref):
    mvec.ref[...] = jnp.zeros_like(mvec.ref)
    for n in range(2):
        c = 256 * n
        dyr = dy_ref[:, c : c + 256].astype(F32) * wide(mask[...], 2)
        dmid.ref[:, c : c + 256] = dyr
        dout = (vec(V_MS, c, 256) * dyr).astype(BF)
        dout_ref[:, c : c + 256] = dout
        mvec.ref[3:4, c : c + 256] = colsum(dout.astype(F32))
        mvec.ref[4:5, c : c + 256] = colsum(dyr * out_ref[:, c : c + 256].astype(F32))
    wr_ref = wr.get()
    for j in range(8):
        c = 256 * j
        dw = tn(act_ref[:, c : c + 256], dout_ref[...]).astype(BF)
        for q in range(4):
            bucket.ref[pl.ds(piece_rows(masks, 4 * j + q, 128), 64), :] = dw[64 * q : 64 * q + 64, :]
        dact = nt(dout_ref[...], wr_ref[c : c + 256, :])
        dpre = (dact * slope_ref[:, c : c + 256].astype(F32)).astype(BF)
        dpre_ref[:, c : c + 256] = dpre
        mvec.ref[2:3, c : c + 256] = colsum(dpre.astype(F32))
    we_ref = we.get()
    for cb in range(4):
        dw = tn(n2_ref[...], dpre_ref[:, 512 * cb : 512 * cb + 512]).astype(BF)
        for q in range(8):
            rows = pl.multiple_of(piece_rows(masks, 8 * cb + q, 128) + 64, 64)
            bucket.ref[pl.ds(rows, 64), :] = dw[64 * q : 64 * q + 64, :]
    bucket.go()
    for n in range(2):
        c = 256 * n
        dn2_ref[:, c : c + 256] = nt(dpre_ref[...], we_ref[c : c + 256, :])

    def norm_back(r, carry):
        dgain, dshift = carry
        xhat, inv = normalized(mid_ref[r, :])
        up = dn2_ref[r, :]
        dmid.ref[r, :] = dmid.ref[r, :] + norm_gradient(up, xhat, inv, vec(V_N2G, 0, C))
        return dgain + colsum(up * xhat), dshift + colsum(up)

    zero = jnp.zeros((1, C), F32)
    dgain, dshift = row_chunks(norm_back, (zero, zero))
    mvec.ref[0:1, 0:C] = dgain
    mvec.ref[1:2, 0:C] = dshift


def pack_kernel(*refs):
    vectors, taps_in, w1, w2, w3, crop_ref = refs[:14], refs[14], refs[15], refs[16], refs[17], refs[18]
    vec_ref, taps_ref, gates_ref, mask_ref = refs[19:]
    crops = crop_ref[...]
    kind = jnp.where(lax.axis_index("section") == 0, crops[:, 0:1], crops[:, 1:2])
    side = jnp.where(kind == 0, SIDE_S, jnp.where(kind == 1, SIDE_M, CANVAS))
    r = lax.broadcasted_iota(jnp.int32, (PIX, LANES), 0)
    inside = ((r // CANVAS) < side) & ((r % CANVAS) < side)
    mask_ref[...] = inside.astype(F32)
    gates_ref[0:256, :] = w3[...]
    gates_ref[256:384, 0:256] = w2[...]
    gates_ref[256:384, 256:384] = jnp.concatenate([w1[...], jnp.zeros((64, 128), BF)], axis=0)
    gates_ref[256:384, 384:512] = jnp.zeros((128, 128), BF)
    vec_ref[...] = jnp.zeros_like(vec_ref)
    for row, ref in enumerate(vectors):
        n = ref.shape[1]
        vec_ref[row : row + 1, 0:n] = ref[...].astype(F32)
    taps = taps_in[...].astype(F32)
    bias = vectors[V_CB][...].astype(F32)
    for g in range(GROUPS):
        if g == 0:
            t = jnp.concatenate([jnp.zeros((49, 64), F32), taps[:, 0:64]], axis=1)
            b = jnp.concatenate([jnp.zeros((1, 64), F32), bias[:, 0:64]], axis=1)
        else:
            t = taps[:, g * LANES - 64 : g * LANES + 64]
            b = bias[:, g * LANES - 64 : g * LANES + 64]
        taps_ref[pl.ds(g, 49, stride=GROUPS), :] = t
        taps_ref[49 * GROUPS + g : 49 * GROUPS + g + 1, :] = b


def gn_forward_kernel(mask, x, vec, win, taps, gates, wo, n1, cin, mix, p, gl, mid, br, mx_ref):
    x_ref = x.get()
    gn_forward_part(mask.get(), x_ref, reader(vec.get()), taps, gates, win, wo, n1, cin, mix, p, gl, mid, br, mx_ref)


def middle_kernel(mask, mid0, vec0, we0, wr0, vec1, win, taps, gates, wo, we1, wr1, dy,
                  hidden, n2, act, slope, out, n1, cin, mix, p, gl, br, final, swap, dmid, mvec, bucket,
                  mx_ref, mid1, n2_1, act1, slope1, out1, dout_ref, dpre_ref, dn2_ref):
    section = lax.axis_index("section")
    masks = piece_masks(section, True)
    mask = mask.get()
    mid0_ref = mid0.get()
    vec0_ref = vec0.get()
    wr0.begin()
    for slot in (vec1, win, taps, gates, wo, we1, wr1, dy):
        slot.begin()
    mlp_forward_part(mask, mid0_ref, reader(vec0_ref), we0, wr0, n2.ref, act.ref, slope.ref, out.ref, hidden.ref)
    for ship in (hidden, n2, act, slope, out):
        ship.go()
    vec = reader(vec1.get())
    gn_forward_part(mask, hidden.ref, vec, taps, gates, win, wo, n1, cin, mix, p, gl, Slot(mid1, None), br, mx_ref)
    mlp_forward_part(mask, mid1, vec, we1, wr1, n2_1, act1, slope1, out1, final.ref)
    final.go()
    swap.ref[...] = jnp.where(section == 0, final.ref[...], hidden.ref[...])
    swap.go()
    mlp_back_part(mask, masks, dy.get(), vec, n2_1, act1, slope1, out1, mid1, we1, wr1,
                  dmid, mvec, bucket, dout_ref, dpre_ref, dn2_ref)


def mlp_back_kernel(mask, dy, vec, n2, act, slope, out, mid, wr, we, dmid, mvec, bucket,
                    dout_ref, dpre_ref, dn2_ref):
    mlp_back_part(mask.get(), piece_masks(lax.axis_index("section"), True), dy.get(), reader(vec.get()), n2.get(), act.get(), slope.get(), out.get(),
                  mid.get(), we, wr, dmid, mvec, bucket, dout_ref, dpre_ref, dn2_ref)


def gn_back_kernel(block, mask, dmid, br, vec, wo, mix, p, gates, mvec, taps, win, x, *rest):
    if block == 0:
        following, dv, swap, dbr, dp, dmg, dcp, gvec = rest[:8]
    else:
        dv, dvb, dbr, dp, dmg, dcp, gvec = rest[:7]
    dg_ref, dmix_ref, ds_ref, dn1_ref = rest[-4:]
    section = lax.axis_index("section")
    mask = mask.get()
    zero_border(dcp.ref)
    dmid_ref, br_ref = dmid.get(), br.get()
    vec = reader(vec.get())
    dbs, dbo = [], []
    for n in range(2):
        c = 256 * n
        dm = dmid_ref[:, c : c + 256]
        dbs.append(colsum(dm * br_ref[:, c : c + 256].astype(F32)))
        d = (vec(V_BS, c, 256) * dm).astype(BF)
        dbr.ref[:, c : c + 256] = d
        dbo.append(colsum(d.astype(F32)))
    dbr.go()
    wo_ref, mix_ref, p_ref = wo.get(), mix.get(), p.get()
    db3 = []
    for n in range(2):
        c = 256 * n
        dg = nt(dbr.ref[...], wo_ref[c : c + 256, :])
        d = (dg * mix_ref[:, 512 + c : 768 + c]).astype(BF)
        dmix_ref[:, 512 + c : 768 + c] = dg * p_ref[:, 512 + c : 768 + c] * (1.0 / 3.0)
        dp.ref[:, 512 + c : 768 + c] = d
        db3.append(colsum(d.astype(F32)))
    gates_ref = gates.get()
    dg = nt(dp.ref[:, 512:1024], gates_ref[0:256, :])
    d = (dg * mix_ref[:, 256:512]).astype(BF)
    dmix_ref[:, 256:512] = dg * p_ref[:, 256:512] * (1.0 / 3.0)
    dp.ref[:, 256:512] = d
    db2 = colsum(d.astype(F32))
    dg = nt(dp.ref[:, 256:512], gates_ref[256:384, 0:256])
    d = (dg * mix_ref[:, 128:256]).astype(BF)
    dmix_ref[:, 128:256] = dg * p_ref[:, 128:256] * (1.0 / 3.0)
    dp.ref[:, 128:256] = d
    db1 = colsum(d.astype(F32))
    dg = nt(dp.ref[:, 128:256], gates_ref[256:384, 256:384])
    dmix_ref[:, 0:128] = pltpu.roll(dg * p_ref[:, 0:128], 64, 1) * (1.0 / 3.0)
    dg_ref[...] = dg * pltpu.roll(mix_ref[:, 0:128], 64, 1)
    dp.ref[:, 0:128] = jnp.zeros((PIX, LANES), BF)
    dp.go()
    for g in range(GROUPS):
        dcp.ref[pl.ds(3 * CANVAS * GROUPS + g, PIX, stride=GROUPS), :] = dmix_ref[:, g * LANES : (g + 1) * LANES]
    dcp.go()

    def keep(pixel, acc):
        ds_ref[pl.ds(pl.multiple_of(pixel * GROUPS, GROUPS), GROUPS), :] = acc

    conv_rows(dcp.ref, taps.get(), True, None, keep)
    dbin = []
    for g in range(GROUPS):
        d = lane_group(ds_ref, g) * mask[...]
        if g == 0:
            d = d + dg_ref[...]
        d = d.astype(BF)
        dmg.ref[:, g * LANES : (g + 1) * LANES] = d
        dbin.append(colsum(d.astype(F32)))
    dmg.go()
    win_ref, x_ref = win.get(), x.get()
    next_ref = following.get() if block == 0 else None
    for n in range(2):
        c = 256 * n
        dn1_ref[:, c : c + 256] = nt(dmg.ref[...], win_ref[c : c + 256, :])

    def norm_back(r, carry):
        dgain, dshift = carry
        m = wide(mask[r, :], 4)
        xhat, inv = normalized(x_ref[r, :].astype(F32) * m)
        up = dn1_ref[r, :]
        d = m * (dmid_ref[r, :] + norm_gradient(up, xhat, inv, vec(V_N1G, 0, C)))
        dv.ref[r, :] = d
        if block == 0:
            swap.ref[r, :] = jnp.where(section == 0, next_ref[r, :], d)
        else:
            dvb.ref[r, :] = d.astype(BF)
        return dgain + colsum(up * xhat), dshift + colsum(up)

    zero = jnp.zeros((1, C), F32)
    dgain, dshift = row_chunks(norm_back, (zero, zero))
    z = jnp.zeros((1, LANES), F32)
    mvec_ref = mvec.get()
    rows = [
        dgain,
        dshift,
        jnp.concatenate(dbin[0:4], axis=1),
        jnp.concatenate(dbin[4:8], axis=1),
        jnp.concatenate([db1, z, z, z], axis=1),
        jnp.concatenate([db2, z, z], axis=1),
        jnp.concatenate(db3, axis=1),
        jnp.concatenate(dbo, axis=1),
        jnp.concatenate(dbs, axis=1),
        mvec_ref[0:1, 0:C],
        mvec_ref[1:2, 0:C],
        mvec_ref[2:3, 0:512],
        mvec_ref[2:3, 512:1024],
        mvec_ref[2:3, 1024:1536],
        mvec_ref[2:3, 1536:2048],
        mvec_ref[3:4, 0:C],
        mvec_ref[4:5, 0:C],
    ]
    rows.append(jnp.zeros((32 - len(rows), C), F32))
    gvec.ref[...] = jnp.concatenate(rows, axis=0).astype(BF)


def gn_weights_kernel(n1, dmg, gl, dbr, dp, gvec, cin, dcp, bucket, dk_ref):
    masks = piece_masks(lax.axis_index("section"), False)

    def put(p, val, sub=0):
        n = val.shape[0]
        bucket.ref[pl.ds(pl.multiple_of(piece_rows(masks, p, 64) + sub, 16), n), :] = val

    n1_ref, dmg_ref = n1.get(), dmg.get()
    for cb in range(2):
        dw = tn(n1_ref[...], dmg_ref[:, 512 * cb : 512 * cb + 512]).astype(BF)
        for q in range(8):
            put(8 * cb + q, dw[64 * q : 64 * q + 64, :])
    gl_ref, dbr_ref, dp_ref = gl.get(), dbr.get(), dp.get()
    dw = tn(gl_ref[:, 512:1024], dbr_ref[...]).astype(BF)
    for q in range(8):
        put(16 + q, dw[64 * q : 64 * q + 64, :])
    dw = tn(gl_ref[:, 256:512], dp_ref[:, 512:1024]).astype(BF)
    for q in range(4):
        put(24 + q, dw[64 * q : 64 * q + 64, :])
    dw = tn(gl_ref[:, 128:256], dp_ref[:, 256:512]).astype(BF)
    put(28, jnp.concatenate([dw[0:64, :], dw[64:128, :]], axis=1))
    dw1 = tn(gl_ref[:, 0:128], dp_ref[:, 128:256]).astype(BF)
    put(31, jnp.concatenate([dw1[16 * i : 16 * i + 16, :] for i in range(4)], axis=1))
    put(31, jnp.zeros((16, 512), BF), 16)
    put(31, gvec.get()[...], 32)
    cin_ref, dcp_ref = cin.get(), dcp.get()
    dk_ref[...] = jnp.zeros_like(dk_ref)
    for taps in ((0, 1), (2, 3), (4, 5), (6,)):

        def row(h, accs):
            accs = list(accs)
            ds = [vreg(dcp_ref, (h + 3) * CANVAS + w) for w in range(CANVAS)]
            for i, a in enumerate(taps):
                for w2 in range(CANVAS):
                    x = vreg(cin_ref, (h + a) * CANVAS + w2)
                    for e in range(KS):
                        w = w2 + 3 - e
                        if 0 <= w < CANVAS:
                            accs[i * KS + e] = accs[i * KS + e] + x * ds[w]
            if len(taps) == 1:
                for w in range(CANVAS):
                    accs[KS] = accs[KS] + ds[w]
            return tuple(accs)

        count = len(taps) * KS + (1 if len(taps) == 1 else 0)
        accs = lax.fori_loop(0, CANVAS, row, tuple(jnp.zeros((GROUPS, LANES), F32) for _ in range(count)))
        for i in range(count):
            t = taps[0] * KS + i
            dk_ref[t * GROUPS : (t + 1) * GROUPS, :] = accs[i]
    for half in range(2):
        put(29 + half, jnp.concatenate([lane_group(dk_ref, 4 * half + i, 64) for i in range(4)], axis=1).astype(BF))


def start_half(far, rows, sources, buf, sems, over_z):
    section = lax.axis_index("section")
    half = 1 - section if far else section
    masks = piece_masks(section, over_z)
    mask = jnp.where(half == 0, masks[0], masks[1]) & 15
    for p in range(16):
        off = pl.multiple_of((p ^ mask) * rows, 64)
        dst = buf.at[p * rows : (p + 1) * rows]
        for sec in range(2):

            @pl.when(section == sec)
            def _():
                pltpu.make_async_copy(sources[sec].at[pl.ds(off, rows)], dst, sems.at[p // 4]).start()

    return half


def wait_quarter(i, rows, sources, buf, sems):
    part = buf.at[pl.ds(i * 4 * rows, 4 * rows)]
    pltpu.make_async_copy(sources[0].at[pl.ds(0, 4 * rows)], part, sems.at[i]).wait()


def mlp_finish_kernel(far, *refs):
    sources = refs[:2]
    wr_any, we_any, buf, wr_ref, we_ref, sems, out_sems = refs[-7:]
    half = start_half(far, 128, sources, buf, sems, True)
    copies = []
    for i in range(4):
        wait_quarter(i, 128, sources, buf, sems)
        cb = i // 2
        for q in range(4):
            p = 4 * i + q
            r = p % 8
            wr_ref[64 * p : 64 * p + 64, :] = buf[128 * p : 128 * p + 64, :].astype(F32)
            we_ref[64 * r : 64 * r + 64, 512 * cb : 512 * cb + 512] = buf[128 * p + 64 : 128 * p + 128, :].astype(F32)
        rows = pl.ds(pl.multiple_of(half * 1024 + 256 * i, 256), 256)
        copies.append(pltpu.make_async_copy(wr_ref.at[256 * i : 256 * i + 256], wr_any.at[rows], out_sems.at[i]))
        part = slice(256 * (i % 2), 256 * (i % 2) + 256)
        cols = pl.ds(pl.multiple_of(half * 1024 + 512 * cb, 512), 512)
        src = we_ref.at[part, 512 * cb : 512 * cb + 512]
        copies.append(pltpu.make_async_copy(src, we_any.at[part, cols], out_sems.at[4 + i]))
        copies[-2].start()
        copies[-1].start()
    for copy in copies:
        copy.wait()


def gn_finish_kernel(far, *refs):
    sources = refs[:2]
    count = len(GN_OUTS)
    results, buf, vals, sems, out_sems = refs[-2 * count - 3 : -count - 3], refs[-count - 3], refs[-count - 2 : -2], refs[-2], refs[-1]
    (n1g, n1s, win, bin_, conv, cbias, w1, b1, w2, b2, w3, b3, wo, bo, bs, n2g, n2s, be, br, ms) = vals
    half = start_half(far, 64, sources, buf, sems, False)
    for i in range(4):
        wait_quarter(i, 64, sources, buf, sems)

    def out(i):
        return pltpu.make_async_copy(vals[i], results[i], out_sems.at[i])

    @pl.when(half == 0)
    def _():
        for cb in range(2):
            win[:, 512 * cb : 512 * cb + 512] = buf[512 * cb : 512 * cb + 512, :].astype(F32)
        out(2).start()
        out(2).wait()

    @pl.when(half == 1)
    def _():
        wo[...] = buf[0:512, :].astype(F32)
        out(12).start()
        w3[...] = buf[512:768, :].astype(F32)
        out(10).start()
        for i in range(2):
            w2[64 * i : 64 * i + 64, :] = buf[768:832, 256 * i : 256 * i + 256].astype(F32)
        for i in range(4):
            w1[16 * i : 16 * i + 16, :] = buf[960:976, 128 * i : 128 * i + 128].astype(F32)
        taps = jnp.concatenate([buf[832:896, :], buf[896:960, :]], axis=1).astype(F32)
        for i in range(49):
            conv[i] = taps[i : i + 1, 64:1024]
        cbias[...] = taps[49:50, 64:1024]
        v = buf[992:1024, :].astype(F32)
        n1g[...] = v[0:1]
        n1s[...] = v[1:2]
        bin_[:, 0:512] = v[2:3]
        bin_[:, 512:1024] = v[3:4]
        b1[...] = v[4:5, 0:128]
        b2[...] = v[5:6, 0:256]
        b3[...] = v[6:7]
        bo[...] = v[7:8]
        bs[...] = v[8:9]
        n2g[...] = v[9:10]
        n2s[...] = v[10:11]
        for i in range(4):
            be[:, 512 * i : 512 * i + 512] = v[11 + i : 12 + i]
        br[...] = v[15:16]
        ms[...] = v[16:17]
        rest = [i for i in range(count) if i not in (2, 10, 12)]
        for i in rest:
            out(i).start()
        for i in rest + [10, 12]:
            out(i).wait()


def place_kernel(first, second, got, out):
    section = lax.axis_index("section")

    @pl.when(section == 0)
    def _():
        out[0] = first[...]
        out[1] = got[...]

    @pl.when(section != 0)
    def _():
        out[0] = got[...]
        out[1] = second[...]


VM = pl.BlockSpec(memory_space=pltpu.VMEM)


def plain_call(kernel, name, operands, outs, scratch, most=False, aliases={}):
    return pl.pallas_call(
        kernel,
        name=name,
        out_shape=[shape for _, shape in outs],
        in_specs=[spec for spec, _ in operands],
        out_specs=[spec for spec, _ in outs],
        scratch_shapes=scratch,
        compiler_params=room([a for spec, a in operands + outs if spec is VM] + scratch, most),
        input_output_aliases=aliases,
        cost_estimate=pl.CostEstimate(flops=0, bytes_accessed=0, transcendentals=0),
    )(*[array for _, array in operands])


def on(spec, *arrays):
    return [(spec, a) for a in arrays]


PIXEL_CHANNELS = vmem(PIX * GROUPS, LANES, F32)
FIELD_F32, FIELD_BF = sds((PIX, C), F32), sds((PIX, C), BF)
CONV_F32 = sds((PAD_ROWS * GROUPS, LANES), F32)
WIDE_F32, WIDE_BF = sds((PIX, 1024), F32), sds((PIX, 1024), BF)
HIDE_BF = sds((PIX, FF), BF)
GN_SAVED = [FIELD_BF, CONV_F32, WIDE_F32, WIDE_F32, WIDE_BF]


def run_pack(vectors, taps, gates, crop):
    outs = on(VM, sds((VEC_ROWS, FF), F32), sds((50 * GROUPS, LANES), F32), sds((384, 512), BF), sds((PIX, LANES), F32))
    return plain_call(pack_kernel, "pack", on(VM, *vectors, taps, *gates, crop), outs, [], True)


def run_gn_forward(mask, images, w):
    operands = [load(mask), image(images)] + [pick(0, w[k]) for k in ("vec", "win", "taps", "gates", "wo")]
    return call(gn_forward_kernel, "gnconv_forward", operands, GN_SAVED + [FIELD_F32, FIELD_BF],
                [PIXEL_CHANNELS], True)


def run_middle(mask, mid, cotangent, w):
    operands = [load(mask), load(mid)] + [pick(0, w[k]) for k in ("vec", "we", "wr")]
    operands += [pick(1, w[k]) for k in ("vec", "win", "taps", "gates", "wo", "we", "wr")] + [image(cotangent)]
    outs = [FIELD_BF, FIELD_BF, HIDE_BF, HIDE_BF, FIELD_BF] + GN_SAVED + [FIELD_BF, FIELD_BF, FIELD_BF, FIELD_F32]
    outs += [sds((8, FF), F32), Halves(4096)]
    scratch = [PIXEL_CHANNELS, vmem(PIX, C, F32), vmem(PIX, C, BF), vmem(PIX, FF, BF), vmem(PIX, FF, BF),
               vmem(PIX, C, BF), vmem(PIX, C, BF), vmem(PIX, FF, BF), vmem(PIX, C, F32)]
    return call(middle_kernel, "middle", operands, outs, scratch, True, 4)


def run_mlp_back(mask, dy, n2, act, slope, out, mid, w):
    operands = [load(mask), near(dy), pick(0, w["vec"]), load(n2), load(act), load(slope), load(out), load(mid),
                pick(0, w["wr"]), pick(0, w["we"])]
    outs = [FIELD_F32, sds((8, FF), F32), Halves(4096)]
    scratch = [vmem(PIX, C, BF), vmem(PIX, FF, BF), vmem(PIX, C, F32)]
    return call(mlp_back_kernel, "mlp_backward", operands, outs, scratch, True)


def run_gn_back(block, mask, x, following, dmid, mvec, mix, p, br, w):
    far = load if block == 1 else near
    operands = [load(mask), far(dmid), load(br), pick(block, w["vec"]), pick(block, w["wo"]), load(mix), load(p),
                pick(block, w["gates"]), far(mvec), pick(block, w["taps"]), pick(block, w["win"])]
    operands += [image(x), near(following)] if block == 0 else [load(x)]
    outs = [FIELD_F32, FIELD_F32 if block == 0 else FIELD_BF, FIELD_BF, WIDE_BF, WIDE_BF, CONV_F32, sds((32, 512), BF)]
    scratch = [vmem(PIX, LANES, F32), vmem(PIX, 1024, F32), PIXEL_CHANNELS, vmem(PIX, C, F32)]
    return call(functools.partial(gn_back_kernel, block), "gnconv_backward", operands, outs, scratch, block == 1)


def run_gn_weights(block, n1, dmg, gl, dbr, dp, gvec, cin, dcp):
    operands = [load(n1), near(dmg), load(gl), near(dbr), near(dp), near(gvec), load(cin), near(dcp)]
    return call(gn_weights_kernel, "gnconv_weights", operands, [Halves(2048)], [vmem(64 * GROUPS, LANES, F32)],
                block == 1)


def turn_kernel(token, out):
    out[...] = jnp.zeros_like(out)


def run_turn(token):
    return plain_call(turn_kernel, "turn", on(ANY, token), on(VM, sds((8, LANES), F32)), [])[0]


def run_mlp_finish(far, sources, earlier=()):
    outs = on(ANY, sds((FF, C), F32), sds((C, FF), F32))
    scratch = [vmem(2048, 512, BF), vmem(1024, C, F32), vmem(C, 1024, F32), pltpu.SemaphoreType.DMA((4,)),
               pltpu.SemaphoreType.DMA((8,))]
    return plain_call(functools.partial(mlp_finish_kernel, far), "mlp_finish", on(ANY, *sources, *earlier), outs, scratch,
                      True, {2: 0, 3: 1} if far else {})


GN_OUTS = [sds((1, w) if isinstance(w, int) else w, F32) for w in (
    512, 512, (512, 1024), 1024, (49, 1, 960), 960, (64, 128), 128, (128, 256), 256, (256, 512), 512, (512, 512), 512,
    512, 512, 512, 2048, 512, 512)]


def run_gn_finish(far, sources, earlier=()):
    scratch = [vmem(1024, 512, BF)] + [pltpu.VMEM(o.shape, F32) for o in GN_OUTS]
    scratch += [pltpu.SemaphoreType.DMA((4,)), pltpu.SemaphoreType.DMA((len(GN_OUTS),))]
    return plain_call(functools.partial(gn_finish_kernel, far), "gn_finish", on(ANY, *sources, *earlier),
                      on(ANY, *GN_OUTS), scratch, True, {2 + i: i for i in range(len(GN_OUTS))} if far else {})


def run_place(first, second, got):
    outs = on(VM, sds((2, PIX, C), first.dtype))
    return plain_call(place_kernel, "place", on(VM, first, second, got), outs, [])[0]


AXES = ("section", "dp")
X_BIT, Y_BIT, Z_LOW, Z_HIGH = 1, 2, 4, 8

FIRST, SECOND, LOW, HIGH = (X_BIT, Y_BIT), (Y_BIT, X_BIT), (Z_LOW, Z_LOW), (Z_HIGH, Z_HIGH)

BUCKETS = ("m1", "g1", "m0", "g0")
STEPS = ("core", "x1", "x2", "zl", "zh", "fl", "fh", "ZH", "ZL", "X2", "X1", "Core")
OTHERS = ("fo", "go")
KERNELS = ("K1", "K2", "K3", "K4", "K5", "MF1", "MF2", "GF1", "GF2", "P1", "P2")

ORDER = (
    1, -1, 2, 60, 62, -2, 3, 25, 61, -25, 26, -3, 4, 13, 63, 50, -4, 5, -26, 27, 64, -13, 14, -27, 28, -5, 8, 49, 37,
    -37, 38, -28, 29, -8, 9, -29, 32, -14, 15, -38, 39, -32, 33, -9, 10, -15, 18, -39, 42, -33, 34, -49, 69, -42, 43,
    -10, 11, -18, 19, -34, 35, -43, 46, -46, 47, -50, 70, -11, 12, -19, 22, -35, -47, 48, -22, 23, 36, -12, 65, -36,
    66, -48, -23, 24, 67, -24, 68,
)


def event_name(number):
    at = abs(number) - 1
    if at >= 59:
        return KERNELS[at - 59]
    sign = "+" if number > 0 else "-"
    return sign + (OTHERS[at - 48] if at >= 48 else BUCKETS[at // 12] + "." + STEPS[at % 12])


GROUPED = (("m1", ("m1",)), ("m0", ("m0",)), ("g1", ("g1",)), ("g0", ("g0",)))


def after(x, *others):
    return lax.optimization_barrier((x,) + others)[0]


class Flow:
    def __init__(self, count):
        self.count = count
        self.token = None
        self.flying = {}

    def exchange(self, x, flips=None, only=None):
        n = self.count
        other, bits = (1, (0, 0)) if flips is None else (0, flips)
        pairs = [
            (s * n + d, (s ^ other) * n + (d ^ bits[s])) for s in range(2) for d in range(n) if only is None or s == only
        ]
        return lax.ppermute(x, AXES, pairs)

    def start(self, name, x, flips=None, only=None):
        with jax.named_scope("transfer_" + name.replace(".", "_")):
            self.flying[name] = self.exchange(after(x, self.token), flips, only)

    def end(self, name):
        got, token = lax.optimization_barrier((self.flying.pop(name), self.token))
        self.token = run_turn(token)
        return got

    def tie(self, x):
        return after(x, self.token)


VECTORS = (0, 1, 3, 5, 7, 9, 11, 13, 14, 15, 16, 18, 20, 21)


def on_device(flow, images, cotangent, crop, *stacked):
    images = images.reshape(2, PIX, C)
    cotangent = cotangent.reshape(2, PIX, C)
    win, wo, we, wr = [stacked[i][0] for i in (2, 12, 17, 19)]
    vec, taps, gates, mask = run_pack(
        [stacked[i] for i in VECTORS], stacked[4][0], [stacked[i][0] for i in (6, 8, 10)], crop.reshape(1, 2)
    )
    swap = flow.exchange
    win_other, wo_other = swap(win), swap(wo)
    taps_other, vec_other, gates_other = swap(taps), swap(vec), swap(gates)
    we, wr = after((we, wr), win_other, wo_other, taps_other, vec_other, gates_other)
    we_other, wr_other = swap(we), swap(wr)
    w = {
        "win": (win, win_other), "wo": (wo, wo_other), "we": (we, we_other), "wr": (wr, wr_other),
        "vec": (vec, vec_other), "taps": (taps, taps_other), "gates": (gates, gates_other),
    }

    n1_0, cin_0, mix_0, p_0, gl_0, mid_0, br_0 = run_gn_forward(mask, images, w)
    (hidden, n2_0, act_0, slope_0, out_0, n1_1, cin_1, mix_1, p_1, gl_1, br_1, final, field_swap, dmid_1, mvec_1,
     keep, send) = run_middle(mask, mid_0, cotangent, w)
    flow.token = mvec_1
    value = {"m1.core": (keep, send)}
    chips = flow.count // 16

    def sum_all(total):
        if chips > 1:
            groups = [[g * 16 + r for g in range(chips)] for r in range(16)]
            total = lax.psum(total, "dp", axis_index_groups=groups)
        return total

    def begin(name):
        bucket, step = name.split(".")
        only = {"m1": 0, "g1": 0, "m0": 1, "g0": 1}.get(bucket)
        flips = {"x1": FIRST, "x2": SECOND, "zl": LOW, "zh": HIGH, "fl": LOW, "fh": HIGH}.get(step.lower())
        whole = step.isupper() or step in ("Core", "fl", "fh")
        flow.start(name, value[name] if whole else value[name][1], flips, only if step == "Core" else None)

    def finish(name):
        bucket, step = name.split(".")
        got = flow.end(name)
        mine = value[name]
        after_step = {"core": "x1", "x1": "x2", "x2": "zl" if bucket[0] == "m" else "fl", "zl": "zh", "fl": "fh",
                      "ZH": "ZL", "ZL": "X2", "X2": "X1", "X1": "Core"}
        if step == "Core":
            value[bucket] = (mine, got)
            return
        if step.isupper():
            total = jnp.stack([mine, got])
            value[bucket + "." + after_step[step]] = total.reshape(-1, 512) if step == "X1" else total
            return
        if step in ("fl", "fh"):
            total = mine + got
        else:
            mine = mine[0]
            if step == "core":
                shape = (2, 2, 2, 2, mine.shape[0] // 16, 512)
                mine, got = mine.reshape(shape), got.reshape(shape)
            if step in ("core", "x1", "zl"):
                total = (mine[0] + got[0], mine[1] + got[1])
            else:
                total = mine + got
        if step == "x2" and bucket[0] == "m":
            total = (total[0], total[1])
        if step in ("zh", "fh"):
            total = sum_all(total)
            for group, members in GROUPED:
                if bucket in members:
                    value["sum of " + bucket] = total
                    sums = [value.get("sum of " + m) for m in members]
                    if all(v is not None for v in sums):
                        value[group + (".ZH" if step == "zh" else ".X2")] = jnp.concatenate(sums, axis=-2)
        else:
            value[bucket + "." + after_step[step]] = total

    for event in map(event_name, ORDER):
        if event in ("+fo", "+go"):
            flow.start(event[1:], field_swap if event == "+fo" else grad_swap)
        elif event in ("-fo", "-go"):
            value[event[1:]] = flow.end(event[1:])
        elif event[0] == "+":
            begin(event[1:])
        elif event[0] == "-":
            finish(event[1:])
        elif event == "K1":
            back = run_gn_back(1, mask, hidden, None, flow.tie(dmid_1), mvec_1, mix_1, p_1, br_1, w)
            dv_1, dvb, dbr_1, dp_1, dmg_1, dcp_1, gvec_1 = back
            flow.token = gvec_1
        elif event == "K2":
            value["g1.core"] = run_gn_weights(1, n1_1, dmg_1, gl_1, dbr_1, dp_1, flow.tie(gvec_1), cin_1, dcp_1)
            flow.token = value["g1.core"][0]
        elif event == "K3":
            dmid_0, mvec_0, *value["m0.core"] = run_mlp_back(mask, flow.tie(dvb), n2_0, act_0, slope_0, out_0, mid_0, w)
            flow.token = mvec_0
        elif event == "K4":
            back = run_gn_back(0, mask, images, dv_1, flow.tie(dmid_0), mvec_0, mix_0, p_0, br_0, w)
            dv_0, grad_swap, dbr_0, dp_0, dmg_0, dcp_0, gvec_0 = back
            flow.token = gvec_0
        elif event == "K5":
            value["g0.core"] = run_gn_weights(0, n1_0, dmg_0, gl_0, dbr_0, dp_0, flow.tie(gvec_0), cin_0, dcp_0)
            flow.token = value["g0.core"][0]
        elif event == "P1":
            flow.token = block_outputs = run_place(hidden, final, flow.tie(value["fo"]))
        elif event == "P2":
            flow.token = input_grads = run_place(dv_0, dv_1, flow.tie(value["go"]))
        elif event in ("MF1", "MF2"):
            far = event == "MF2"
            one, two = (value[b][1] if far else value[b + ".Core"] for b in ("m0", "m1"))
            wr, we = mlp_grads = run_mlp_finish(far, (flow.tie(one), two), mlp_grads if far else ())
            flow.token = wr
        elif event in ("GF1", "GF2"):
            far = event == "GF2"
            one, two = (value[b][1] if far else value[b + ".Core"] for b in ("g0", "g1"))
            grads = run_gn_finish(far, (flow.tie(one), two), grads if far else ())
            flow.token = grads[0]
    (n1g, n1s, win, bin_, conv, cbias, w1, b1, w2, b2, w3, b3, wo, bo, bs, n2g, n2s, be, br, ms) = grads
    shape = (1, 2, 1, CANVAS, CANVAS, C)
    return (
        block_outputs.reshape(shape), input_grads.reshape(shape), n1g, n1s, win[None], bin_, conv.reshape(1, 49, 960), cbias,
        w1[None], b1, w2[None], b2, w3[None], b3, wo[None], bo, bs, n2g, n2s, we[None], be, wr[None], br, ms,
    )


def solution(mesh):
    count = mesh.shape["dp"]
    image = P(None, "dp", None, None, None)
    one, two = P("section", None), P("section", None, None)
    weights = (one, one, two, one, two, one, two, one, two, one, two, one, two, one, one, one, one, two, one, two,
               one, one)
    field = P("section", None, "dp", None, None, None)
    return jax.shard_map(
        lambda *arrays: on_device(Flow(count), *arrays),
        mesh=mesh,
        in_specs=(image, image, P(None, "dp")) + weights,
        out_specs=(field, field) + weights,
        check_vma=False,
    )
```
